32 devices in a mesh: groups: 2 (over x), hour: 16 (over z, y, core).
Axes of the slice: x: 2, y: 2, z: 4, core: 2. Of those that a mesh axis runs over, the one named last changes fastest.
Arguments:
- power: float32 [32, 16, 2048], P('groups', 'hour'), parts along dimension 0, may hold values from -3 to 3
- capacity: float32 [4096], P(('groups', 'hour')), parts along dimension 0, may hold values from 0.01 to 20
- flow_dual: float32 [32, 16, 4096], P('groups', 'hour'), parts along dimension 0, may hold values from -3 to 3
- upper_dual: float32 [32, 16, 2048], P('groups', 'hour'), parts along dimension 0, may hold values from 0 to 0.1
- lower_dual: float32 [32, 16, 2048], P('groups', 'hour'), parts along dimension 0, may hold values from 0 to 0.1
- price: float32 [32, 16], P('groups', 'hour'), parts along dimension 0, may hold values from -5 to 5
- load: bfloat16 [32, 16, 512], P('groups', 'hour'), parts along dimension 0, may hold values from -5 to 5
- shift_factors: bfloat16 [4096, 512], replicated, may hold values from -0.25 to 0.25
- line_limit: float32 [4096], replicated, may hold values from 0.5 to 3
- unit_bus: int32 [2048], replicated, may hold values from 0 to 511
- leakage: float32 [2048], replicated, may hold values from 0.015625 to 0.0625
- initial_state: float32 [4096], P('groups'), parts along dimension 0, may hold values from 0 to 10
- power_limit: float32 [2048], replicated, may hold values from 0.5 to 1.5
- capacity_cost: float32 [2048], replicated, may hold values from 0 to 0.1
Outputs:
- new_power: float32 [32, 16, 2048], P('groups', 'hour'), parts along dimension 0
- new_capacity: float32 [4096], P(('groups', 'hour')), parts along dimension 0
- new_flow_dual: float32 [32, 16, 4096], P('groups', 'hour'), parts along dimension 0
- new_upper_dual: float32 [32, 16, 2048], P('groups', 'hour'), parts along dimension 0
- new_lower_dual: float32 [32, 16, 2048], P('groups', 'hour'), parts along dimension 0
The draws below stay inside these ranges and needn't reach their ends.
There are 2 independent parts, one for each index of `groups`. The reference program is written for one: setup_inputs(seed, part) draws one part's arguments, and reference() takes and returns one part's arrays. A program takes and returns all parts, laid end to end along the dimension named above; an argument that names none is the same for every part. Nothing has to cross between parts.
All inputs are finite; a program needn't handle non-finite values.
Results may differ from the reference program's by a relative error of at most 0.00093.
Values sent between devices are 32-bit elements; how exact they have to be, the bound alone decides.
No kernel may reach another device: no remote copies, remote signals or barrier semaphores. Data moves between devices by JAX's collectives and lax.ppermute only.
A program may use at most 128 MiB of HBM per device.

```python
import math
import jax
import jax.numpy as jnp
from jax import lax

U = 2048
LINES = 4096
BUSES = 512
SCEN = 16
ITERS = 4
HOURS = 16


def plant(array, own_key, low, largest):
    index_at = [jax.random.randint(jax.random.fold_in(own_key, axis), (), 0, length) for axis, length in enumerate(array.shape)]
    widest = array.shape.index(max(array.shape))
    neighbour = index_at[:widest] + [(index_at[widest] + 1) % array.shape[widest]] + index_at[widest + 1:]
    return array.at[tuple(index_at)].set(low).at[tuple(neighbour)].set(largest)


def steps_of(key, dims, pieces, smallest, largest):
    loudness, own = 1.0, jax.random.fold_in(key, 6)
    for axis_at, blocks in pieces:
        heights = jnp.exp(jax.random.uniform(jax.random.fold_in(own, axis_at), (blocks,), jnp.float32, smallest / len(pieces), largest / len(pieces)))
        loudness = loudness * jnp.repeat(heights, dims[axis_at] // blocks).reshape([-1 if axis == axis_at else 1 for axis in range(len(dims))])
    return loudness


def gaussian(key, shape, width, reach, cuts=(), kind=jnp.bfloat16):
    result = jax.random.normal(key, shape, jnp.float32) * width
    if len(cuts) > 0:
        result = steps_of(key, shape, cuts, -0.22, 0.18) * result
    return jnp.clip(result, min=-reach, max=reach).astype(kind)


def setup_inputs(seed: int = 0, part: int = 0) -> dict:
    arg_keys = jax.random.split(jax.random.key(seed), 15)
    part_splits = jax.random.split(jax.random.fold_in(arg_keys[14], part), 15)
    return {
        "power": gaussian(part_splits[0], (SCEN, HOURS, U), 0.5, 3.0, ((1, 16),), jnp.float32),
        "capacity": jnp.clip(jnp.exp(math.log(20.0) - 7.6009025 * jax.random.uniform(part_splits[1], (U,), jnp.float32) ** steps_of(part_splits[1], (U,), ((0, 16),), -0.2, 0.2)), 0.01, 20.0),
        "flow_dual": gaussian(part_splits[2], (SCEN, HOURS, LINES), 0.5, 3.0, ((1, 16),), jnp.float32),
        "upper_dual": jnp.clip(0.1 * jax.random.uniform(part_splits[3], (SCEN, HOURS, U), jnp.float32) ** steps_of(part_splits[3], (SCEN, HOURS, U), ((1, 16),), -0.2, 0.2), 0.0, 0.1),
        "lower_dual": jnp.clip(0.1 * jax.random.uniform(part_splits[4], (SCEN, HOURS, U), jnp.float32) ** steps_of(part_splits[4], (SCEN, HOURS, U), ((1, 16),), -0.2, 0.2), 0.0, 0.1),
        "price": gaussian(part_splits[5], (SCEN, HOURS), 1.0, 5.0, ((1, 16),), jnp.float32),
        "load": gaussian(part_splits[6], (SCEN, HOURS, BUSES), 1.0, 5.0, ((1, 16),)),
        "shift_factors": gaussian(arg_keys[7], (LINES, BUSES), BUSES ** -0.5, 0.25),
        "line_limit": jnp.clip(jax.random.uniform(arg_keys[8], (LINES,), jnp.float32, 0.5, 3.0), 0.5, 3.0),
        "unit_bus": plant(jax.random.randint(arg_keys[9], (U,), 0, BUSES), jax.random.fold_in(arg_keys[9], 1), 0, BUSES - 1).astype(jnp.int32),
        "leakage": jnp.clip(jnp.exp(jax.random.uniform(arg_keys[10], (U,), jnp.float32, math.log(0.015625), math.log(0.0625))), 0.015625, 0.0625),
        "initial_state": jnp.clip(jax.random.uniform(part_splits[11], (U,), jnp.float32, 0.0, 10.0), 0.0, 10.0),
        "power_limit": jnp.clip(jax.random.uniform(arg_keys[12], (U,), jnp.float32, 0.5, 1.5), 0.5, 1.5),
        "capacity_cost": jnp.clip(jax.random.uniform(arg_keys[13], (U,), jnp.float32, 0.0, 0.1), 0.0, 0.1),
    }


primal_step = 0.05
dual_step = 0.01


def state_forward(field, retain, start):
    def advance(carry, item):
        carry = retain * carry - item
        return carry, carry
    begin = jnp.broadcast_to(start, (field.shape[0], field.shape[2])).astype(jnp.float32)
    final, states = lax.scan(advance, begin, jnp.moveaxis(field, 1, 0))
    return jnp.moveaxis(states, 0, 1)


def state_adjoint(values, retain):
    def advance(carry, item):
        carry = retain * carry + item
        return carry, carry
    begin = jnp.zeros((values.shape[0], values.shape[2]), jnp.float32)
    final, states = lax.scan(advance, begin, jnp.moveaxis(values, 1, 0), reverse=True)
    return jnp.moveaxis(states, 0, 1)


def reference(power, capacity, flow_dual, upper_dual, lower_dual, price, load, shift_factors, line_limit, unit_bus, leakage, initial_state, power_limit, capacity_cost):
    retain = 1.0 - leakage
    incidence = (unit_bus[:, None] == jnp.arange(BUSES, dtype=jnp.int32)[None, :]).astype(jnp.bfloat16)
    for step in range(ITERS):
        bus_dual = jnp.dot(flow_dual.astype(jnp.bfloat16).reshape(-1, LINES), shift_factors, preferred_element_type=jnp.float32).astype(jnp.bfloat16)
        grid_grad = jnp.dot(bus_dual, incidence.T, preferred_element_type=jnp.float32).reshape(SCEN, HOURS, U)
        state_grad = -state_adjoint(upper_dual - lower_dual, retain)
        trial_power = jnp.clip(power - primal_step * (grid_grad + state_grad - price[:, :, None]), -power_limit, power_limit)
        dual_total = jnp.sum(upper_dual, axis=(0, 1))
        trial_capacity = jnp.maximum(capacity - primal_step * (HOURS * capacity_cost - dual_total / SCEN), 0.0)
        power_bar = 2.0 * trial_power - power
        capacity_bar = 2.0 * trial_capacity - capacity
        injection = jnp.dot(power_bar.astype(jnp.bfloat16).reshape(-1, U), incidence, preferred_element_type=jnp.float32)
        injection = (injection - load.astype(jnp.float32).reshape(-1, BUSES)).astype(jnp.bfloat16)
        flows = jnp.dot(injection, shift_factors.T, preferred_element_type=jnp.float32).reshape(SCEN, HOURS, LINES)
        probe = flow_dual + dual_step * flows
        flow_dual = probe - dual_step * jnp.clip(probe / dual_step, -line_limit, line_limit)
        state_bar = state_forward(power_bar, retain, initial_state)
        upper_dual = jnp.maximum(upper_dual + dual_step * (state_bar - capacity_bar), 0.0)
        lower_dual = jnp.maximum(lower_dual - dual_step * state_bar, 0.0)
        power = trial_power
        capacity = trial_capacity
    return power, capacity, flow_dual, upper_dual, lower_dual
```

```python
import jax
import jax.numpy as jnp
from jax import lax
from jax.experimental import pallas as pl
from jax.experimental.pallas import tpu as pltpu
from jax.sharding import PartitionSpec as P

ITERS = 4


primal_step = 0.05
dual_step = 0.01
LANES = 128
SUBLANES = 8


def compose(earlier, later):
    return (earlier[0] * later[0], later[0] * earlier[1] + later[1])


def chain_scan(factor, values, reverse):
    factors = jnp.broadcast_to(factor, values.shape)
    return lax.associative_scan(compose, (factors, values), reverse=reverse, axis=1)[1]


def grid_gradient(flow_dual, shift_factors, incidence):
    scen, hours, lines = flow_dual.shape
    bus_dual = jnp.dot(
        flow_dual.astype(jnp.bfloat16).reshape(-1, lines),
        shift_factors,
        preferred_element_type=jnp.float32,
    ).astype(jnp.bfloat16)
    grid_grad = jnp.dot(bus_dual, incidence.T, preferred_element_type=jnp.float32)
    return grid_grad.reshape(scen, hours, incidence.shape[0])


def flow_update(flow_dual, power_bar, load, shift_factors, incidence, line_limit):
    scen, hours, lines = flow_dual.shape
    injection = jnp.dot(
        power_bar.astype(jnp.bfloat16).reshape(-1, incidence.shape[0]),
        incidence,
        preferred_element_type=jnp.float32,
    )
    injection = (injection - load.astype(jnp.float32).reshape(-1, incidence.shape[1])).astype(
        jnp.bfloat16
    )
    flows = jnp.dot(injection, shift_factors.T, preferred_element_type=jnp.float32).reshape(
        scen, hours, lines
    )
    probe = flow_dual + dual_step * flows
    return probe - dual_step * jnp.clip(probe / dual_step, -line_limit, line_limit)


def by_units(
    power,
    capacity,
    flow_dual,
    upper_dual,
    lower_dual,
    price,
    load,
    shift_factors,
    line_limit,
    unit_bus,
    leakage,
    initial_state,
    power_limit,
    capacity_cost,
):
    retain = 1.0 - leakage
    buses = shift_factors.shape[1]
    incidence = (unit_bus[:, None] == jnp.arange(buses, dtype=jnp.int32)[None, :]).astype(
        jnp.bfloat16
    )
    scen, hdev, units = power.shape
    unit_dev = capacity.shape[0]
    ndev = lax.axis_size("hour")
    position = lax.axis_index("hour")
    hours_total = hdev * ndev

    def own(vector):
        return lax.dynamic_slice_in_dim(vector, position * unit_dev, unit_dev)

    upper_units, lower_units = (
        lax.all_to_all(upper_dual, "hour", split_axis=2, concat_axis=1, tiled=True),
        lax.all_to_all(lower_dual, "hour", split_axis=2, concat_axis=1, tiled=True),
    )
    retain_own = own(retain)
    start_own = own(initial_state)
    cost_own = own(capacity_cost)
    for step in range(ITERS):
        grid_grad = grid_gradient(flow_dual, shift_factors, incidence)
        adjoint_units = -chain_scan(retain_own, upper_units - lower_units, True)
        state_grad = lax.all_to_all(adjoint_units, "hour", split_axis=1, concat_axis=2, tiled=True)
        trial_power = jnp.clip(
            power - primal_step * (grid_grad + state_grad - price[:, :, None]),
            -power_limit,
            power_limit,
        )
        dual_total = jnp.sum(upper_units, axis=(0, 1))
        trial_capacity = jnp.maximum(
            capacity - primal_step * (hours_total * cost_own - dual_total / scen), 0.0
        )
        power_bar = 2.0 * trial_power - power
        capacity_bar = 2.0 * trial_capacity - capacity
        flow_dual = flow_update(flow_dual, power_bar, load, shift_factors, incidence, line_limit)
        bar_units = lax.all_to_all(power_bar, "hour", split_axis=2, concat_axis=1, tiled=True)
        driven = -bar_units
        driven = driven.at[:, 0, :].add(retain_own * start_own)
        state_bar = chain_scan(retain_own, driven, False)
        upper_units = jnp.maximum(upper_units + dual_step * (state_bar - capacity_bar), 0.0)
        lower_units = jnp.maximum(lower_units - dual_step * state_bar, 0.0)
        power = trial_power
        capacity = trial_capacity
    upper_dual, lower_dual = (
        lax.all_to_all(upper_units, "hour", split_axis=1, concat_axis=2, tiled=True),
        lax.all_to_all(lower_units, "hour", split_axis=1, concat_axis=2, tiled=True),
    )
    return (power, capacity, flow_dual, upper_dual, lower_dual)


def by_scenarios(
    power,
    capacity,
    flow_dual,
    upper_dual,
    lower_dual,
    price,
    load,
    shift_factors,
    line_limit,
    unit_bus,
    leakage,
    initial_state,
    power_limit,
    capacity_cost,
):
    ndev = lax.axis_size("hour")
    position = lax.axis_index("hour")
    scen = hours = ndev
    units = power.shape[2]
    lines, buses = shift_factors.shape
    ut, lt, bt = units // LANES, lines // LANES, buses // LANES
    small = -(-(bt + 2) // SUBLANES) * SUBLANES
    at_power, at_upper, at_lower, at_flow = 0, ut, 2 * ut, 3 * ut
    at_total = at_flow + lt
    at_load = at_total + ut
    at_price, at_capacity = at_load + bt, at_load + bt + 1
    rows_in = at_load + small
    back_total, back_flow = 3 * ut, 4 * ut
    rows_back = back_flow + lt
    f32, bf16 = jnp.float32, jnp.bfloat16
    vmem = pl.BlockSpec(memory_space=pltpu.VMEM)

    def call(body, outs, *args, flops=0):
        moved = sum(a.size * a.dtype.itemsize for a in args)
        return pl.pallas_call(
            body,
            out_shape=[jax.ShapeDtypeStruct(s, d) for s, d in outs],
            in_specs=[vmem] * len(args),
            out_specs=[vmem] * len(outs),
            compiler_params=pltpu.CompilerParams(vmem_limit_bytes=40 * 1024 * 1024),
            cost_estimate=pl.CostEstimate(flops=flops, bytes_accessed=moved, transcendentals=0),
        )(*args)

    def exchange(blocks):
        return lax.all_to_all(blocks, "hour", split_axis=0, concat_axis=0, tiled=True)

    def rows(ref, first, step):
        return ref[pl.ds(first, ref.shape[0] // step, stride=step), :]

    def wide(ref, first, count, step):
        return jnp.concatenate([rows(ref, first + j, step) for j in range(count)], axis=1)

    def spread(ref, first, step, value):
        for j in range(value.shape[1] // LANES):
            ref[pl.ds(first + j, value.shape[0], stride=step), :] = value[
                :, j * LANES : (j + 1) * LANES
            ]

    def gradient(flow, shift, buses_units, grid_ref):
        bus_dual = jnp.dot(flow.astype(bf16), shift[...], preferred_element_type=f32).astype(bf16)
        spread(
            grid_ref, 0, ut, jnp.dot(bus_dual, buses_units[...], preferred_element_type=f32)
        )

    def inject(bar_ref, load, units_buses):
        bar = wide(bar_ref, 0, ut, ut).astype(bf16)
        return (jnp.dot(bar, units_buses[...], preferred_element_type=f32) - load).astype(bf16)

    def advance(flow, injection, shift, limit):
        flows = lax.dot_general(
            injection, shift[...], (((1,), (1,)), ((), ())), preferred_element_type=f32
        )
        probe = flow + dual_step * flows
        bound = dual_step * limit[...]
        return probe - jnp.clip(probe, -bound, bound)

    def hour_of(ref, hour, step=ut, first=0):
        return ref[pl.ds(hour * step + first, ut), :]

    def local(upper, lower, before, grid_ref, price, retain, start, limit, put_power, bar_ref, put):
        carry = jnp.zeros((ut, LANES), f32)
        keep, bound = retain[...], limit[...]
        for hour in reversed(range(hours)):
            carry = keep * carry + (upper(hour) - lower(hour))
            old = before(hour)
            trial = jnp.clip(
                old - primal_step * (hour_of(grid_ref, hour) - carry - price(hour)), -bound, bound
            )
            put_power(hour, trial)
            bar_ref[pl.ds(hour * ut, ut), :] = 2.0 * trial - old
        state = start[...]
        for hour in range(hours):
            state = keep * state - hour_of(bar_ref, hour)
            put(
                hour,
                upper(hour) + dual_step * state,
                jnp.maximum(lower(hour) - dual_step * state, 0.0),
            )

    def capacities(capacity, cost, total):
        trial = jnp.maximum(capacity - primal_step * (hours * cost - total / scen), 0.0)
        return trial, dual_step * (2.0 * trial - capacity)

    def sum_blocks(ref, first, step):
        return sum(hour_of(ref, hour, step, first) for hour in range(hours))

    def store(ref):
        def put(hour, value):
            ref[pl.ds(hour * ut, ut), :] = value

        return put

    def send_total(ref, total):
        for peer in range(ndev):
            ref[pl.ds(peer * ut, ut), :] = total


    def pack(power, upper, lower, flow, load, price, capacity, out):
        total = jnp.zeros((ut, LANES), f32)
        for peer in range(ndev):
            base = peer * rows_in
            out[pl.ds(base + at_power, ut), :] = power[peer]
            out[pl.ds(base + at_upper, ut), :] = upper[peer]
            out[pl.ds(base + at_lower, ut), :] = lower[peer]
            out[pl.ds(base + at_flow, lt), :] = flow[peer]
            out[pl.ds(base + at_load + bt + 2, small - bt - 2), :] = jnp.zeros(
                (small - bt - 2, LANES), f32
            )
            total = total + upper[peer]
        for peer in range(ndev):
            out[pl.ds(peer * rows_in + at_total, ut), :] = total
        spread(out, at_load, rows_in, load[...].astype(f32))
        spread(out, at_price, rows_in, price[...])
        spread(out, at_capacity, rows_in, jnp.broadcast_to(capacity[...], (ndev, LANES)))

    def first(
        came, shift, buses_units, retain, start, limit, cost,
        power_out, upper_out, lower_out, bar, capacity_out, total_out, flow_out, load_out,
        price_out, grid,
    ):
        flow = wide(came, at_flow, lt, rows_in)
        flow_out[...] = flow
        load_out[...] = wide(came, at_load, bt, rows_in)
        price_out[...] = rows(came, at_price, rows_in)
        gradient(flow, shift, buses_units, grid)
        capacity, pull = capacities(
            rows(came, at_capacity, rows_in), cost[...], sum_blocks(came, at_total, rows_in)
        )
        capacity_out[...] = capacity
        total = [jnp.zeros((ut, LANES), f32)]

        def put(hour, lifted, low):
            new = jnp.maximum(lifted - pull, 0.0)
            upper_out[pl.ds(hour * ut, ut), :] = new
            lower_out[pl.ds(hour * ut, ut), :] = low
            total[0] = total[0] + new

        local(
            lambda hour: hour_of(came, hour, rows_in, at_upper),
            lambda hour: hour_of(came, hour, rows_in, at_lower),
            lambda hour: hour_of(came, hour, rows_in, at_power),
            grid,
            lambda hour: came[pl.ds(hour * rows_in + at_price, 1), :],
            retain, start, limit, store(power_out), bar, put,
        )
        send_total(total_out, total[0])

    def network(bar, flow_ref, load, shift, limit, units_buses, buses_units, flow_out, grid):
        flow = advance(flow_ref[...], inject(bar, load[...], units_buses), shift, limit)
        flow_out[...] = flow
        gradient(flow, shift, buses_units, grid)

    def step(upper, lower, power, price, retain, start, limit, grid, power_out, bar_out, lifted, low):
        def put(hour, lift, new_low):
            lifted[pl.ds(hour * ut, ut), :] = lift
            low[pl.ds(hour * ut, ut), :] = new_low

        local(
            lambda hour: hour_of(upper, hour),
            lambda hour: hour_of(lower, hour),
            lambda hour: hour_of(power, hour),
            grid,
            lambda hour: price[pl.ds(hour, 1), :],
            retain, start, limit, store(power_out), bar_out, put,
        )

    def middle(
        bar, flow, load, shift, line, units_buses, buses_units, upper, lower, power, price, retain,
        start, limit, flow_out, power_out, bar_out, lifted, low, grid,
    ):
        network(bar, flow, load, shift, line, units_buses, buses_units, flow_out, grid)
        step(upper, lower, power, price, retain, start, limit, grid, power_out, bar_out, lifted, low)

    def middle_ahead(
        bar, flow, load, shift, line, units_buses, buses_units, upper, lower, power, price, retain,
        start, limit, flow_out, power_out, bar_out, lifted, low, grid,
    ):
        network(bar, flow, load, shift, line, units_buses, buses_units, flow_out, grid)
        step(upper, lower, power, price, retain, start, limit, grid, power_out, bar_out, lifted, low)
        network(bar_out, flow_out, load, shift, line, units_buses, buses_units, flow_out, grid)

    def raise_upper(came, capacity, cost, lifted, capacity_out, put):
        new_capacity, pull = capacities(capacity[...], cost[...], sum_blocks(came, 0, ut))
        capacity_out[...] = new_capacity
        total = jnp.zeros((ut, LANES), f32)
        for hour in range(hours):
            new = jnp.maximum(hour_of(lifted, hour) - pull, 0.0)
            put(hour, new)
            total = total + new
        return total

    def update(came, capacity, cost, lifted, upper_out, capacity_out, total_out):
        send_total(
            total_out, raise_upper(came, capacity, cost, lifted, capacity_out, store(upper_out))
        )

    def last(
        came, capacity, cost, lifted, lower, power, price, retain, start, limit, grid, flow, load,
        shift, line, units_buses, out, capacity_out, upper, bar,
    ):
        total = raise_upper(came, capacity, cost, lifted, capacity_out, store(upper))
        for peer in range(ndev):
            out[pl.ds(peer * rows_back + back_total, ut), :] = total

        def put_power(hour, value):
            out[pl.ds(hour * rows_back, ut), :] = value

        def put(hour, lift, low):
            out[pl.ds(hour * rows_back + ut, ut), :] = lift
            out[pl.ds(hour * rows_back + 2 * ut, ut), :] = low

        local(
            lambda hour: hour_of(upper, hour),
            lambda hour: hour_of(lower, hour),
            lambda hour: hour_of(power, hour),
            grid,
            lambda hour: price[pl.ds(hour, 1), :],
            retain, start, limit, put_power, bar, put,
        )
        new = advance(flow[...], inject(bar, load[...], units_buses), shift, line)
        spread(out, back_flow, rows_back, new)

    def finish(came, capacity, cost, power_out, capacity_out, flow_out, upper_out, lower_out):
        new_capacity, pull = capacities(
            capacity[...], cost[...], sum_blocks(came, back_total, rows_back)
        )
        capacity_out[...] = new_capacity
        for peer in range(ndev):
            base = peer * rows_back
            power_out[peer] = came[pl.ds(base, ut), :]
            upper_out[peer] = jnp.maximum(came[pl.ds(base + ut, ut), :] - pull, 0.0)
            lower_out[peer] = came[pl.ds(base + 2 * ut, ut), :]
            flow_out[peer] = came[pl.ds(base + back_flow, lt), :]


    def tiles(vector):
        return vector.reshape(-1, LANES)

    retain, start = tiles(1.0 - leakage), tiles(initial_state)
    limit, cost = tiles(power_limit), tiles(capacity_cost)
    line = line_limit.reshape(1, lines)
    bus_ids = jnp.arange(buses, dtype=jnp.int32)
    units_buses = (unit_bus[:, None] == bus_ids[None, :]).astype(bf16)
    buses_units = (bus_ids[:, None] == unit_bus[None, :]).astype(bf16)
    shift = shift_factors

    state = (hours * ut, LANES)
    (sent,) = call(
        pack,
        [((ndev * rows_in, LANES), f32)],
        power.reshape(scen, ut, LANES),
        upper_dual.reshape(scen, ut, LANES),
        lower_dual.reshape(scen, ut, LANES),
        flow_dual.reshape(scen, lt, LANES),
        load.reshape(scen, buses),
        jnp.broadcast_to(price, (scen, LANES)),
        capacity.reshape(1, LANES),
    )
    came = exchange(sent)
    power, upper, lower, bar, capacity, total, flow, load, price, _ = call(
        first,
        [(state, f32)] * 4
        + [((ut, LANES), f32), (state, f32), ((hours, lines), f32), ((hours, buses), f32)]
        + [((hours, LANES), f32), (state, f32)],
        came, shift, buses_units, retain, start, limit, cost,
    )
    middle_outs = [((hours, lines), f32)] + [(state, f32)] * 5
    for iteration in range(1, ITERS - 1):
        came = exchange(total)
        flow, power, bar, lifted, lower, grid = call(
            middle if iteration < ITERS - 2 else middle_ahead, middle_outs,
            bar, flow, load, shift, line, units_buses, buses_units, upper, lower, power, price,
            retain, start, limit,
            flops=3 * 4 * hours * buses * (lines + units),
        )
        if iteration < ITERS - 2:
            upper, capacity, total = call(
                update, [(state, f32), ((ut, LANES), f32), (state, f32)],
                came, capacity, cost, lifted,
            )
    sent, capacity, _, _ = call(
        last,
        [((ndev * rows_back, LANES), f32), ((ut, LANES), f32), (state, f32), (state, f32)],
        came, capacity, cost, lifted, lower, power, price, retain, start, limit, grid, flow, load,
        shift, line, units_buses,
    )
    came = exchange(sent)
    hourly = ((scen, ut, LANES), f32)
    power, capacity, flow, upper, lower = call(
        finish,
        [hourly, ((ut, LANES), f32), ((scen, lt, LANES), f32), hourly, hourly],
        came, capacity, cost,
    )
    return (
        power.reshape(scen, 1, units),
        lax.dynamic_slice_in_dim(capacity, position, 1).reshape(LANES),
        flow.reshape(scen, 1, lines),
        upper.reshape(scen, 1, units),
        lower.reshape(scen, 1, units),
    )


def on_device(power, capacity, flow_dual, *rest):
    ndev = lax.axis_size("hour")
    buses = rest[4].shape[1]
    fits = (
        power.shape[0] == ndev
        and power.shape[1] == 1
        and capacity.shape[0] == LANES
        and ndev % (2 * SUBLANES) == 0
        and all(size % (SUBLANES * LANES) == 0 for size in (power.shape[2], flow_dual.shape[2]))
        and buses % LANES == 0
    )
    plan = by_scenarios if fits else by_units
    return plan(power, capacity, flow_dual, *rest)


def solution(mesh):
    return jax.shard_map(
        on_device,
        mesh=mesh,
        in_specs=(
            P("groups", "hour", None),
            P(("groups", "hour")),
            P("groups", "hour", None),
            P("groups", "hour", None),
            P("groups", "hour", None),
            P("groups", "hour"),
            P("groups", "hour", None),
            P(),
            P(),
            P(),
            P(),
            P("groups"),
            P(),
            P(),
        ),
        out_specs=(
            P("groups", "hour", None),
            P(("groups", "hour")),
            P("groups", "hour", None),
            P("groups", "hour", None),
            P("groups", "hour", None),
        ),
        check_vma=False,
    )
```

```python
import functools

import jax
import jax.numpy as jnp
from jax import lax
from jax.experimental import pallas as pl
from jax.experimental.pallas import tpu as pltpu
from jax.sharding import PartitionSpec as P

ITERS = 4


primal_step = 0.05
dual_step = 0.01
LANES = 128
SUBLANES = 8
CHUNKS = 4


def compose(earlier, later):
    return (earlier[0] * later[0], later[0] * earlier[1] + later[1])


def chain_scan(factor, values, reverse):
    factors = jnp.broadcast_to(factor, values.shape)
    return lax.associative_scan(compose, (factors, values), reverse=reverse, axis=1)[1]


def grid_gradient(flow_dual, shift_factors, incidence):
    scen, hours, lines = flow_dual.shape
    bus_dual = jnp.dot(
        flow_dual.astype(jnp.bfloat16).reshape(-1, lines),
        shift_factors,
        preferred_element_type=jnp.float32,
    ).astype(jnp.bfloat16)
    grid_grad = jnp.dot(bus_dual, incidence.T, preferred_element_type=jnp.float32)
    return grid_grad.reshape(scen, hours, incidence.shape[0])


def flow_update(flow_dual, power_bar, load, shift_factors, incidence, line_limit):
    scen, hours, lines = flow_dual.shape
    injection = jnp.dot(
        power_bar.astype(jnp.bfloat16).reshape(-1, incidence.shape[0]),
        incidence,
        preferred_element_type=jnp.float32,
    )
    injection = (injection - load.astype(jnp.float32).reshape(-1, incidence.shape[1])).astype(
        jnp.bfloat16
    )
    flows = jnp.dot(injection, shift_factors.T, preferred_element_type=jnp.float32).reshape(
        scen, hours, lines
    )
    probe = flow_dual + dual_step * flows
    return probe - dual_step * jnp.clip(probe / dual_step, -line_limit, line_limit)


def by_units(
    power,
    capacity,
    flow_dual,
    upper_dual,
    lower_dual,
    price,
    load,
    shift_factors,
    line_limit,
    unit_bus,
    leakage,
    initial_state,
    power_limit,
    capacity_cost,
):
    retain = 1.0 - leakage
    buses = shift_factors.shape[1]
    incidence = (unit_bus[:, None] == jnp.arange(buses, dtype=jnp.int32)[None, :]).astype(
        jnp.bfloat16
    )
    scen, hdev, units = power.shape
    unit_dev = capacity.shape[0]
    ndev = lax.axis_size("hour")
    position = lax.axis_index("hour")
    hours_total = hdev * ndev

    def own(vector):
        return lax.dynamic_slice_in_dim(vector, position * unit_dev, unit_dev)

    upper_units, lower_units = (
        lax.all_to_all(upper_dual, "hour", split_axis=2, concat_axis=1, tiled=True),
        lax.all_to_all(lower_dual, "hour", split_axis=2, concat_axis=1, tiled=True),
    )
    retain_own = own(retain)
    start_own = own(initial_state)
    cost_own = own(capacity_cost)
    for step in range(ITERS):
        grid_grad = grid_gradient(flow_dual, shift_factors, incidence)
        adjoint_units = -chain_scan(retain_own, upper_units - lower_units, True)
        state_grad = lax.all_to_all(adjoint_units, "hour", split_axis=1, concat_axis=2, tiled=True)
        trial_power = jnp.clip(
            power - primal_step * (grid_grad + state_grad - price[:, :, None]),
            -power_limit,
            power_limit,
        )
        dual_total = jnp.sum(upper_units, axis=(0, 1))
        trial_capacity = jnp.maximum(
            capacity - primal_step * (hours_total * cost_own - dual_total / scen), 0.0
        )
        power_bar = 2.0 * trial_power - power
        capacity_bar = 2.0 * trial_capacity - capacity
        flow_dual = flow_update(flow_dual, power_bar, load, shift_factors, incidence, line_limit)
        bar_units = lax.all_to_all(power_bar, "hour", split_axis=2, concat_axis=1, tiled=True)
        driven = -bar_units
        driven = driven.at[:, 0, :].add(retain_own * start_own)
        state_bar = chain_scan(retain_own, driven, False)
        upper_units = jnp.maximum(upper_units + dual_step * (state_bar - capacity_bar), 0.0)
        lower_units = jnp.maximum(lower_units - dual_step * state_bar, 0.0)
        power = trial_power
        capacity = trial_capacity
    upper_dual, lower_dual = (
        lax.all_to_all(upper_units, "hour", split_axis=1, concat_axis=2, tiled=True),
        lax.all_to_all(lower_units, "hour", split_axis=1, concat_axis=2, tiled=True),
    )
    return (power, capacity, flow_dual, upper_dual, lower_dual)


def by_scenarios(
    power,
    capacity,
    flow_dual,
    upper_dual,
    lower_dual,
    price,
    load,
    shift_factors,
    line_limit,
    unit_bus,
    leakage,
    initial_state,
    power_limit,
    capacity_cost,
):
    ndev = lax.axis_size("hour")
    position = lax.axis_index("hour")
    scen = hours = ndev
    units = power.shape[2]
    lines, buses = shift_factors.shape
    ut, lt, bt = units // LANES, lines // LANES, buses // LANES
    chunk = lines // CHUNKS
    small = -(-(bt + 2) // SUBLANES) * SUBLANES
    at_power, at_upper, at_lower, at_flow = 0, ut, 2 * ut, 3 * ut
    at_total = at_flow + lt
    at_load = at_total + ut
    at_price, at_capacity = at_load + bt, at_load + bt + 1
    rows_in = at_load + small
    back_total, back_flow = 3 * ut, 4 * ut
    rows_back = back_flow + lt
    f32, bf16 = jnp.float32, jnp.bfloat16
    state = (hours * ut, LANES)

    def call(body, outs, scratch, copies, *args, near=0, flops=0):
        moved = sum(a.size * a.dtype.itemsize for a in args)
        far = pl.BlockSpec(memory_space=pltpu.HBM)
        return pl.pallas_call(
            body,
            out_shape=[pltpu.HBM(s, f32) for s in outs],
            in_specs=[pl.BlockSpec(memory_space=pltpu.VMEM)] * near + [far] * (len(args) - near),
            out_specs=[far] * len(outs),
            scratch_shapes=[pltpu.VMEM(*s) for s in scratch] + [pltpu.SemaphoreType.DMA((copies,))],
            compiler_params=pltpu.CompilerParams(vmem_limit_bytes=24 * 1024 * 1024),
            cost_estimate=pl.CostEstimate(flops=flops, bytes_accessed=moved, transcendentals=0),
        )(*args[:near], *(pltpu.with_memory_space_constraint(a, pltpu.HBM) for a in args[near:]))

    class Copies:
        def __init__(self, semaphores):
            self.semaphores, self.count, self.sent = semaphores, 0, []

        def bring(self, source, target):
            copy = pltpu.make_async_copy(source, target, self.semaphores.at[self.count])
            self.count += 1
            copy.start()
            return copy

        def send(self, source, target):
            self.sent.append(self.bring(source, target))

        def close(self):
            for copy in self.sent:
                copy.wait()

    def exchange(blocks):
        return lax.all_to_all(blocks, "hour", split_axis=0, concat_axis=0, tiled=True)

    def rows(ref, first, step):
        return ref[pl.ds(first, ref.shape[0] // step, stride=step), :]

    def wide(ref, first, count, step):
        return jnp.concatenate([rows(ref, first + j, step) for j in range(count)], axis=1)

    def spread(ref, first, step, value):
        for j in range(value.shape[1] // LANES):
            ref[pl.ds(first + j, value.shape[0], stride=step), :] = value[
                :, j * LANES : (j + 1) * LANES
            ]

    def part(ref, index):
        return ref[pl.ds(index * ut, ut), :]

    def bring_chunks(copies, shift, shift_v):
        return [
            copies.bring(shift.at[pl.ds(c * chunk, chunk)], shift_v.at[pl.ds(c * chunk, chunk)])
            for c in range(CHUNKS)
        ]

    def to_units(bus_dual, incidence, grid):
        grid_grad = lax.dot_general(
            bus_dual.astype(bf16), incidence[...], (((1,), (1,)), ((), ())),
            preferred_element_type=f32,
        )
        spread(grid, 0, ut, grid_grad)

    def inject(bar, load, incidence):
        wide_bar = wide(bar, 0, ut, ut).astype(bf16)
        total = jnp.dot(wide_bar, incidence[...], preferred_element_type=f32)
        return (total - load[...]).astype(bf16)

    def advance(flow, injection, shift, limit, c):
        at = pl.ds(c * chunk, chunk)
        flows = lax.dot_general(
            injection, shift[at, :], (((1,), (1,)), ((), ())), preferred_element_type=f32
        )
        probe = flow[:, at] + dual_step * flows
        bound = dual_step * limit[:, at]
        return probe - jnp.clip(probe, -bound, bound)

    def to_buses(flow, shift, c):
        return jnp.dot(
            flow.astype(bf16), shift[pl.ds(c * chunk, chunk), :], preferred_element_type=f32
        )

    def network(bar, load, flow, shift, limit, incidence, grid, arrived):
        injection = inject(bar, load, incidence)
        for c in range(CHUNKS):
            arrived(c)
            flow[:, pl.ds(c * chunk, chunk)] = advance(flow, injection, shift, limit, c)
        to_units(
            jnp.dot(flow[...].astype(bf16), shift[...], preferred_element_type=f32), incidence, grid
        )

    def local(upper, lower, before, grid, price, settings, put_power, bar, put):
        keep, bound = part(settings, 0), part(settings, 2)
        carry = jnp.zeros((ut, LANES), f32)
        for hour in reversed(range(hours)):
            carry = keep * carry + (upper(hour) - lower(hour))
            old = before(hour)
            gradient = part(grid, hour) - carry - price(hour)
            trial = jnp.clip(old - primal_step * gradient, -bound, bound)
            put_power(hour, trial)
            bar[pl.ds(hour * ut, ut), :] = 2.0 * trial - old
        level = part(settings, 1)
        for hour in range(hours):
            level = keep * level - part(bar, hour)
            put(
                hour,
                upper(hour) + dual_step * level,
                jnp.maximum(lower(hour) - dual_step * level, 0.0),
            )

    def capacities(capacity, settings, total):
        cost = part(settings, 3)
        trial = jnp.maximum(capacity - primal_step * (hours * cost - total / scen), 0.0)
        return trial, dual_step * (2.0 * trial - capacity)

    def sum_blocks(ref, first, step):
        return sum(ref[pl.ds(hour * step + first, ut), :] for hour in range(hours))

    def reader(ref):
        return lambda hour: part(ref, hour)

    def writer(ref):
        def put(hour, value):
            ref[pl.ds(hour * ut, ut), :] = value

        return put


    def pack(power, upper, lower, flow, load, price, capacity, out, *scratch):
        load_v, price_v, capacity_v, blocks_v, semaphores = scratch
        copies = Copies(semaphores)
        blocks = blocks_v.reshape(ndev, rows_in, LANES)
        places = [
            blocks.at[:, pl.ds(at, source.shape[1])]
            for source, at in (
                (upper, at_upper), (flow, at_flow), (power, at_power), (lower, at_lower),
            )
        ]
        big = [copies.bring(*pair) for pair in zip((upper, flow, power, lower), places)]
        come = [
            copies.bring(load, load_v),
            copies.bring(price, price_v),
            copies.bring(capacity, capacity_v),
        ]
        for peer in range(ndev):
            blocks_v[pl.ds(peer * rows_in + at_load, small), :] = jnp.zeros((small, LANES), f32)
        for copy in come:
            copy.wait()
        spread(blocks_v, at_load, rows_in, load_v[...].astype(f32))
        across = lax.broadcasted_iota(jnp.int32, (ndev, ndev), 0)
        along = lax.broadcasted_iota(jnp.int32, (ndev, ndev), 1)
        own_price = jnp.sum(
            jnp.where(across == along, jnp.broadcast_to(price_v[...], (ndev, ndev)), 0.0),
            axis=1, keepdims=True,
        )
        spread(blocks_v, at_price, rows_in, jnp.broadcast_to(own_price, (ndev, LANES)))
        spread(blocks_v, at_capacity, rows_in, jnp.broadcast_to(capacity_v[...], (ndev, LANES)))
        big[0].wait()
        total = sum_blocks(blocks_v, at_upper, rows_in)
        for peer in range(ndev):
            blocks_v[pl.ds(peer * rows_in + at_total, ut), :] = total
        for copy in big[1:]:
            copy.wait()
        copies.send(blocks, out)
        copies.close()

    def first(came, incidence, shift, settings, *rest):
        power_o, upper_o, lower_o, bar_o, flow_o, load_o, notes_o, total_o = rest[:8]
        shift_v, settings_v, power, upper, lower, bar, flow, load, notes, out, grid = rest[8:-1]
        copies = Copies(rest[-1])
        chunks = bring_chunks(copies, shift, shift_v)
        come = [copies.bring(settings, settings_v)]
        flow[...] = wide(came, at_flow, lt, rows_in)
        load[...] = wide(came, at_load, bt, rows_in)
        notes[pl.ds(ut, hours), :] = rows(came, at_price, rows_in)
        copies.send(flow, flow_o)
        copies.send(load, load_o)
        come[0].wait()
        capacity, pull = capacities(
            rows(came, at_capacity, rows_in), settings_v, sum_blocks(came, at_total, rows_in)
        )
        notes[pl.ds(0, ut), :] = capacity
        copies.send(notes, notes_o)
        bus_dual = jnp.zeros((hours, buses), f32)
        for c in range(CHUNKS):
            chunks[c].wait()
            bus_dual = bus_dual + to_buses(flow[:, pl.ds(c * chunk, chunk)], shift_v, c)
        to_units(bus_dual, incidence, grid)
        total = [jnp.zeros((ut, LANES), f32)]

        def put(hour, lifted, low):
            new = jnp.maximum(lifted - pull, 0.0)
            upper[pl.ds(hour * ut, ut), :] = new
            lower[pl.ds(hour * ut, ut), :] = low
            total[0] = total[0] + new

        def received(first_row, count=ut):
            return lambda hour: came[pl.ds(hour * rows_in + first_row, count), :]

        local(
            received(at_upper), received(at_lower), received(at_power), grid,
            received(at_price, 1), settings_v, writer(power), bar, put,
        )
        for peer in range(ndev):
            out[pl.ds(peer * ut, ut), :] = total[0]
        copies.send(out, total_o)
        copies.send(power, power_o)
        copies.send(bar, bar_o)
        copies.send(upper, upper_o)
        copies.send(lower, lower_o)
        copies.close()

    def middle(ahead, *refs):
        given, outs, scratch = refs[:11], refs[11:16], refs[16:-1]
        copies = Copies(refs[-1])
        held = dict(zip(names, scratch))
        incidence, shift, *others = given
        come = {}
        for name, source in zip(names, others):
            come[name] = copies.bring(source, held[name])
            if name == "flow":
                chunks = bring_chunks(copies, shift, scratch[-6])
        shift_v, grid, power_v, bar_v, lifted, low = scratch[-6:]
        for name in ("bar", "load", "flow", "line"):
            come.pop(name).wait()
        net = (held["load"], held["flow"], shift_v, held["line"], incidence, grid)
        network(held["bar"], *net, lambda c: chunks[c].wait())
        if not ahead:
            copies.send(held["flow"], outs[0])
        for copy in come.values():
            copy.wait()

        def put(hour, lift, new_low):
            lifted[pl.ds(hour * ut, ut), :] = lift
            low[pl.ds(hour * ut, ut), :] = new_low

        local(
            reader(held["upper"]), reader(held["lower"]), reader(held["power"]), grid,
            lambda hour: held["notes"][pl.ds(ut + hour, 1), :], held["settings"],
            writer(power_v), bar_v, put,
        )
        for value, out in zip((power_v, lifted, low), outs[1:]):
            copies.send(value, out)
        if ahead:
            network(bar_v, *net, lambda c: None)
            copies.send(held["flow"], outs[0])
            copies.send(grid, outs[4])
        else:
            copies.send(bar_v, outs[4])
        copies.close()

    names = (
        "bar", "load", "flow", "line", "upper", "lower", "power", "notes", "settings",
    )

    def update(came, lifted, notes, settings, *rest):
        upper_o, notes_o, total_o, lifted_v, notes_v, settings_v, upper, out, semaphores = rest
        copies = Copies(semaphores)
        come = [
            copies.bring(notes, notes_v),
            copies.bring(settings, settings_v),
            copies.bring(lifted, lifted_v),
        ]
        total = sum_blocks(came, 0, ut)
        come[0].wait()
        come[1].wait()
        capacity, pull = capacities(part(notes_v, 0), settings_v, total)
        notes_v[pl.ds(0, ut), :] = capacity
        copies.send(notes_v, notes_o)
        come[2].wait()
        total = jnp.zeros((ut, LANES), f32)
        for hour in range(hours):
            new = jnp.maximum(part(lifted_v, hour) - pull, 0.0)
            upper[pl.ds(hour * ut, ut), :] = new
            total = total + new
        for peer in range(ndev):
            out[pl.ds(peer * ut, ut), :] = total
        copies.send(out, total_o)
        copies.send(upper, upper_o)
        copies.close()

    def last(came, incidence, *refs):
        outs, scratch, copies = refs[10:12], refs[12:-1], Copies(refs[-1])
        held = dict(zip(final_names, scratch))
        shift_v, out, upper, bar = scratch[-4:]
        come = {
            name: copies.bring(source, held[name]) for name, source in zip(final_names, refs)
        }
        chunks = bring_chunks(copies, refs[9], shift_v)
        total = sum_blocks(came, 0, ut)
        for name in ("notes", "settings", "lifted"):
            come.pop(name).wait()
        notes, settings = held["notes"], held["settings"]
        capacity, pull = capacities(part(notes, 0), settings, total)
        notes[pl.ds(0, ut), :] = capacity
        copies.send(notes, outs[1])
        total = jnp.zeros((ut, LANES), f32)
        for hour in range(hours):
            new = jnp.maximum(part(held["lifted"], hour) - pull, 0.0)
            upper[pl.ds(hour * ut, ut), :] = new
            total = total + new
        for peer in range(ndev):
            out[pl.ds(peer * rows_back + back_total, ut), :] = total
        for name in ("lower", "power", "grid"):
            come.pop(name).wait()

        def put_power(hour, value):
            out[pl.ds(hour * rows_back, ut), :] = value

        def put(hour, lift, low):
            out[pl.ds(hour * rows_back + ut, ut), :] = lift
            out[pl.ds(hour * rows_back + 2 * ut, ut), :] = low

        local(
            reader(upper), reader(held["lower"]), reader(held["power"]), held["grid"],
            lambda hour: notes[pl.ds(ut + hour, 1), :], settings, put_power, bar, put,
        )
        blocks = out.reshape(ndev, rows_back, LANES)
        copies.send(blocks.at[:, pl.ds(0, back_flow)], outs[0].at[:, pl.ds(0, back_flow)])
        for copy in come.values():
            copy.wait()
        injection = inject(bar, held["load"], incidence)
        tiles_of = chunk // LANES
        for c in range(CHUNKS):
            chunks[c].wait()
            new = advance(held["flow"], injection, shift_v, held["line"], c)
            spread(out, back_flow + c * tiles_of, rows_back, new)
        at = pl.ds(back_flow, lt)
        copies.send(blocks.at[:, at], outs[0].at[:, at])
        copies.close()

    final_names = (
        "notes", "settings", "lifted", "lower", "power", "grid", "load", "flow", "line",
    )

    def finish(came, notes, settings, power_o, upper_o, lower_o, flow_o, capacity_o, *rest):
        notes_v, settings_v, upper, own, semaphores = rest
        copies = Copies(semaphores)
        come = [copies.bring(notes, notes_v), copies.bring(settings, settings_v)]
        blocks = came.reshape(ndev, rows_back, LANES)
        copies.send(blocks.at[:, pl.ds(0, ut)], power_o)
        copies.send(blocks.at[:, pl.ds(2 * ut, ut)], lower_o)
        copies.send(blocks.at[:, pl.ds(back_flow, lt)], flow_o)
        total = sum_blocks(came, back_total, rows_back)
        for copy in come:
            copy.wait()
        capacity, pull = capacities(part(notes_v, 0), settings_v, total)
        notes_v[pl.ds(0, ut), :] = capacity
        own[...] = notes_v[pl.ds(lax.axis_index("hour"), 1), :]
        copies.send(own, capacity_o)
        for peer in range(ndev):
            upper[peer] = jnp.maximum(came[pl.ds(peer * rows_back + ut, ut), :] - pull, 0.0)
        copies.send(upper, upper_o)
        copies.close()


    def tiles(vector):
        return vector.reshape(-1, LANES)

    settings = jnp.concatenate(
        [tiles(v) for v in (1.0 - leakage, initial_state, power_limit, capacity_cost)]
    )
    line = line_limit.reshape(1, lines)
    incidence = (unit_bus[:, None] == jnp.arange(buses, dtype=jnp.int32)[None, :]).astype(bf16)
    shift = shift_factors

    state_v, wide_v, load_v = (state, f32), ((hours, lines), f32), ((hours, buses), f32)
    notes, notes_v = (ut + hours, LANES), ((ut + hours, LANES), f32)
    settings_v, line_v = ((4 * ut, LANES), f32), ((1, lines), f32)
    shift_v = ((lines, buses), bf16)
    flops = 4 * hours * buses * (lines + units)

    (sent,) = call(
        pack,
        [(ndev, rows_in, LANES)],
        [
            ((scen, buses), bf16), ((1, scen), f32), ((1, LANES), f32),
            ((ndev * rows_in, LANES), f32),
        ],
        8,
        power.reshape(scen, ut, LANES),
        upper_dual.reshape(scen, ut, LANES),
        lower_dual.reshape(scen, ut, LANES),
        flow_dual.reshape(scen, lt, LANES),
        load.reshape(scen, buses),
        price.reshape(1, scen),
        capacity.reshape(1, LANES),
    )
    came = exchange(sent).reshape(-1, LANES)
    power, upper, lower, bar, flow, load, note, total = call(
        first,
        [state] * 4 + [(hours, lines), (hours, buses), notes, state],
        [shift_v, settings_v] + [state_v] * 4 + [wide_v, load_v, notes_v, state_v, state_v],
        CHUNKS + 9,
        came, incidence, shift, settings,
        near=2, flops=flops,
    )
    for iteration in range(1, ITERS - 1):
        ahead = iteration == ITERS - 2
        came = exchange(total.reshape(ndev, ut, LANES)).reshape(-1, LANES)
        flow, power, lifted, lower, more = call(
            functools.partial(middle, ahead),
            [(hours, lines)] + [state] * 4,
            [state_v, load_v, wide_v, line_v, state_v, state_v, state_v, notes_v]
            + [settings_v, shift_v] + [state_v] * 5,
            CHUNKS + 14,
            incidence, shift, bar, load, flow, line, upper, lower, power, note, settings,
            near=1, flops=flops * (1 + ahead),
        )
        if not ahead:
            bar = more
            upper, note, total = call(
                update,
                [state, notes, state],
                [state_v, notes_v, settings_v, state_v, state_v],
                6,
                came, lifted, note, settings,
                near=1,
            )
    sent, note = call(
        last,
        [(ndev, rows_back, LANES), notes],
        [notes_v, settings_v] + [state_v] * 4 + [load_v, wide_v, line_v, shift_v]
        + [((ndev * rows_back, LANES), f32), state_v, state_v],
        CHUNKS + 12,
        came, incidence, note, settings, lifted, lower, power, more, load, flow, line, shift,
        near=2, flops=flops,
    )
    came = exchange(sent).reshape(-1, LANES)
    hourly = (scen, ut, LANES)
    power, upper, lower, flow, capacity = call(
        finish,
        [hourly, hourly, hourly, (scen, lt, LANES), (1, LANES)],
        [notes_v, settings_v, (hourly, f32), ((1, LANES), f32)],
        7,
        came, note, settings,
        near=1,
    )
    return (
        power.reshape(scen, 1, units),
        capacity.reshape(LANES),
        flow.reshape(scen, 1, lines),
        upper.reshape(scen, 1, units),
        lower.reshape(scen, 1, units),
    )


def on_device(power, capacity, flow_dual, *rest):
    ndev = lax.axis_size("hour")
    buses = rest[4].shape[1]
    fits = (
        power.shape[0] == ndev
        and power.shape[1] == 1
        and capacity.shape[0] == LANES
        and flow_dual.shape[2] % (CHUNKS * LANES) == 0
        and ndev % (2 * SUBLANES) == 0
        and all(size % (SUBLANES * LANES) == 0 for size in (power.shape[2], flow_dual.shape[2]))
        and buses % LANES == 0
    )
    plan = by_scenarios if fits else by_units
    return plan(power, capacity, flow_dual, *rest)


def solution(mesh):
    return jax.shard_map(
        on_device,
        mesh=mesh,
        in_specs=(
            P("groups", "hour", None),
            P(("groups", "hour")),
            P("groups", "hour", None),
            P("groups", "hour", None),
            P("groups", "hour", None),
            P("groups", "hour"),
            P("groups", "hour", None),
            P(),
            P(),
            P(),
            P(),
            P("groups"),
            P(),
            P(),
        ),
        out_specs=(
            P("groups", "hour", None),
            P(("groups", "hour")),
            P("groups", "hour", None),
            P("groups", "hour", None),
            P("groups", "hour", None),
        ),
        check_vma=False,
    )
```

```python
import functools

import jax
import jax.numpy as jnp
from jax import lax
from jax.experimental import pallas as pl
from jax.experimental.pallas import tpu as pltpu
from jax.sharding import PartitionSpec as P

ITERS = 4


primal_step = 0.05
dual_step = 0.01
LANES = 128
SUBLANES = 8
NEAR = 5


def compose(earlier, later):
    return (earlier[0] * later[0], later[0] * earlier[1] + later[1])


def chain_scan(factor, values, reverse):
    factors = jnp.broadcast_to(factor, values.shape)
    return lax.associative_scan(compose, (factors, values), reverse=reverse, axis=1)[1]


def grid_gradient(flow_dual, shift_factors, incidence):
    scen, hours, lines = flow_dual.shape
    bus_dual = jnp.dot(
        flow_dual.astype(jnp.bfloat16).reshape(-1, lines),
        shift_factors,
        preferred_element_type=jnp.float32,
    ).astype(jnp.bfloat16)
    grid_grad = jnp.dot(bus_dual, incidence.T, preferred_element_type=jnp.float32)
    return grid_grad.reshape(scen, hours, incidence.shape[0])


def flow_update(flow_dual, power_bar, load, shift_factors, incidence, line_limit):
    scen, hours, lines = flow_dual.shape
    injection = jnp.dot(
        power_bar.astype(jnp.bfloat16).reshape(-1, incidence.shape[0]),
        incidence,
        preferred_element_type=jnp.float32,
    )
    injection = (injection - load.astype(jnp.float32).reshape(-1, incidence.shape[1])).astype(
        jnp.bfloat16
    )
    flows = jnp.dot(injection, shift_factors.T, preferred_element_type=jnp.float32).reshape(
        scen, hours, lines
    )
    probe = flow_dual + dual_step * flows
    return probe - dual_step * jnp.clip(probe / dual_step, -line_limit, line_limit)


def by_units(
    power,
    capacity,
    flow_dual,
    upper_dual,
    lower_dual,
    price,
    load,
    shift_factors,
    line_limit,
    unit_bus,
    leakage,
    initial_state,
    power_limit,
    capacity_cost,
):
    retain = 1.0 - leakage
    buses = shift_factors.shape[1]
    incidence = (unit_bus[:, None] == jnp.arange(buses, dtype=jnp.int32)[None, :]).astype(
        jnp.bfloat16
    )
    scen, hdev, units = power.shape
    unit_dev = capacity.shape[0]
    ndev = lax.axis_size("hour")
    position = lax.axis_index("hour")
    hours_total = hdev * ndev

    def own(vector):
        return lax.dynamic_slice_in_dim(vector, position * unit_dev, unit_dev)

    upper_units, lower_units = (
        lax.all_to_all(upper_dual, "hour", split_axis=2, concat_axis=1, tiled=True),
        lax.all_to_all(lower_dual, "hour", split_axis=2, concat_axis=1, tiled=True),
    )
    retain_own = own(retain)
    start_own = own(initial_state)
    cost_own = own(capacity_cost)
    for step in range(ITERS):
        grid_grad = grid_gradient(flow_dual, shift_factors, incidence)
        adjoint_units = -chain_scan(retain_own, upper_units - lower_units, True)
        state_grad = lax.all_to_all(adjoint_units, "hour", split_axis=1, concat_axis=2, tiled=True)
        trial_power = jnp.clip(
            power - primal_step * (grid_grad + state_grad - price[:, :, None]),
            -power_limit,
            power_limit,
        )
        dual_total = jnp.sum(upper_units, axis=(0, 1))
        trial_capacity = jnp.maximum(
            capacity - primal_step * (hours_total * cost_own - dual_total / scen), 0.0
        )
        power_bar = 2.0 * trial_power - power
        capacity_bar = 2.0 * trial_capacity - capacity
        flow_dual = flow_update(flow_dual, power_bar, load, shift_factors, incidence, line_limit)
        bar_units = lax.all_to_all(power_bar, "hour", split_axis=2, concat_axis=1, tiled=True)
        driven = -bar_units
        driven = driven.at[:, 0, :].add(retain_own * start_own)
        state_bar = chain_scan(retain_own, driven, False)
        upper_units = jnp.maximum(upper_units + dual_step * (state_bar - capacity_bar), 0.0)
        lower_units = jnp.maximum(lower_units - dual_step * state_bar, 0.0)
        power = trial_power
        capacity = trial_capacity
    upper_dual, lower_dual = (
        lax.all_to_all(upper_units, "hour", split_axis=1, concat_axis=2, tiled=True),
        lax.all_to_all(lower_units, "hour", split_axis=1, concat_axis=2, tiled=True),
    )
    return (power, capacity, flow_dual, upper_dual, lower_dual)


def by_scenarios(
    power,
    capacity,
    flow_dual,
    upper_dual,
    lower_dual,
    price,
    load,
    shift_factors,
    line_limit,
    unit_bus,
    leakage,
    initial_state,
    power_limit,
    capacity_cost,
):
    ndev = lax.axis_size("hour")
    position = lax.axis_index("hour")
    scen = hours = ndev
    units = power.shape[2]
    lines, buses = shift_factors.shape
    ut, lt, bt = units // LANES, lines // LANES, buses // LANES
    near_lines = lines * NEAR // 16
    parts = (pl.ds(0, near_lines), pl.ds(near_lines, lines - near_lines))
    small = -(-(bt + 2) // SUBLANES) * SUBLANES
    at_power, at_upper, at_lower, at_flow = 0, ut, 2 * ut, 3 * ut
    at_total = at_flow + lt
    at_load = at_total + ut
    at_price, at_capacity = at_load + bt, at_load + bt + 1
    rows_in = at_load + small
    back_total, back_flow = 3 * ut, 4 * ut
    rows_back = back_flow + lt
    f32, bf16 = jnp.float32, jnp.bfloat16
    state = (hours * ut, LANES)

    def call(body, near, far, outs, outs_far, scratch, copies, flops=0):
        moved = sum(a.size * a.dtype.itemsize for a in near + far)
        inner, outer = (pl.BlockSpec(memory_space=m) for m in (pltpu.VMEM, pltpu.HBM))
        return pl.pallas_call(
            body,
            out_shape=[pltpu.VMEM(s, f32) for s in outs] + [pltpu.HBM(s, f32) for s in outs_far],
            in_specs=[inner] * len(near) + [outer] * len(far),
            out_specs=[inner] * len(outs) + [outer] * len(outs_far),
            scratch_shapes=[pltpu.VMEM(*s) for s in scratch] + [pltpu.SemaphoreType.DMA((copies,))],
            compiler_params=pltpu.CompilerParams(vmem_limit_bytes=24 * 1024 * 1024),
            cost_estimate=pl.CostEstimate(flops=flops, bytes_accessed=moved, transcendentals=0),
        )(*near, *(pltpu.with_memory_space_constraint(a, pltpu.HBM) for a in far))

    class Copies:
        def __init__(self, semaphores):
            self.semaphores, self.count, self.sent = semaphores, 0, []

        def bring(self, source, target):
            copy = pltpu.make_async_copy(source, target, self.semaphores.at[self.count])
            self.count += 1
            copy.start()
            return copy

        def send(self, source, target):
            self.sent.append(self.bring(source, target))

        def close(self):
            for copy in self.sent:
                copy.wait()

    def exchange(blocks):
        return lax.all_to_all(blocks, "hour", split_axis=0, concat_axis=0, tiled=True)

    def rows(ref, first, step):
        return ref[pl.ds(first, ref.shape[0] // step, stride=step), :]

    def wide(ref, first, count, step):
        return jnp.concatenate([rows(ref, first + j, step) for j in range(count)], axis=1)

    def spread(ref, first, step, value):
        for j in range(value.shape[1] // LANES):
            ref[pl.ds(first + j, value.shape[0], stride=step), :] = value[
                :, j * LANES : (j + 1) * LANES
            ]

    def part(ref, index):
        return ref[pl.ds(index * ut, ut), :]

    def one_hot(settings, incidence):
        buses_of = lax.broadcasted_iota(jnp.int32, (buses, LANES), 0).astype(f32)
        for j in range(ut):
            same = buses_of == settings[pl.ds(4 * ut + j, 1), :]
            incidence[:, pl.ds(j * LANES, LANES)] = jnp.where(same, 1.0, 0.0).astype(bf16)

    def to_units(bus_dual, incidence, grid):
        spread(
            grid, 0, ut,
            jnp.dot(bus_dual.astype(bf16), incidence[...], preferred_element_type=f32),
        )

    def across(left, right):
        return lax.dot_general(left, right, (((1,), (1,)), ((), ())), preferred_element_type=f32)

    def inject(bar, load, incidence):
        wide_bar = wide(bar, 0, ut, ut).astype(bf16)
        return (across(wide_bar, incidence[...]) - load[...]).astype(bf16)

    def advance(flow, injection, shift, limit, at):
        probe = flow[:, at] + dual_step * across(injection, shift[...])
        bound = dual_step * limit[:, at]
        return probe - jnp.clip(probe, -bound, bound)

    def to_buses(flow, shifts, wait):
        total = jnp.zeros((hours, buses), f32)
        for at, shift, arrived in zip(parts, shifts, (None, wait)):
            if arrived:
                arrived()
            total = total + jnp.dot(
                flow[:, at].astype(bf16), shift[...], preferred_element_type=f32
            )
        return total

    def network(bar, load, flow, shifts, limit, incidence, new_flow, grid, wait):
        injection = inject(bar, load, incidence)
        for at, shift, arrived in zip(parts, shifts, (None, wait)):
            if arrived:
                arrived()
            new_flow[:, at] = advance(flow, injection, shift, limit, at)
        to_units(to_buses(new_flow, shifts, None), incidence, grid)

    def local(upper, lower, before, grid, price, settings, put_power, bar, put):
        keep, bound = part(settings, 0), part(settings, 2)
        carry = jnp.zeros((ut, LANES), f32)
        for hour in reversed(range(hours)):
            carry = keep * carry + (upper(hour) - lower(hour))
            old = before(hour)
            gradient = part(grid, hour) - carry - price(hour)
            trial = jnp.clip(old - primal_step * gradient, -bound, bound)
            put_power(hour, trial)
            bar[pl.ds(hour * ut, ut), :] = 2.0 * trial - old
        level = part(settings, 1)
        for hour in range(hours):
            level = keep * level - part(bar, hour)
            put(
                hour,
                upper(hour) + dual_step * level,
                jnp.maximum(lower(hour) - dual_step * level, 0.0),
            )

    def capacities(capacity, settings, total):
        cost = part(settings, 3)
        trial = jnp.maximum(capacity - primal_step * (hours * cost - total / scen), 0.0)
        return trial, dual_step * (2.0 * trial - capacity)

    def sum_blocks(ref, first, step):
        return sum(ref[pl.ds(hour * step + first, ut), :] for hour in range(hours))

    def reader(ref):
        return lambda hour: part(ref, hour)

    def writer(ref):
        def put(hour, value):
            ref[pl.ds(hour * ut, ut), :] = value

        return put


    def pack(power, upper, lower, flow, load, price, capacity, out, *scratch):
        load_v, price_v, capacity_v, blocks_v, semaphores = scratch
        copies = Copies(semaphores)
        blocks = blocks_v.reshape(ndev, rows_in, LANES)
        places = [
            blocks.at[:, pl.ds(at, source.shape[1])]
            for source, at in (
                (upper, at_upper), (flow, at_flow), (power, at_power), (lower, at_lower),
            )
        ]
        big = [copies.bring(*pair) for pair in zip((upper, flow, power, lower), places)]
        come = [
            copies.bring(load, load_v),
            copies.bring(price, price_v),
            copies.bring(capacity, capacity_v),
        ]
        for peer in range(ndev):
            blocks_v[pl.ds(peer * rows_in + at_load, small), :] = jnp.zeros((small, LANES), f32)
        for copy in come:
            copy.wait()
        spread(blocks_v, at_load, rows_in, load_v[...].astype(f32))
        across = lax.broadcasted_iota(jnp.int32, (ndev, ndev), 0)
        along = lax.broadcasted_iota(jnp.int32, (ndev, ndev), 1)
        own_price = jnp.sum(
            jnp.where(across == along, jnp.broadcast_to(price_v[...], (ndev, ndev)), 0.0),
            axis=1, keepdims=True,
        )
        spread(blocks_v, at_price, rows_in, jnp.broadcast_to(own_price, (ndev, LANES)))
        spread(blocks_v, at_capacity, rows_in, jnp.broadcast_to(capacity_v[...], (ndev, LANES)))
        big[0].wait()
        total = sum_blocks(blocks_v, at_upper, rows_in)
        for peer in range(ndev):
            blocks_v[pl.ds(peer * rows_in + at_total, ut), :] = total
        for copy in big[1:]:
            copy.wait()
        copies.send(blocks, out)
        copies.close()

    def first(came, shift, settings, shift_far, *rest):
        power, upper, lower, bar, flow, load, notes, total_o = rest[:8]
        shift_v, incidence, out, grid, semaphores = rest[8:]
        copies = Copies(semaphores)
        rest_of_shift = copies.bring(shift_far.at[parts[1]], shift_v)
        flow[...] = wide(came, at_flow, lt, rows_in)
        load[...] = wide(came, at_load, bt, rows_in)
        notes[pl.ds(ut, hours), :] = rows(came, at_price, rows_in)
        one_hot(settings, incidence)
        capacity, pull = capacities(
            rows(came, at_capacity, rows_in), settings, sum_blocks(came, at_total, rows_in)
        )
        notes[pl.ds(0, ut), :] = capacity
        to_units(to_buses(flow, (shift, shift_v), rest_of_shift.wait), incidence, grid)
        total = [jnp.zeros((ut, LANES), f32)]

        def put(hour, lifted, low):
            new = jnp.maximum(lifted - pull, 0.0)
            upper[pl.ds(hour * ut, ut), :] = new
            lower[pl.ds(hour * ut, ut), :] = low
            total[0] = total[0] + new

        def received(first_row, count=ut):
            return lambda hour: came[pl.ds(hour * rows_in + first_row, count), :]

        local(
            received(at_upper), received(at_lower), received(at_power), grid,
            received(at_price, 1), settings, writer(power), bar, put,
        )
        for peer in range(ndev):
            out[pl.ds(peer * ut, ut), :] = total[0]
        copies.send(out, total_o)
        copies.close()

    def middle(
        ahead, shift, bar, load, flow, line, upper, lower, power, notes, settings,
        shift_far, new_flow, new_power, lifted, low, more, shift_v, incidence, spare, semaphores,
    ):
        rest_of_shift = Copies(semaphores).bring(shift_far.at[parts[1]], shift_v)
        one_hot(settings, incidence)
        shifts = (shift, shift_v)
        grid, new_bar = (more, spare) if ahead else (spare, more)
        network(
            bar, load, flow, shifts, line, incidence, new_flow, grid, rest_of_shift.wait
        )

        def put(hour, lift, new_low):
            lifted[pl.ds(hour * ut, ut), :] = lift
            low[pl.ds(hour * ut, ut), :] = new_low

        local(
            reader(upper), reader(lower), reader(power), grid,
            lambda hour: notes[pl.ds(ut + hour, 1), :], settings, writer(new_power), new_bar, put,
        )
        if ahead:
            network(new_bar, load, new_flow, shifts, line, incidence, new_flow, grid, None)

    def raise_upper(came, lifted, notes, settings, upper, new_notes):
        capacity, pull = capacities(part(notes, 0), settings, sum_blocks(came, 0, ut))
        new_notes[pl.ds(0, ut), :] = capacity
        new_notes[pl.ds(ut, hours), :] = notes[pl.ds(ut, hours), :]
        total = jnp.zeros((ut, LANES), f32)
        for hour in range(hours):
            new = jnp.maximum(part(lifted, hour) - pull, 0.0)
            upper[pl.ds(hour * ut, ut), :] = new
            total = total + new
        return total

    def update(came, lifted, notes, settings, upper, new_notes, total_o, out, semaphores):
        total = raise_upper(came, lifted, notes, settings, upper, new_notes)
        for peer in range(ndev):
            out[pl.ds(peer * ut, ut), :] = total
        copies = Copies(semaphores)
        copies.send(out, total_o)
        copies.close()

    def last(
        came, shift, lifted, lower, power, grid, notes, settings, load, flow, line,
        shift_far, new_notes, out_o, shift_v, incidence, out, upper, bar, semaphores,
    ):
        copies = Copies(semaphores)
        rest_of_shift = copies.bring(shift_far.at[parts[1]], shift_v)
        total = raise_upper(came, lifted, notes, settings, upper, new_notes)
        for peer in range(ndev):
            out[pl.ds(peer * rows_back + back_total, ut), :] = total

        def put_power(hour, value):
            out[pl.ds(hour * rows_back, ut), :] = value

        def put(hour, lift, low):
            out[pl.ds(hour * rows_back + ut, ut), :] = lift
            out[pl.ds(hour * rows_back + 2 * ut, ut), :] = low

        local(
            reader(upper), reader(lower), reader(power), grid,
            lambda hour: notes[pl.ds(ut + hour, 1), :], settings, put_power, bar, put,
        )
        blocks = out.reshape(ndev, rows_back, LANES)
        copies.send(blocks.at[:, pl.ds(0, back_flow)], out_o.at[:, pl.ds(0, back_flow)])
        one_hot(settings, incidence)
        injection = inject(bar, load, incidence)
        row = back_flow
        for at, factors, arrived in zip(parts, (shift, shift_v), (None, rest_of_shift.wait)):
            if arrived:
                arrived()
            new = advance(flow, injection, factors, line, at)
            spread(out, row, rows_back, new)
            row += new.shape[1] // LANES
        flow_rows = pl.ds(back_flow, lt)
        copies.send(blocks.at[:, flow_rows], out_o.at[:, flow_rows])
        copies.close()

    def finish(came, notes, settings, power_o, upper_o, lower_o, flow_o, capacity_o, *rest):
        notes_v, upper, own, semaphores = rest
        copies = Copies(semaphores)
        blocks = came.reshape(ndev, rows_back, LANES)
        copies.send(blocks.at[:, pl.ds(0, ut)], power_o)
        copies.send(blocks.at[:, pl.ds(2 * ut, ut)], lower_o)
        copies.send(blocks.at[:, pl.ds(back_flow, lt)], flow_o)
        total = sum_blocks(came, back_total, rows_back)
        capacity, pull = capacities(part(notes, 0), settings, total)
        for peer in range(ndev):
            upper[peer] = jnp.maximum(came[pl.ds(peer * rows_back + ut, ut), :] - pull, 0.0)
        copies.send(upper, upper_o)
        notes_v[...] = capacity
        own[...] = notes_v[pl.ds(lax.axis_index("hour"), 1), :]
        copies.send(own, capacity_o)
        copies.close()


    def tiles(vector):
        return vector.reshape(-1, LANES)

    settings = jnp.concatenate(
        [
            tiles(v)
            for v in (1.0 - leakage, initial_state, power_limit, capacity_cost, unit_bus.astype(f32))
        ]
    )
    line = line_limit.reshape(1, lines)
    shift, shift_far = shift_factors[:near_lines], shift_factors

    state_v, incidence_v = (state, f32), ((buses, units), bf16)
    shift_v = ((lines - near_lines, buses), bf16)
    notes = (ut + hours, LANES)
    flops = 4 * hours * buses * (lines + units)

    (sent,) = call(
        pack,
        [],
        [
            power.reshape(scen, ut, LANES),
            upper_dual.reshape(scen, ut, LANES),
            lower_dual.reshape(scen, ut, LANES),
            flow_dual.reshape(scen, lt, LANES),
            load.reshape(scen, buses),
            price.reshape(1, scen),
            capacity.reshape(1, LANES),
        ],
        [],
        [(ndev, rows_in, LANES)],
        [
            ((scen, buses), bf16), ((1, scen), f32), ((1, LANES), f32),
            ((ndev * rows_in, LANES), f32),
        ],
        8,
    )
    came = exchange(sent).reshape(-1, LANES)
    power, upper, lower, bar, flow, load, note, total = call(
        first,
        [came, shift, settings],
        [shift_far],
        [state] * 4 + [(hours, lines), (hours, buses), notes],
        [state],
        [shift_v, incidence_v, state_v, state_v],
        2,
        flops=flops,
    )
    for iteration in range(1, ITERS - 1):
        ahead = iteration == ITERS - 2
        came = exchange(total.reshape(ndev, ut, LANES)).reshape(-1, LANES)
        flow, power, lifted, lower, more = call(
            functools.partial(middle, ahead),
            [shift, bar, load, flow, line, upper, lower, power, note, settings],
            [shift_far],
            [(hours, lines)] + [state] * 4,
            [],
            [shift_v, incidence_v, state_v],
            1,
            flops=flops * (1 + ahead),
        )
        if not ahead:
            bar = more
            upper, note, total = call(
                update, [came, lifted, note, settings], [], [state, notes], [state], [state_v], 1
            )
    note, sent = call(
        last,
        [came, shift, lifted, lower, power, more, note, settings, load, flow, line],
        [shift_far],
        [notes],
        [(ndev, rows_back, LANES)],
        [shift_v, incidence_v, ((ndev * rows_back, LANES), f32), state_v, state_v],
        3,
        flops=flops,
    )
    came = exchange(sent).reshape(-1, LANES)
    hourly = (scen, ut, LANES)
    power, upper, lower, flow, capacity = call(
        finish,
        [came, note, settings],
        [],
        [],
        [hourly, hourly, hourly, (scen, lt, LANES), (1, LANES)],
        [((ut, LANES), f32), (hourly, f32), ((1, LANES), f32)],
        5,
    )
    return (
        power.reshape(scen, 1, units),
        capacity.reshape(LANES),
        flow.reshape(scen, 1, lines),
        upper.reshape(scen, 1, units),
        lower.reshape(scen, 1, units),
    )


def on_device(power, capacity, flow_dual, *rest):
    ndev = lax.axis_size("hour")
    buses = rest[4].shape[1]
    fits = (
        power.shape[0] == ndev
        and power.shape[1] == 1
        and capacity.shape[0] == LANES
        and flow_dual.shape[2] % (16 * LANES) == 0
        and ndev % (2 * SUBLANES) == 0
        and all(size % (SUBLANES * LANES) == 0 for size in (power.shape[2], flow_dual.shape[2]))
        and buses % LANES == 0
    )
    plan = by_scenarios if fits else by_units
    return plan(power, capacity, flow_dual, *rest)


def solution(mesh):
    return jax.shard_map(
        on_device,
        mesh=mesh,
        in_specs=(
            P("groups", "hour", None),
            P(("groups", "hour")),
            P("groups", "hour", None),
            P("groups", "hour", None),
            P("groups", "hour", None),
            P("groups", "hour"),
            P("groups", "hour", None),
            P(),
            P(),
            P(),
            P(),
            P("groups"),
            P(),
            P(),
        ),
        out_specs=(
            P("groups", "hour", None),
            P(("groups", "hour")),
            P("groups", "hour", None),
            P("groups", "hour", None),
            P("groups", "hour", None),
        ),
        check_vma=False,
    )
```

```python
import jax
import jax.numpy as jnp
from jax import lax
from jax.experimental import pallas as pl
from jax.experimental.pallas import tpu as pltpu
from jax.sharding import PartitionSpec as P

ITERS = 4


primal_step = 0.05
dual_step = 0.01
LANES = 128
SUBLANES = 8
NEAR = 5
LAST_NEAR = 6


def compose(earlier, later):
    return (earlier[0] * later[0], later[0] * earlier[1] + later[1])


def chain_scan(factor, values, reverse):
    factors = jnp.broadcast_to(factor, values.shape)
    return lax.associative_scan(compose, (factors, values), reverse=reverse, axis=1)[1]


def grid_gradient(flow_dual, shift_factors, incidence):
    scen, hours, lines = flow_dual.shape
    bus_dual = jnp.dot(
        flow_dual.astype(jnp.bfloat16).reshape(-1, lines),
        shift_factors,
        preferred_element_type=jnp.float32,
    ).astype(jnp.bfloat16)
    grid_grad = jnp.dot(bus_dual, incidence.T, preferred_element_type=jnp.float32)
    return grid_grad.reshape(scen, hours, incidence.shape[0])


def flow_update(flow_dual, power_bar, load, shift_factors, incidence, line_limit):
    scen, hours, lines = flow_dual.shape
    injection = jnp.dot(
        power_bar.astype(jnp.bfloat16).reshape(-1, incidence.shape[0]),
        incidence,
        preferred_element_type=jnp.float32,
    )
    injection = (injection - load.astype(jnp.float32).reshape(-1, incidence.shape[1])).astype(
        jnp.bfloat16
    )
    flows = jnp.dot(injection, shift_factors.T, preferred_element_type=jnp.float32).reshape(
        scen, hours, lines
    )
    probe = flow_dual + dual_step * flows
    return probe - dual_step * jnp.clip(probe / dual_step, -line_limit, line_limit)


def by_units(
    power,
    capacity,
    flow_dual,
    upper_dual,
    lower_dual,
    price,
    load,
    shift_factors,
    line_limit,
    unit_bus,
    leakage,
    initial_state,
    power_limit,
    capacity_cost,
):
    retain = 1.0 - leakage
    buses = shift_factors.shape[1]
    incidence = (unit_bus[:, None] == jnp.arange(buses, dtype=jnp.int32)[None, :]).astype(
        jnp.bfloat16
    )
    scen, hdev, units = power.shape
    unit_dev = capacity.shape[0]
    ndev = lax.axis_size("hour")
    position = lax.axis_index("hour")
    hours_total = hdev * ndev

    def own(vector):
        return lax.dynamic_slice_in_dim(vector, position * unit_dev, unit_dev)

    upper_units, lower_units = (
        lax.all_to_all(upper_dual, "hour", split_axis=2, concat_axis=1, tiled=True),
        lax.all_to_all(lower_dual, "hour", split_axis=2, concat_axis=1, tiled=True),
    )
    retain_own = own(retain)
    start_own = own(initial_state)
    cost_own = own(capacity_cost)
    for step in range(ITERS):
        grid_grad = grid_gradient(flow_dual, shift_factors, incidence)
        adjoint_units = -chain_scan(retain_own, upper_units - lower_units, True)
        state_grad = lax.all_to_all(adjoint_units, "hour", split_axis=1, concat_axis=2, tiled=True)
        trial_power = jnp.clip(
            power - primal_step * (grid_grad + state_grad - price[:, :, None]),
            -power_limit,
            power_limit,
        )
        dual_total = jnp.sum(upper_units, axis=(0, 1))
        trial_capacity = jnp.maximum(
            capacity - primal_step * (hours_total * cost_own - dual_total / scen), 0.0
        )
        power_bar = 2.0 * trial_power - power
        capacity_bar = 2.0 * trial_capacity - capacity
        flow_dual = flow_update(flow_dual, power_bar, load, shift_factors, incidence, line_limit)
        bar_units = lax.all_to_all(power_bar, "hour", split_axis=2, concat_axis=1, tiled=True)
        driven = -bar_units
        driven = driven.at[:, 0, :].add(retain_own * start_own)
        state_bar = chain_scan(retain_own, driven, False)
        upper_units = jnp.maximum(upper_units + dual_step * (state_bar - capacity_bar), 0.0)
        lower_units = jnp.maximum(lower_units - dual_step * state_bar, 0.0)
        power = trial_power
        capacity = trial_capacity
    upper_dual, lower_dual = (
        lax.all_to_all(upper_units, "hour", split_axis=1, concat_axis=2, tiled=True),
        lax.all_to_all(lower_units, "hour", split_axis=1, concat_axis=2, tiled=True),
    )
    return (power, capacity, flow_dual, upper_dual, lower_dual)


def by_scenarios(
    power,
    capacity,
    flow_dual,
    upper_dual,
    lower_dual,
    price,
    load,
    shift_factors,
    line_limit,
    unit_bus,
    leakage,
    initial_state,
    power_limit,
    capacity_cost,
):
    ndev = lax.axis_size("hour")
    position = lax.axis_index("hour")
    scen = hours = ndev
    units = power.shape[2]
    lines, buses = shift_factors.shape
    ut, lt, bt = units // LANES, lines // LANES, buses // LANES
    near_lines = lines * NEAR // 16
    parts = (pl.ds(0, near_lines), pl.ds(near_lines, lines - near_lines))
    last_near = lines * LAST_NEAR // 16
    last_parts = (pl.ds(0, last_near), pl.ds(last_near, lines - last_near))
    small = -(-(bt + 2) // SUBLANES) * SUBLANES
    at_power, at_upper, at_lower, at_flow = 0, ut, 2 * ut, 3 * ut
    at_total = at_flow + lt
    at_load = at_total + ut
    at_price, at_capacity = at_load + bt, at_load + bt + 1
    rows_in = at_load + small
    back_total, back_bus = 3 * ut, 4 * ut
    rows_back = back_bus + 2 * bt
    rows_update = ut + 2 * bt
    f32, bf16 = jnp.float32, jnp.bfloat16
    state = (hours * ut, LANES)

    def call(body, near, far, outs, outs_far, scratch, copies, flops=0):
        moved = sum(a.size * a.dtype.itemsize for a in near + far)
        inner, outer = (pl.BlockSpec(memory_space=m) for m in (pltpu.VMEM, pltpu.HBM))
        return pl.pallas_call(
            body,
            out_shape=[pltpu.VMEM(s, f32) for s in outs] + [pltpu.HBM(s, f32) for s in outs_far],
            in_specs=[inner] * len(near) + [outer] * len(far),
            out_specs=[inner] * len(outs) + [outer] * len(outs_far),
            scratch_shapes=[pltpu.VMEM(*s) for s in scratch] + [pltpu.SemaphoreType.DMA((copies,))],
            compiler_params=pltpu.CompilerParams(vmem_limit_bytes=24 * 1024 * 1024),
            cost_estimate=pl.CostEstimate(flops=flops, bytes_accessed=moved, transcendentals=0),
        )(*near, *(pltpu.with_memory_space_constraint(a, pltpu.HBM) for a in far))

    class Copies:
        def __init__(self, semaphores):
            self.semaphores, self.count, self.sent = semaphores, 0, []

        def bring(self, source, target):
            copy = pltpu.make_async_copy(source, target, self.semaphores.at[self.count])
            self.count += 1
            copy.start()
            return copy

        def send(self, source, target):
            self.sent.append(self.bring(source, target))

        def close(self):
            for copy in self.sent:
                copy.wait()

    def exchange(blocks):
        return lax.all_to_all(blocks, "hour", split_axis=0, concat_axis=0, tiled=True)

    def rows(ref, first, step):
        return ref[pl.ds(first, ref.shape[0] // step, stride=step), :]

    def wide(ref, first, count, step):
        return jnp.concatenate([rows(ref, first + j, step) for j in range(count)], axis=1)

    def spread(ref, first, step, value):
        for j in range(value.shape[1] // LANES):
            ref[pl.ds(first + j, value.shape[0], stride=step), :] = value[
                :, j * LANES : (j + 1) * LANES
            ]

    def part(ref, index):
        return ref[pl.ds(index * ut, ut), :]

    def one_hot(settings, incidence):
        buses_of = lax.broadcasted_iota(jnp.int32, (buses, LANES), 0).astype(f32)
        for j in range(ut):
            same = buses_of == settings[pl.ds(4 * ut + j, 1), :]
            incidence[:, pl.ds(j * LANES, LANES)] = jnp.where(same, 1.0, 0.0).astype(bf16)

    def to_units(bus_dual, incidence, grid):
        spread(
            grid, 0, ut,
            jnp.dot(bus_dual.astype(bf16), incidence[...], preferred_element_type=f32),
        )

    def across(left, right):
        return lax.dot_general(left, right, (((1,), (1,)), ((), ())), preferred_element_type=f32)

    def inject(bar, load, incidence):
        wide_bar = wide(bar, 0, ut, ut).astype(bf16)
        return (across(wide_bar, incidence[...]) - load[...]).astype(bf16)

    def to_buses(flow, shifts, wait):
        total = jnp.zeros((hours, buses), f32)
        for at, shift, arrived in zip(parts, shifts, (None, wait)):
            if arrived:
                arrived()
            total = total + jnp.dot(
                flow[:, at].astype(bf16), shift[...], preferred_element_type=f32
            )
        return total

    def held_back(probe, limit, at):
        bound = dual_step * limit[:, at]
        return probe - jnp.clip(probe, -bound, bound)

    def network(injection, flow, shifts, limit, incidence, new_flow, grid, wait):
        for at, shift, arrived in zip(parts, shifts, (None, wait)):
            if arrived:
                arrived()
            probe = flow[:, at] + dual_step * across(injection, shift[...])
            new_flow[:, at] = held_back(probe, limit, at)
        to_units(to_buses(new_flow, shifts, None), incidence, grid)

    def local(upper, lower, before, grid, price, settings, put_power, bar, put):
        keep, bound = part(settings, 0), part(settings, 2)
        carry = jnp.zeros((ut, LANES), f32)
        for hour in reversed(range(hours)):
            carry = keep * carry + (upper(hour) - lower(hour))
            old = before(hour)
            gradient = part(grid, hour) - carry - price(hour)
            trial = jnp.clip(old - primal_step * gradient, -bound, bound)
            put_power(hour, trial)
            bar[pl.ds(hour * ut, ut), :] = 2.0 * trial - old
        level = part(settings, 1)
        for hour in range(hours):
            level = keep * level - part(bar, hour)
            put(
                hour,
                upper(hour) + dual_step * level,
                jnp.maximum(lower(hour) - dual_step * level, 0.0),
            )

    def capacities(capacity, settings, total):
        cost = part(settings, 3)
        trial = jnp.maximum(capacity - primal_step * (hours * cost - total / scen), 0.0)
        return trial, dual_step * (2.0 * trial - capacity)

    def sum_blocks(ref, first, step):
        return sum(ref[pl.ds(hour * step + first, ut), :] for hour in range(hours))

    def reader(ref):
        return lambda hour: part(ref, hour)

    def writer(ref):
        def put(hour, value):
            ref[pl.ds(hour * ut, ut), :] = value

        return put


    def pack(power, upper, lower, flow, load, price, capacity, out, *scratch):
        load_v, price_v, capacity_v, blocks_v, semaphores = scratch
        copies = Copies(semaphores)
        blocks = blocks_v.reshape(ndev, rows_in, LANES)
        places = [
            blocks.at[:, pl.ds(at, source.shape[1])]
            for source, at in (
                (upper, at_upper), (flow, at_flow), (power, at_power), (lower, at_lower),
            )
        ]
        big = [copies.bring(*pair) for pair in zip((upper, flow, power, lower), places)]
        come = [
            copies.bring(load, load_v),
            copies.bring(price, price_v),
            copies.bring(capacity, capacity_v),
        ]
        for peer in range(ndev):
            blocks_v[pl.ds(peer * rows_in + at_load, small), :] = jnp.zeros((small, LANES), f32)
        for copy in come:
            copy.wait()
        spread(blocks_v, at_load, rows_in, load_v[...].astype(f32))
        across = lax.broadcasted_iota(jnp.int32, (ndev, ndev), 0)
        along = lax.broadcasted_iota(jnp.int32, (ndev, ndev), 1)
        own_price = jnp.sum(
            jnp.where(across == along, jnp.broadcast_to(price_v[...], (ndev, ndev)), 0.0),
            axis=1, keepdims=True,
        )
        spread(blocks_v, at_price, rows_in, jnp.broadcast_to(own_price, (ndev, LANES)))
        spread(blocks_v, at_capacity, rows_in, jnp.broadcast_to(capacity_v[...], (ndev, LANES)))
        big[0].wait()
        total = sum_blocks(blocks_v, at_upper, rows_in)
        for peer in range(ndev):
            blocks_v[pl.ds(peer * rows_in + at_total, ut), :] = total
        for copy in big[1:]:
            copy.wait()
        copies.send(blocks, out)
        copies.close()

    def first(came, shift, settings, shift_far, *rest):
        power, upper, lower, bar, flow, load, notes, total_o = rest[:8]
        shift_v, incidence, out, grid, semaphores = rest[8:]
        copies = Copies(semaphores)
        rest_of_shift = copies.bring(shift_far.at[parts[1]], shift_v)
        flow[...] = wide(came, at_flow, lt, rows_in)
        load[...] = wide(came, at_load, bt, rows_in)
        notes[pl.ds(ut, hours), :] = rows(came, at_price, rows_in)
        one_hot(settings, incidence)
        capacity, pull = capacities(
            rows(came, at_capacity, rows_in), settings, sum_blocks(came, at_total, rows_in)
        )
        notes[pl.ds(0, ut), :] = capacity
        to_units(to_buses(flow, (shift, shift_v), rest_of_shift.wait), incidence, grid)
        total = [jnp.zeros((ut, LANES), f32)]

        def put(hour, lifted, low):
            new = jnp.maximum(lifted - pull, 0.0)
            upper[pl.ds(hour * ut, ut), :] = new
            lower[pl.ds(hour * ut, ut), :] = low
            total[0] = total[0] + new

        def received(first_row, count=ut):
            return lambda hour: came[pl.ds(hour * rows_in + first_row, count), :]

        local(
            received(at_upper), received(at_lower), received(at_power), grid,
            received(at_price, 1), settings, writer(power), bar, put,
        )
        for peer in range(ndev):
            out[pl.ds(peer * ut, ut), :] = total[0]
        copies.send(out, total_o)
        copies.close()

    def second(
        shift, bar, load, flow, line, upper, lower, power, notes, settings, shift_far,
        new_flow, new_power, lifted, low, sent, shift_v, incidence, grid, new_bar, semaphores,
    ):
        rest_of_shift = Copies(semaphores).bring(shift_far.at[parts[1]], shift_v)
        one_hot(settings, incidence)
        injection = inject(bar, load, incidence)
        sent[pl.ds(0, hours), :] = injection.astype(f32)
        network(
            injection, flow, (shift, shift_v), line, incidence, new_flow, grid, rest_of_shift.wait
        )
        local(
            reader(upper), reader(lower), reader(power), grid,
            lambda hour: notes[pl.ds(ut + hour, 1), :], settings, writer(new_power), new_bar,
            lift(lifted, low),
        )
        sent[pl.ds(hours, hours), :] = inject(new_bar, load, incidence).astype(f32)

    def third(
        shift, sent, load, flow, line, upper, lower, power, notes, settings, shift_far,
        new_flow, new_power, lifted, low, grid, later, shift_v, incidence, new_bar, semaphores,
    ):
        rest_of_shift = Copies(semaphores).bring(shift_far.at[parts[1]], shift_v)
        one_hot(settings, incidence)
        shifts = (shift, shift_v)
        injection = sent[pl.ds(hours, hours), :].astype(bf16)
        network(injection, flow, shifts, line, incidence, new_flow, grid, rest_of_shift.wait)
        local(
            reader(upper), reader(lower), reader(power), grid,
            lambda hour: notes[pl.ds(ut + hour, 1), :], settings, writer(new_power), new_bar,
            lift(lifted, low),
        )
        injection = inject(new_bar, load, incidence)
        later[...] = injection.astype(f32)
        network(injection, new_flow, shifts, line, incidence, new_flow, grid, None)

    def lift(lifted, low):
        def put(hour, new_lifted, new_low):
            lifted[pl.ds(hour * ut, ut), :] = new_lifted
            low[pl.ds(hour * ut, ut), :] = new_low

        return put

    def raise_upper(came, step, lifted, notes, settings, upper, new_notes):
        capacity, pull = capacities(part(notes, 0), settings, sum_blocks(came, 0, step))
        new_notes[pl.ds(0, ut), :] = capacity
        new_notes[pl.ds(ut, hours), :] = notes[pl.ds(ut, hours), :]
        total = jnp.zeros((ut, LANES), f32)
        for hour in range(hours):
            new = jnp.maximum(part(lifted, hour) - pull, 0.0)
            upper[pl.ds(hour * ut, ut), :] = new
            total = total + new
        return total

    def update(came, lifted, notes, settings, sent, upper, new_notes, out_o, out, semaphores):
        spread(out, ut, rows_update, sent[pl.ds(0, hours), :])
        spread(out, ut + bt, rows_update, sent[pl.ds(hours, hours), :])
        total = raise_upper(came, ut, lifted, notes, settings, upper, new_notes)
        for peer in range(ndev):
            out[pl.ds(peer * rows_update, ut), :] = total
        copies = Copies(semaphores)
        copies.send(out, out_o)
        copies.close()

    def last(
        came, lifted, lower, power, grid, notes, settings, load, later,
        new_notes, out_o, early_o, incidence, out, early, upper, bar, semaphores,
    ):
        copies = Copies(semaphores)
        for step in range(2):
            early[pl.ds(step * scen, scen), :] = wide(came, ut + step * bt, bt, rows_update)
        copies.send(early, early_o)
        total = raise_upper(came, rows_update, lifted, notes, settings, upper, new_notes)
        for peer in range(ndev):
            out[pl.ds(peer * rows_back + back_total, ut), :] = total

        def put_power(hour, value):
            out[pl.ds(hour * rows_back, ut), :] = value

        def put(hour, new_lifted, low):
            out[pl.ds(hour * rows_back + ut, ut), :] = new_lifted
            out[pl.ds(hour * rows_back + 2 * ut, ut), :] = low

        local(
            reader(upper), reader(lower), reader(power), grid,
            lambda hour: notes[pl.ds(ut + hour, 1), :], settings, put_power, bar, put,
        )
        one_hot(settings, incidence)
        spread(out, back_bus, rows_back, later[...])
        spread(out, back_bus + bt, rows_back, inject(bar, load, incidence).astype(f32))
        copies.send(out, out_o)
        copies.close()

    def hourly_flow(line, early, flow, turned, new_flow, early_v, flow_v, turned_v, semaphores):
        copies = Copies(semaphores)
        come = [copies.bring(*pair) for pair in ((early, early_v), (flow, flow_v), (turned, turned_v))]
        for copy in come:
            copy.wait()
        flows = jnp.dot(early_v[...].astype(bf16), turned_v[...], preferred_element_type=f32)
        every = pl.ds(0, lines)
        value = wide(flow_v, 0, lt, lt)
        for step in range(2):
            flow_step = flows[step * scen : (step + 1) * scen]
            value = held_back(value + dual_step * flow_step, line, every)
        new_flow[...] = value

    def finish(
        came, notes, settings, line, flow, turned, turned_far,
        power_o, upper_o, lower_o, flow_o, capacity_o,
        turned_v, notes_v, upper, own, out, semaphores,
    ):
        copies = Copies(semaphores)
        rest_of_turned = copies.bring(turned_far.at[:, last_parts[1]], turned_v)
        blocks = came.reshape(ndev, rows_back, LANES)
        copies.send(blocks.at[:, pl.ds(0, ut)], power_o)
        copies.send(blocks.at[:, pl.ds(2 * ut, ut)], lower_o)
        total = sum_blocks(came, back_total, rows_back)
        capacity, pull = capacities(part(notes, 0), settings, total)
        for peer in range(ndev):
            upper[peer] = jnp.maximum(came[pl.ds(peer * rows_back + ut, ut), :] - pull, 0.0)
        copies.send(upper, upper_o)
        notes_v[...] = capacity
        own[...] = notes_v[pl.ds(lax.axis_index("hour"), 1), :]
        copies.send(own, capacity_o)
        injections = jnp.concatenate(
            [wide(came, back_bus + step * bt, bt, rows_back) for step in range(2)], axis=0
        ).astype(bf16)
        row = 0
        for at, factors, arrived in zip(last_parts, (turned, turned_v), (None, rest_of_turned.wait)):
            if arrived:
                arrived()
            flows = dual_step * jnp.dot(injections, factors[...], preferred_element_type=f32)
            value = flow[:, at]
            for step in range(2):
                value = held_back(value + flows[step * scen : (step + 1) * scen], line, at)
            spread(out, row, lt, value)
            row += value.shape[1] // LANES
        copies.send(out.reshape(scen, lt, LANES), flow_o)
        copies.close()


    def tiles(vector):
        return vector.reshape(-1, LANES)

    settings = jnp.concatenate(
        [
            tiles(v)
            for v in (1.0 - leakage, initial_state, power_limit, capacity_cost, unit_bus.astype(f32))
        ]
    )
    line = line_limit.reshape(1, lines)
    shift, shift_far, turned = shift_factors[:near_lines], shift_factors, shift_factors.T

    state_v, incidence_v = (state, f32), ((buses, units), bf16)
    shift_v = ((lines - near_lines, buses), bf16)
    notes = (ut + hours, LANES)
    flops = 4 * hours * buses * (lines + units)

    (sent,) = call(
        pack,
        [],
        [
            power.reshape(scen, ut, LANES),
            upper_dual.reshape(scen, ut, LANES),
            lower_dual.reshape(scen, ut, LANES),
            flow_dual.reshape(scen, lt, LANES),
            load.reshape(scen, buses),
            price.reshape(1, scen),
            capacity.reshape(1, LANES),
        ],
        [],
        [(ndev, rows_in, LANES)],
        [
            ((scen, buses), bf16), ((1, scen), f32), ((1, LANES), f32),
            ((ndev * rows_in, LANES), f32),
        ],
        8,
    )
    came = exchange(sent).reshape(-1, LANES)
    power, upper, lower, bar, flow, load, note, total = call(
        first,
        [came, shift, settings],
        [shift_far],
        [state] * 4 + [(hours, lines), (hours, buses), notes],
        [state],
        [shift_v, incidence_v, state_v, state_v],
        2,
        flops=flops,
    )
    came = exchange(total.reshape(ndev, ut, LANES)).reshape(-1, LANES)
    flow, power, lifted, lower, injections = call(
        second,
        [shift, bar, load, flow, line, upper, lower, power, note, settings],
        [shift_far],
        [(hours, lines)] + [state] * 3 + [(2 * hours, buses)],
        [],
        [shift_v, incidence_v, state_v, state_v],
        1,
        flops=flops,
    )
    upper, note, sent = call(
        update,
        [came, lifted, note, settings, injections],
        [],
        [state, notes],
        [(ndev * rows_update, LANES)],
        [((ndev * rows_update, LANES), f32)],
        1,
    )
    came = exchange(sent.reshape(ndev, rows_update, LANES)).reshape(-1, LANES)
    flow, power, lifted, lower, grid, injection = call(
        third,
        [shift, injections, load, flow, line, upper, lower, power, note, settings],
        [shift_far],
        [(hours, lines)] + [state] * 4 + [(hours, buses)],
        [],
        [shift_v, incidence_v, state_v],
        1,
        flops=2 * flops,
    )
    note, sent, early = call(
        last,
        [came, lifted, lower, power, grid, note, settings, load, injection],
        [],
        [notes],
        [(ndev * rows_back, LANES), (2 * scen, buses)],
        [
            incidence_v, ((ndev * rows_back, LANES), f32), ((2 * scen, buses), f32), state_v,
            state_v,
        ],
        2,
        flops=flops,
    )
    came = exchange(sent.reshape(ndev, rows_back, LANES)).reshape(-1, LANES)
    own_flow = ((scen * lt, LANES), f32)
    (flow,) = call(
        hourly_flow,
        [line],
        [early, flow_dual.reshape(scen * lt, LANES), turned],
        [(scen, lines)],
        [],
        [((2 * scen, buses), f32), own_flow, ((buses, lines), bf16)],
        3,
        flops=flops,
    )
    hourly = (scen, ut, LANES)
    power, upper, lower, flow, capacity = call(
        finish,
        [came, note, settings, line, flow, turned[:, :last_near]],
        [turned],
        [],
        [hourly, hourly, hourly, (scen, lt, LANES), (1, LANES)],
        [
            ((buses, lines - last_near), bf16), ((ut, LANES), f32), (hourly, f32),
            ((1, LANES), f32), own_flow,
        ],
        6,
    )
    return (
        power.reshape(scen, 1, units),
        capacity.reshape(LANES),
        flow.reshape(scen, 1, lines),
        upper.reshape(scen, 1, units),
        lower.reshape(scen, 1, units),
    )


def on_device(power, capacity, flow_dual, *rest):
    ndev = lax.axis_size("hour")
    buses = rest[4].shape[1]
    fits = (
        ITERS == 4
        and power.shape[0] == ndev
        and power.shape[1] == 1
        and capacity.shape[0] == LANES
        and flow_dual.shape[2] % (16 * LANES) == 0
        and ndev % (2 * SUBLANES) == 0
        and all(size % (SUBLANES * LANES) == 0 for size in (power.shape[2], flow_dual.shape[2]))
        and buses % LANES == 0
    )
    plan = by_scenarios if fits else by_units
    return plan(power, capacity, flow_dual, *rest)


def solution(mesh):
    return jax.shard_map(
        on_device,
        mesh=mesh,
        in_specs=(
            P("groups", "hour", None),
            P(("groups", "hour")),
            P("groups", "hour", None),
            P("groups", "hour", None),
            P("groups", "hour", None),
            P("groups", "hour"),
            P("groups", "hour", None),
            P(),
            P(),
            P(),
            P(),
            P("groups"),
            P(),
            P(),
        ),
        out_specs=(
            P("groups", "hour", None),
            P(("groups", "hour")),
            P("groups", "hour", None),
            P("groups", "hour", None),
            P("groups", "hour", None),
        ),
        check_vma=False,
    )
```

```python
import jax
import jax.numpy as jnp
from jax import lax
from jax.experimental import pallas as pl
from jax.experimental.pallas import tpu as pltpu
from jax.sharding import PartitionSpec as P

ITERS = 4


primal_step = 0.05
dual_step = 0.01
LANES = 128
SUBLANES = 8
NEAR = 5
LAST_NEAR = 8
FAR_PARTS = 2


def compose(earlier, later):
    return (earlier[0] * later[0], later[0] * earlier[1] + later[1])


def chain_scan(factor, values, reverse):
    factors = jnp.broadcast_to(factor, values.shape)
    return lax.associative_scan(compose, (factors, values), reverse=reverse, axis=1)[1]


def grid_gradient(flow_dual, shift_factors, incidence):
    scen, hours, lines = flow_dual.shape
    bus_dual = jnp.dot(
        flow_dual.astype(jnp.bfloat16).reshape(-1, lines),
        shift_factors,
        preferred_element_type=jnp.float32,
    ).astype(jnp.bfloat16)
    grid_grad = jnp.dot(bus_dual, incidence.T, preferred_element_type=jnp.float32)
    return grid_grad.reshape(scen, hours, incidence.shape[0])


def flow_update(flow_dual, power_bar, load, shift_factors, incidence, line_limit):
    scen, hours, lines = flow_dual.shape
    injection = jnp.dot(
        power_bar.astype(jnp.bfloat16).reshape(-1, incidence.shape[0]),
        incidence,
        preferred_element_type=jnp.float32,
    )
    injection = (injection - load.astype(jnp.float32).reshape(-1, incidence.shape[1])).astype(
        jnp.bfloat16
    )
    flows = jnp.dot(injection, shift_factors.T, preferred_element_type=jnp.float32).reshape(
        scen, hours, lines
    )
    probe = flow_dual + dual_step * flows
    return probe - dual_step * jnp.clip(probe / dual_step, -line_limit, line_limit)


def by_units(
    power,
    capacity,
    flow_dual,
    upper_dual,
    lower_dual,
    price,
    load,
    shift_factors,
    line_limit,
    unit_bus,
    leakage,
    initial_state,
    power_limit,
    capacity_cost,
):
    retain = 1.0 - leakage
    buses = shift_factors.shape[1]
    incidence = (unit_bus[:, None] == jnp.arange(buses, dtype=jnp.int32)[None, :]).astype(
        jnp.bfloat16
    )
    scen, hdev, units = power.shape
    unit_dev = capacity.shape[0]
    ndev = lax.axis_size("hour")
    position = lax.axis_index("hour")
    hours_total = hdev * ndev

    def own(vector):
        return lax.dynamic_slice_in_dim(vector, position * unit_dev, unit_dev)

    upper_units, lower_units = (
        lax.all_to_all(upper_dual, "hour", split_axis=2, concat_axis=1, tiled=True),
        lax.all_to_all(lower_dual, "hour", split_axis=2, concat_axis=1, tiled=True),
    )
    retain_own = own(retain)
    start_own = own(initial_state)
    cost_own = own(capacity_cost)
    for step in range(ITERS):
        grid_grad = grid_gradient(flow_dual, shift_factors, incidence)
        adjoint_units = -chain_scan(retain_own, upper_units - lower_units, True)
        state_grad = lax.all_to_all(adjoint_units, "hour", split_axis=1, concat_axis=2, tiled=True)
        trial_power = jnp.clip(
            power - primal_step * (grid_grad + state_grad - price[:, :, None]),
            -power_limit,
            power_limit,
        )
        dual_total = jnp.sum(upper_units, axis=(0, 1))
        trial_capacity = jnp.maximum(
            capacity - primal_step * (hours_total * cost_own - dual_total / scen), 0.0
        )
        power_bar = 2.0 * trial_power - power
        capacity_bar = 2.0 * trial_capacity - capacity
        flow_dual = flow_update(flow_dual, power_bar, load, shift_factors, incidence, line_limit)
        bar_units = lax.all_to_all(power_bar, "hour", split_axis=2, concat_axis=1, tiled=True)
        driven = -bar_units
        driven = driven.at[:, 0, :].add(retain_own * start_own)
        state_bar = chain_scan(retain_own, driven, False)
        upper_units = jnp.maximum(upper_units + dual_step * (state_bar - capacity_bar), 0.0)
        lower_units = jnp.maximum(lower_units - dual_step * state_bar, 0.0)
        power = trial_power
        capacity = trial_capacity
    upper_dual, lower_dual = (
        lax.all_to_all(upper_units, "hour", split_axis=1, concat_axis=2, tiled=True),
        lax.all_to_all(lower_units, "hour", split_axis=1, concat_axis=2, tiled=True),
    )
    return (power, capacity, flow_dual, upper_dual, lower_dual)


def by_scenarios(
    power,
    capacity,
    flow_dual,
    upper_dual,
    lower_dual,
    price,
    load,
    shift_factors,
    line_limit,
    unit_bus,
    leakage,
    initial_state,
    power_limit,
    capacity_cost,
):
    ndev = lax.axis_size("hour")
    position = lax.axis_index("hour")
    scen = hours = ndev
    units = power.shape[2]
    lines, buses = shift_factors.shape
    ut, lt, bt = units // LANES, lines // LANES, buses // LANES
    near_lines = lines * NEAR // 16
    last_near = lines * LAST_NEAR // 16
    small = -(-(bt + 2) // SUBLANES) * SUBLANES
    at_power, at_upper, at_lower, at_flow = 0, ut, 2 * ut, 3 * ut
    at_total = at_flow + lt
    at_load = at_total + ut
    at_price, at_capacity = at_load + bt, at_load + bt + 1
    rows_in = at_load + small
    back_total, back_bus = 3 * ut, 4 * ut
    rows_back = back_bus + 2 * bt
    rows_update = ut + 2 * bt
    f32, bf16 = jnp.float32, jnp.bfloat16
    state = (hours * ut, LANES)

    def call(body, near, far, outs, outs_far, scratch, copies, flops=0):
        moved = sum(a.size * a.dtype.itemsize for a in near + far)
        inner, outer = (pl.BlockSpec(memory_space=m) for m in (pltpu.VMEM, pltpu.HBM))
        return pl.pallas_call(
            body,
            out_shape=[pltpu.VMEM(s, f32) for s in outs] + [pltpu.HBM(s, f32) for s in outs_far],
            in_specs=[inner] * len(near) + [outer] * len(far),
            out_specs=[inner] * len(outs) + [outer] * len(outs_far),
            scratch_shapes=[pltpu.VMEM(*s) for s in scratch] + [pltpu.SemaphoreType.DMA((copies,))],
            compiler_params=pltpu.CompilerParams(vmem_limit_bytes=24 * 1024 * 1024),
            cost_estimate=pl.CostEstimate(flops=flops, bytes_accessed=moved, transcendentals=0),
        )(*near, *(pltpu.with_memory_space_constraint(a, pltpu.HBM) for a in far))

    class Copies:
        def __init__(self, semaphores):
            self.semaphores, self.count, self.sent = semaphores, 0, []

        def bring(self, source, target):
            copy = pltpu.make_async_copy(source, target, self.semaphores.at[self.count])
            self.count += 1
            copy.start()
            return copy

        def send(self, source, target):
            self.sent.append(self.bring(source, target))

        def close(self):
            for copy in self.sent:
                copy.wait()

    def exchange(blocks):
        return lax.all_to_all(blocks, "hour", split_axis=0, concat_axis=0, tiled=True)

    def rows(ref, first, step):
        return ref[pl.ds(first, ref.shape[0] // step, stride=step), :]

    def wide(ref, first, count, step):
        return jnp.concatenate([rows(ref, first + j, step) for j in range(count)], axis=1)

    def spread(ref, first, step, value):
        for j in range(value.shape[1] // LANES):
            ref[pl.ds(first + j, value.shape[0], stride=step), :] = value[
                :, j * LANES : (j + 1) * LANES
            ]

    def part(ref, index):
        return ref[pl.ds(index * ut, ut), :]

    def bring_lines(copies, near, far, far_v, axis):
        here = near.shape[axis]
        size = (lines - here) // FAR_PARTS
        result = [(pl.ds(0, here), near, lambda: None)]
        for c in range(FAR_PARTS):
            source, target = pl.ds(here + c * size, size), pl.ds(c * size, size)
            if axis == 1:
                copy = copies.bring(far.at[:, source], far_v.at[:, target])
                part_v = far_v.at[:, target]
            else:
                copy = copies.bring(far.at[source], far_v.at[target])
                part_v = far_v.at[target]
            result.append((source, part_v, copy.wait))
        return result

    def arrived(factors):
        return [(at, part_v, lambda: None) for at, part_v, _ in factors]

    def one_hot(settings, incidence):
        buses_of = lax.broadcasted_iota(jnp.int32, (buses, LANES), 0).astype(f32)
        for j in range(ut):
            same = buses_of == settings[pl.ds(4 * ut + j, 1), :]
            incidence[:, pl.ds(j * LANES, LANES)] = jnp.where(same, 1.0, 0.0).astype(bf16)

    def to_units(bus_dual, incidence, grid):
        spread(
            grid, 0, ut,
            jnp.dot(bus_dual.astype(bf16), incidence[...], preferred_element_type=f32),
        )

    def across(left, right):
        return lax.dot_general(left, right, (((1,), (1,)), ((), ())), preferred_element_type=f32)

    def inject(bar, load, incidence):
        wide_bar = wide(bar, 0, ut, ut).astype(bf16)
        return (across(wide_bar, incidence[...]) - load[...]).astype(bf16)

    def to_buses(flow, shift):
        total = jnp.zeros((hours, buses), f32)
        for at, factors, wait in shift:
            wait()
            total = total + jnp.dot(
                flow[:, at].astype(bf16), factors[...], preferred_element_type=f32
            )
        return total

    def held_back(probe, limit, at):
        bound = dual_step * limit[:, at]
        return probe - jnp.clip(probe, -bound, bound)

    def network(injection, flow, shift, limit, incidence, new_flow, grid, turned=None):
        if turned is None:
            for at, factors, wait in shift:
                wait()
                probe = flow[:, at] + dual_step * across(injection, factors[...])
                new_flow[:, at] = held_back(probe, limit, at)
        else:
            flows = jnp.dot(injection, turned[...], preferred_element_type=f32)
            every = pl.ds(0, lines)
            new_flow[...] = held_back(flow[...] + dual_step * flows, limit, every)
        to_units(to_buses(new_flow, arrived(shift)), incidence, grid)

    def local(upper, lower, before, grid, price, settings, put_power, bar, put):
        keep, bound = part(settings, 0), part(settings, 2)
        carry = jnp.zeros((ut, LANES), f32)
        for hour in reversed(range(hours)):
            carry = keep * carry + (upper(hour) - lower(hour))
            old = before(hour)
            gradient = part(grid, hour) - carry - price(hour)
            trial = jnp.clip(old - primal_step * gradient, -bound, bound)
            put_power(hour, trial)
            bar[pl.ds(hour * ut, ut), :] = 2.0 * trial - old
        level = part(settings, 1)
        for hour in range(hours):
            level = keep * level - part(bar, hour)
            put(
                hour,
                upper(hour) + dual_step * level,
                jnp.maximum(lower(hour) - dual_step * level, 0.0),
            )

    def capacities(capacity, settings, total):
        cost = part(settings, 3)
        trial = jnp.maximum(capacity - primal_step * (hours * cost - total / scen), 0.0)
        return trial, dual_step * (2.0 * trial - capacity)

    def sum_blocks(ref, first, step):
        return sum(ref[pl.ds(hour * step + first, ut), :] for hour in range(hours))

    def reader(ref):
        return lambda hour: part(ref, hour)

    def writer(ref):
        def put(hour, value):
            ref[pl.ds(hour * ut, ut), :] = value

        return put


    def pack(power, upper, lower, flow, load, price, capacity, out, *scratch):
        load_v, price_v, capacity_v, blocks_v, semaphores = scratch
        copies = Copies(semaphores)
        blocks = blocks_v.reshape(ndev, rows_in, LANES)
        places = [
            blocks.at[:, pl.ds(at, source.shape[1])]
            for source, at in (
                (upper, at_upper), (flow, at_flow), (power, at_power), (lower, at_lower),
            )
        ]
        big = [copies.bring(*pair) for pair in zip((upper, flow, power, lower), places)]
        come = [
            copies.bring(load, load_v),
            copies.bring(price, price_v),
            copies.bring(capacity, capacity_v),
        ]
        for peer in range(ndev):
            blocks_v[pl.ds(peer * rows_in + at_load, small), :] = jnp.zeros((small, LANES), f32)
        for copy in come:
            copy.wait()
        spread(blocks_v, at_load, rows_in, load_v[...].astype(f32))
        across = lax.broadcasted_iota(jnp.int32, (ndev, ndev), 0)
        along = lax.broadcasted_iota(jnp.int32, (ndev, ndev), 1)
        own_price = jnp.sum(
            jnp.where(across == along, jnp.broadcast_to(price_v[...], (ndev, ndev)), 0.0),
            axis=1, keepdims=True,
        )
        spread(blocks_v, at_price, rows_in, jnp.broadcast_to(own_price, (ndev, LANES)))
        spread(blocks_v, at_capacity, rows_in, jnp.broadcast_to(capacity_v[...], (ndev, LANES)))
        for copy in big:
            copy.wait()
        at = pl.ds(0, at_total)
        copies.send(blocks.at[:, at], out.at[:, at])
        total = sum_blocks(blocks_v, at_upper, rows_in)
        for peer in range(ndev):
            blocks_v[pl.ds(peer * rows_in + at_total, ut), :] = total
        at = pl.ds(at_total, rows_in - at_total)
        copies.send(blocks.at[:, at], out.at[:, at])
        copies.close()

    def first(came, shift, settings, shift_far, turned, *rest):
        del turned
        power, upper, lower, bar, flow, load, notes, total_o = rest[:8]
        shift_v, incidence, out, grid, semaphores = rest[8:]
        copies = Copies(semaphores)
        factors = bring_lines(copies, shift, shift_far, shift_v, 0)
        flow[...] = wide(came, at_flow, lt, rows_in)
        load[...] = wide(came, at_load, bt, rows_in)
        notes[pl.ds(ut, hours), :] = rows(came, at_price, rows_in)
        one_hot(settings, incidence)
        capacity, pull = capacities(
            rows(came, at_capacity, rows_in), settings, sum_blocks(came, at_total, rows_in)
        )
        notes[pl.ds(0, ut), :] = capacity
        to_units(to_buses(flow, factors), incidence, grid)
        total = [jnp.zeros((ut, LANES), f32)]

        def put(hour, lifted, low):
            new = jnp.maximum(lifted - pull, 0.0)
            upper[pl.ds(hour * ut, ut), :] = new
            lower[pl.ds(hour * ut, ut), :] = low
            total[0] = total[0] + new

        def received(first_row, count=ut):
            return lambda hour: came[pl.ds(hour * rows_in + first_row, count), :]

        local(
            received(at_upper), received(at_lower), received(at_power), grid,
            received(at_price, 1), settings, writer(power), bar, put,
        )
        for peer in range(ndev):
            out[pl.ds(peer * ut, ut), :] = total[0]
        copies.send(out, total_o)
        copies.close()

    def second(
        shift, bar, load, flow, line, upper, lower, power, notes, settings, shift_far,
        new_flow, new_power, lifted, low, sent, shift_v, incidence, grid, new_bar, semaphores,
    ):
        factors = bring_lines(Copies(semaphores), shift, shift_far, shift_v, 0)
        one_hot(settings, incidence)
        injection = inject(bar, load, incidence)
        sent[pl.ds(0, hours), :] = injection.astype(f32)
        network(injection, flow, factors, line, incidence, new_flow, grid)
        local(
            reader(upper), reader(lower), reader(power), grid,
            lambda hour: notes[pl.ds(ut + hour, 1), :], settings, writer(new_power), new_bar,
            lift(lifted, low),
        )
        sent[pl.ds(hours, hours), :] = inject(new_bar, load, incidence).astype(f32)

    def third(
        shift, sent, load, flow, line, upper, lower, power, notes, settings, shift_far, turned,
        new_flow, new_power, lifted, low, grid, later,
        shift_v, turned_v, incidence, new_bar, semaphores,
    ):
        copies = Copies(semaphores)
        factors = bring_lines(copies, shift, shift_far, shift_v, 0)
        turned_factors = copies.bring(turned, turned_v)
        one_hot(settings, incidence)
        injection = sent[pl.ds(hours, hours), :].astype(bf16)
        network(injection, flow, factors, line, incidence, new_flow, grid)
        local(
            reader(upper), reader(lower), reader(power), grid,
            lambda hour: notes[pl.ds(ut + hour, 1), :], settings, writer(new_power), new_bar,
            lift(lifted, low),
        )
        injection = inject(new_bar, load, incidence)
        later[...] = injection.astype(f32)
        turned_factors.wait()
        network(
            injection, new_flow, arrived(factors), line, incidence, new_flow, grid, turned_v
        )

    def lift(lifted, low):
        def put(hour, new_lifted, new_low):
            lifted[pl.ds(hour * ut, ut), :] = new_lifted
            low[pl.ds(hour * ut, ut), :] = new_low

        return put

    def raise_upper(came, step, lifted, notes, settings, upper, new_notes):
        capacity, pull = capacities(part(notes, 0), settings, sum_blocks(came, 0, step))
        new_notes[pl.ds(0, ut), :] = capacity
        new_notes[pl.ds(ut, hours), :] = notes[pl.ds(ut, hours), :]
        total = jnp.zeros((ut, LANES), f32)
        for hour in range(hours):
            new = jnp.maximum(part(lifted, hour) - pull, 0.0)
            upper[pl.ds(hour * ut, ut), :] = new
            total = total + new
        return total

    def update(came, lifted, notes, settings, sent, upper, new_notes, out_o, out, semaphores):
        spread(out, ut, rows_update, sent[pl.ds(0, hours), :])
        spread(out, ut + bt, rows_update, sent[pl.ds(hours, hours), :])
        total = raise_upper(came, ut, lifted, notes, settings, upper, new_notes)
        for peer in range(ndev):
            out[pl.ds(peer * rows_update, ut), :] = total
        copies = Copies(semaphores)
        copies.send(out, out_o)
        copies.close()

    def last(
        came, lifted, lower, power, grid, notes, settings, load, later,
        new_notes, out_o, early_o, incidence, out, early, upper, bar, semaphores,
    ):
        copies = Copies(semaphores)
        for step in range(2):
            early[pl.ds(step * scen, scen), :] = wide(came, ut + step * bt, bt, rows_update)
        copies.send(early, early_o)
        total = raise_upper(came, rows_update, lifted, notes, settings, upper, new_notes)
        for peer in range(ndev):
            out[pl.ds(peer * rows_back + back_total, ut), :] = total

        def put_power(hour, value):
            out[pl.ds(hour * rows_back, ut), :] = value

        def put(hour, new_lifted, low):
            out[pl.ds(hour * rows_back + ut, ut), :] = new_lifted
            out[pl.ds(hour * rows_back + 2 * ut, ut), :] = low

        local(
            reader(upper), reader(lower), reader(power), grid,
            lambda hour: notes[pl.ds(ut + hour, 1), :], settings, put_power, bar, put,
        )
        blocks = out.reshape(ndev, rows_back, LANES)
        at = pl.ds(0, back_bus)
        copies.send(blocks.at[:, at], out_o.at[:, at])
        one_hot(settings, incidence)
        spread(out, back_bus, rows_back, later[...])
        spread(out, back_bus + bt, rows_back, inject(bar, load, incidence).astype(f32))
        at = pl.ds(back_bus, rows_back - back_bus)
        copies.send(blocks.at[:, at], out_o.at[:, at])
        copies.close()

    def hourly_flow(line, early, flow, turned, new_o, early_v, flow_v, turned_v, new, semaphores):
        copies = Copies(semaphores)
        come = [copies.bring(*pair) for pair in ((early, early_v), (flow, flow_v), (turned, turned_v))]
        for copy in come:
            copy.wait()
        flows = jnp.dot(early_v[...].astype(bf16), turned_v[...], preferred_element_type=f32)
        every = pl.ds(0, lines)
        value = wide(flow_v, 0, lt, lt)
        for step in range(2):
            flow_step = flows[step * scen : (step + 1) * scen]
            value = held_back(value + dual_step * flow_step, line, every)
        new[...] = value
        copies.send(new, new_o)
        copies.close()

    def finish(
        came, notes, settings, line, turned, flow, turned_far,
        power_o, upper_o, lower_o, flow_o, capacity_o,
        turned_v, flow_v, notes_v, upper, own, out, semaphores,
    ):
        copies = Copies(semaphores)
        flow_came = copies.bring(flow, flow_v)
        factors = bring_lines(copies, turned, turned_far, turned_v, 1)
        blocks = came.reshape(ndev, rows_back, LANES)
        copies.send(blocks.at[:, pl.ds(0, ut)], power_o)
        copies.send(blocks.at[:, pl.ds(2 * ut, ut)], lower_o)
        injections = jnp.concatenate(
            [wide(came, back_bus + step * bt, bt, rows_back) for step in range(2)], axis=0
        ).astype(bf16)
        flow_came.wait()
        row = 0
        for at, part_v, wait in factors:
            wait()
            flows = dual_step * jnp.dot(injections, part_v[...], preferred_element_type=f32)
            value = flow_v[:, at]
            for step in range(2):
                value = held_back(value + flows[step * scen : (step + 1) * scen], line, at)
            spread(out, row, lt, value)
            row += value.shape[1] // LANES
        copies.send(out.reshape(scen, lt, LANES), flow_o)
        total = sum_blocks(came, back_total, rows_back)
        capacity, pull = capacities(part(notes, 0), settings, total)
        for peer in range(ndev):
            upper[peer] = jnp.maximum(came[pl.ds(peer * rows_back + ut, ut), :] - pull, 0.0)
        copies.send(upper, upper_o)
        notes_v[...] = capacity
        own[...] = notes_v[pl.ds(lax.axis_index("hour"), 1), :]
        copies.send(own, capacity_o)
        copies.close()


    def tiles(vector):
        return vector.reshape(-1, LANES)

    settings = jnp.concatenate(
        [
            tiles(v)
            for v in (1.0 - leakage, initial_state, power_limit, capacity_cost, unit_bus.astype(f32))
        ]
    )
    line = line_limit.reshape(1, lines)
    shift, shift_far, turned = shift_factors[:near_lines], shift_factors, shift_factors.T

    state_v, incidence_v = (state, f32), ((buses, units), bf16)
    shift_v = ((lines - near_lines, buses), bf16)
    notes = (ut + hours, LANES)
    flops = 4 * hours * buses * (lines + units)

    (sent,) = call(
        pack,
        [],
        [
            power.reshape(scen, ut, LANES),
            upper_dual.reshape(scen, ut, LANES),
            lower_dual.reshape(scen, ut, LANES),
            flow_dual.reshape(scen, lt, LANES),
            load.reshape(scen, buses),
            price.reshape(1, scen),
            capacity.reshape(1, LANES),
        ],
        [],
        [(ndev, rows_in, LANES)],
        [
            ((scen, buses), bf16), ((1, scen), f32), ((1, LANES), f32),
            ((ndev * rows_in, LANES), f32),
        ],
        9,
    )
    came = exchange(sent).reshape(-1, LANES)
    power, upper, lower, bar, flow, load, note, total = call(
        first,
        [came, shift, settings],
        [shift_far, turned],
        [state] * 4 + [(hours, lines), (hours, buses), notes],
        [state],
        [shift_v, incidence_v, state_v, state_v],
        1 + FAR_PARTS,
        flops=flops,
    )
    came = exchange(total.reshape(ndev, ut, LANES)).reshape(-1, LANES)
    flow, power, lifted, lower, injections = call(
        second,
        [shift, bar, load, flow, line, upper, lower, power, note, settings],
        [shift_far],
        [(hours, lines)] + [state] * 3 + [(2 * hours, buses)],
        [],
        [shift_v, incidence_v, state_v, state_v],
        FAR_PARTS,
        flops=flops,
    )
    upper, note, sent = call(
        update,
        [came, lifted, note, settings, injections],
        [],
        [state, notes],
        [(ndev * rows_update, LANES)],
        [((ndev * rows_update, LANES), f32)],
        1,
    )
    came = exchange(sent.reshape(ndev, rows_update, LANES)).reshape(-1, LANES)
    flow, power, lifted, lower, grid, injection = call(
        third,
        [shift, injections, load, flow, line, upper, lower, power, note, settings],
        [shift_far, turned],
        [(hours, lines)] + [state] * 4 + [(hours, buses)],
        [],
        [shift_v, ((buses, lines), bf16), incidence_v, state_v],
        FAR_PARTS + 1,
        flops=2 * flops,
    )
    note, sent, early = call(
        last,
        [came, lifted, lower, power, grid, note, settings, load, injection],
        [],
        [notes],
        [(ndev, rows_back, LANES), (2 * scen, buses)],
        [
            incidence_v, ((ndev * rows_back, LANES), f32), ((2 * scen, buses), f32), state_v,
            state_v,
        ],
        3,
        flops=flops,
    )
    came = exchange(sent).reshape(-1, LANES)
    own_flow = ((scen * lt, LANES), f32)
    (flow,) = call(
        hourly_flow,
        [line],
        [early, flow_dual.reshape(scen * lt, LANES), turned],
        [],
        [(scen, lines)],
        [((2 * scen, buses), f32), own_flow, ((buses, lines), bf16), ((scen, lines), f32)],
        4,
        flops=flops,
    )
    hourly = (scen, ut, LANES)
    power, upper, lower, flow, capacity = call(
        finish,
        [came, note, settings, line, turned[:, :last_near]],
        [flow, turned],
        [],
        [hourly, hourly, hourly, (scen, lt, LANES), (1, LANES)],
        [
            ((buses, lines - last_near), bf16), ((scen, lines), f32), ((ut, LANES), f32),
            (hourly, f32), ((1, LANES), f32), own_flow,
        ],
        6 + FAR_PARTS,
    )
    return (
        power.reshape(scen, 1, units),
        capacity.reshape(LANES),
        flow.reshape(scen, 1, lines),
        upper.reshape(scen, 1, units),
        lower.reshape(scen, 1, units),
    )


def on_device(power, capacity, flow_dual, *rest):
    ndev = lax.axis_size("hour")
    buses = rest[4].shape[1]
    fits = (
        ITERS == 4
        and power.shape[0] == ndev
        and power.shape[1] == 1
        and capacity.shape[0] == LANES
        and flow_dual.shape[2] % (16 * FAR_PARTS * LANES) == 0
        and ndev % (2 * SUBLANES) == 0
        and all(size % (SUBLANES * LANES) == 0 for size in (power.shape[2], flow_dual.shape[2]))
        and buses % LANES == 0
    )
    plan = by_scenarios if fits else by_units
    return plan(power, capacity, flow_dual, *rest)


def solution(mesh):
    return jax.shard_map(
        on_device,
        mesh=mesh,
        in_specs=(
            P("groups", "hour", None),
            P(("groups", "hour")),
            P("groups", "hour", None),
            P("groups", "hour", None),
            P("groups", "hour", None),
            P("groups", "hour"),
            P("groups", "hour", None),
            P(),
            P(),
            P(),
            P(),
            P("groups"),
            P(),
            P(),
        ),
        out_specs=(
            P("groups", "hour", None),
            P(("groups", "hour")),
            P("groups", "hour", None),
            P("groups", "hour", None),
            P("groups", "hour", None),
        ),
        check_vma=False,
    )
```

```python
import jax
import jax.numpy as jnp
from jax import lax
from jax.experimental import pallas as pl
from jax.experimental.pallas import tpu as pltpu
from jax.sharding import PartitionSpec as P

ITERS = 4


primal_step = 0.05
dual_step = 0.01
LANES = 128
SUBLANES = 8
NEAR = 5
FAR_PARTS = 2


def compose(earlier, later):
    return (earlier[0] * later[0], later[0] * earlier[1] + later[1])


def chain_scan(factor, values, reverse):
    factors = jnp.broadcast_to(factor, values.shape)
    return lax.associative_scan(compose, (factors, values), reverse=reverse, axis=1)[1]


def grid_gradient(flow_dual, shift_factors, incidence):
    scen, hours, lines = flow_dual.shape
    bus_dual = jnp.dot(
        flow_dual.astype(jnp.bfloat16).reshape(-1, lines),
        shift_factors,
        preferred_element_type=jnp.float32,
    ).astype(jnp.bfloat16)
    grid_grad = jnp.dot(bus_dual, incidence.T, preferred_element_type=jnp.float32)
    return grid_grad.reshape(scen, hours, incidence.shape[0])


def flow_update(flow_dual, power_bar, load, shift_factors, incidence, line_limit):
    scen, hours, lines = flow_dual.shape
    injection = jnp.dot(
        power_bar.astype(jnp.bfloat16).reshape(-1, incidence.shape[0]),
        incidence,
        preferred_element_type=jnp.float32,
    )
    injection = (injection - load.astype(jnp.float32).reshape(-1, incidence.shape[1])).astype(
        jnp.bfloat16
    )
    flows = jnp.dot(injection, shift_factors.T, preferred_element_type=jnp.float32).reshape(
        scen, hours, lines
    )
    probe = flow_dual + dual_step * flows
    return probe - dual_step * jnp.clip(probe / dual_step, -line_limit, line_limit)


def by_units(
    power,
    capacity,
    flow_dual,
    upper_dual,
    lower_dual,
    price,
    load,
    shift_factors,
    line_limit,
    unit_bus,
    leakage,
    initial_state,
    power_limit,
    capacity_cost,
):
    retain = 1.0 - leakage
    buses = shift_factors.shape[1]
    incidence = (unit_bus[:, None] == jnp.arange(buses, dtype=jnp.int32)[None, :]).astype(
        jnp.bfloat16
    )
    scen, hdev, units = power.shape
    unit_dev = capacity.shape[0]
    ndev = lax.axis_size("hour")
    position = lax.axis_index("hour")
    hours_total = hdev * ndev

    def own(vector):
        return lax.dynamic_slice_in_dim(vector, position * unit_dev, unit_dev)

    upper_units, lower_units = (
        lax.all_to_all(upper_dual, "hour", split_axis=2, concat_axis=1, tiled=True),
        lax.all_to_all(lower_dual, "hour", split_axis=2, concat_axis=1, tiled=True),
    )
    retain_own = own(retain)
    start_own = own(initial_state)
    cost_own = own(capacity_cost)
    for step in range(ITERS):
        grid_grad = grid_gradient(flow_dual, shift_factors, incidence)
        adjoint_units = -chain_scan(retain_own, upper_units - lower_units, True)
        state_grad = lax.all_to_all(adjoint_units, "hour", split_axis=1, concat_axis=2, tiled=True)
        trial_power = jnp.clip(
            power - primal_step * (grid_grad + state_grad - price[:, :, None]),
            -power_limit,
            power_limit,
        )
        dual_total = jnp.sum(upper_units, axis=(0, 1))
        trial_capacity = jnp.maximum(
            capacity - primal_step * (hours_total * cost_own - dual_total / scen), 0.0
        )
        power_bar = 2.0 * trial_power - power
        capacity_bar = 2.0 * trial_capacity - capacity
        flow_dual = flow_update(flow_dual, power_bar, load, shift_factors, incidence, line_limit)
        bar_units = lax.all_to_all(power_bar, "hour", split_axis=2, concat_axis=1, tiled=True)
        driven = -bar_units
        driven = driven.at[:, 0, :].add(retain_own * start_own)
        state_bar = chain_scan(retain_own, driven, False)
        upper_units = jnp.maximum(upper_units + dual_step * (state_bar - capacity_bar), 0.0)
        lower_units = jnp.maximum(lower_units - dual_step * state_bar, 0.0)
        power = trial_power
        capacity = trial_capacity
    upper_dual, lower_dual = (
        lax.all_to_all(upper_units, "hour", split_axis=1, concat_axis=2, tiled=True),
        lax.all_to_all(lower_units, "hour", split_axis=1, concat_axis=2, tiled=True),
    )
    return (power, capacity, flow_dual, upper_dual, lower_dual)


def by_scenarios(
    power,
    capacity,
    flow_dual,
    upper_dual,
    lower_dual,
    price,
    load,
    shift_factors,
    line_limit,
    unit_bus,
    leakage,
    initial_state,
    power_limit,
    capacity_cost,
):
    ndev = lax.axis_size("hour")
    position = lax.axis_index("hour")
    scen = hours = ndev
    units = power.shape[2]
    lines, buses = shift_factors.shape
    ut, lt, bt = units // LANES, lines // LANES, buses // LANES
    near_lines = lines * NEAR // 16
    small = -(-(bt + 2) // SUBLANES) * SUBLANES
    at_power, at_upper, at_lower, at_flow = 0, ut, 2 * ut, 3 * ut
    at_total = at_flow + lt
    at_load = at_total
    at_price, at_capacity = at_load + bt, at_load + bt + 1
    rows_in = at_load + small
    back_bus = 3 * ut
    rows_back = back_bus + 2 * bt
    rows_update = ut + 2 * bt
    f32, bf16 = jnp.float32, jnp.bfloat16
    state = (hours * ut, LANES)

    def call(body, near, far, outs, outs_far, scratch, copies, flops=0):
        moved = sum(a.size * a.dtype.itemsize for a in near + far)
        inner, outer = (pl.BlockSpec(memory_space=m) for m in (pltpu.VMEM, pltpu.HBM))
        return pl.pallas_call(
            body,
            out_shape=[pltpu.VMEM(*s) if isinstance(s[0], tuple) else pltpu.VMEM(s, f32) for s in outs]
            + [pltpu.HBM(s, f32) for s in outs_far],
            in_specs=[inner] * len(near) + [outer] * len(far),
            out_specs=[inner] * len(outs) + [outer] * len(outs_far),
            scratch_shapes=[pltpu.VMEM(*s) for s in scratch] + [pltpu.SemaphoreType.DMA((copies,))],
            compiler_params=pltpu.CompilerParams(vmem_limit_bytes=24 * 1024 * 1024),
            cost_estimate=pl.CostEstimate(flops=flops, bytes_accessed=moved, transcendentals=0),
        )(*near, *(pltpu.with_memory_space_constraint(a, pltpu.HBM) for a in far))

    class Copies:
        def __init__(self, semaphores):
            self.semaphores, self.count, self.sent = semaphores, 0, []

        def bring(self, source, target):
            copy = pltpu.make_async_copy(source, target, self.semaphores.at[self.count])
            self.count += 1
            copy.start()
            return copy

        def send(self, source, target):
            self.sent.append(self.bring(source, target))

        def close(self):
            for copy in self.sent:
                copy.wait()

    def add_up(value, stages):
        for stage in stages:
            value = sum(
                [value]
                + [
                    lax.ppermute(value, "hour", [(j, j ^ other) for j in range(ndev)])
                    for other in stage
                ]
            )
        return value

    bits = [1 << b for b in range(ndev.bit_length() - 1)]
    half = 1 << (len(bits) // 2)
    two_stages = [range(1, half), range(half, ndev, half)]

    def exchange(blocks):
        return lax.all_to_all(blocks, "hour", split_axis=0, concat_axis=0, tiled=True)

    def rows(ref, first, step):
        return ref[pl.ds(first, ref.shape[0] // step, stride=step), :]

    def wide(ref, first, count, step):
        return jnp.concatenate([rows(ref, first + j, step) for j in range(count)], axis=1)

    def spread(ref, first, step, value):
        for j in range(value.shape[1] // LANES):
            ref[pl.ds(first + j, value.shape[0], stride=step), :] = value[
                :, j * LANES : (j + 1) * LANES
            ]

    def part(ref, index):
        return ref[pl.ds(index * ut, ut), :]

    def bring_lines(copies, near, far, far_v):
        size = (lines - near_lines) // FAR_PARTS
        result = [(pl.ds(0, near_lines), near, lambda: None)]
        for c in range(FAR_PARTS):
            source, target = pl.ds(near_lines + c * size, size), pl.ds(c * size, size)
            copy = copies.bring(far.at[source], far_v.at[target])
            result.append((source, far_v.at[target], copy.wait))
        return result

    def arrived(factors):
        return [(at, part_v, lambda: None) for at, part_v, _ in factors]

    def one_hot(settings, incidence):
        buses_of = lax.broadcasted_iota(jnp.int32, (buses, LANES), 0).astype(f32)
        for j in range(ut):
            same = buses_of == settings[pl.ds(4 * ut + j, 1), :]
            incidence[:, pl.ds(j * LANES, LANES)] = jnp.where(same, 1.0, 0.0).astype(bf16)

    def to_units(bus_dual, incidence, grid):
        spread(
            grid, 0, ut,
            jnp.dot(bus_dual.astype(bf16), incidence[...], preferred_element_type=f32),
        )

    def across(left, right):
        return lax.dot_general(left, right, (((1,), (1,)), ((), ())), preferred_element_type=f32)

    def inject(bar, load, incidence):
        wide_bar = wide(bar, 0, ut, ut).astype(bf16)
        return (across(wide_bar, incidence[...]) - load[...]).astype(bf16)

    def to_buses(flow, shift):
        total = jnp.zeros((hours, buses), f32)
        for at, factors, wait in shift:
            wait()
            total = total + jnp.dot(
                flow[:, at].astype(bf16), factors[...], preferred_element_type=f32
            )
        return total

    def held_back(probe, limit, at):
        bound = dual_step * limit[:, at]
        return probe - jnp.clip(probe, -bound, bound)

    def network(injection, flow, shift, limit, incidence, new_flow, grid):
        for at, factors, wait in shift:
            wait()
            probe = flow[:, at] + dual_step * across(injection, factors[...])
            new_flow[:, at] = held_back(probe, limit, at)
        to_units(to_buses(new_flow, arrived(shift)), incidence, grid)

    def local(upper, lower, before, grid, price, settings, put_power, bar, put):
        keep, bound = part(settings, 0), part(settings, 2)
        carry = jnp.zeros((ut, LANES), f32)
        for hour in reversed(range(hours)):
            carry = keep * carry + (upper(hour) - lower(hour))
            old = before(hour)
            gradient = part(grid, hour) - carry - price(hour)
            trial = jnp.clip(old - primal_step * gradient, -bound, bound)
            put_power(hour, trial)
            bar[pl.ds(hour * ut, ut), :] = 2.0 * trial - old
        level = part(settings, 1)
        for hour in range(hours):
            level = keep * level - part(bar, hour)
            put(
                hour,
                upper(hour) + dual_step * level,
                jnp.maximum(lower(hour) - dual_step * level, 0.0),
            )

    def capacities(capacity, settings, total):
        cost = part(settings, 3)
        trial = jnp.maximum(capacity - primal_step * (hours * cost - total / scen), 0.0)
        return trial, dual_step * (2.0 * trial - capacity)

    def sum_blocks(ref, first, step):
        return sum(ref[pl.ds(hour * step + first, ut), :] for hour in range(hours))

    def reader(ref):
        return lambda hour: part(ref, hour)

    def writer(ref):
        def put(hour, value):
            ref[pl.ds(hour * ut, ut), :] = value

        return put


    def pack(power, upper, lower, flow, load, price, capacity, *rest):
        vectors, shift_far, unit_bus, total_o, settings, shift, out = rest[:4], *rest[4:10]
        load_v, price_v, capacity_v, units_v, blocks_v, semaphores = rest[10:]
        copies = Copies(semaphores)
        blocks = blocks_v.reshape(ndev, rows_in, LANES)
        places = [
            blocks.at[:, pl.ds(at, source.shape[1])]
            for source, at in (
                (upper, at_upper), (flow, at_flow), (power, at_power), (lower, at_lower),
            )
        ]
        big = [copies.bring(*pair) for pair in zip((upper, flow, power, lower), places)]
        come = [
            copies.bring(load, load_v),
            copies.bring(price, price_v),
            copies.bring(capacity, capacity_v),
            copies.bring(unit_bus, units_v),
        ] + [
            copies.bring(vector, settings.at[pl.ds(place * ut, ut)])
            for place, vector in enumerate(vectors)
        ]
        copies.send(shift_far.at[pl.ds(0, near_lines)], shift)
        for peer in range(ndev):
            blocks_v[pl.ds(peer * rows_in + at_load, small), :] = jnp.zeros((small, LANES), f32)
        for copy in come:
            copy.wait()
        spread(blocks_v, at_load, rows_in, load_v[...].astype(f32))
        across = lax.broadcasted_iota(jnp.int32, (ndev, ndev), 0)
        along = lax.broadcasted_iota(jnp.int32, (ndev, ndev), 1)
        own_price = jnp.sum(
            jnp.where(across == along, jnp.broadcast_to(price_v[...], (ndev, ndev)), 0.0),
            axis=1, keepdims=True,
        )
        spread(blocks_v, at_price, rows_in, jnp.broadcast_to(own_price, (ndev, LANES)))
        spread(blocks_v, at_capacity, rows_in, jnp.broadcast_to(capacity_v[...], (ndev, LANES)))
        for copy in big:
            copy.wait()
        copies.send(blocks, out)
        total_o[...] = sum_blocks(blocks_v, at_upper, rows_in)
        settings[pl.ds(0, ut), :] = 1.0 - settings[pl.ds(0, ut), :]
        settings[pl.ds(4 * ut, ut), :] = units_v[...].astype(f32)
        copies.close()

    def first(came, total_in, shift, settings, shift_far, *rest):
        power, upper, lower, bar, flow, load, notes, total_o = rest[:8]
        shift_v, incidence, out, grid, semaphores = rest[8:]
        copies = Copies(semaphores)
        factors = bring_lines(copies, shift, shift_far, shift_v)
        flow[...] = wide(came, at_flow, lt, rows_in)
        load[...] = wide(came, at_load, bt, rows_in)
        notes[pl.ds(ut, hours), :] = rows(came, at_price, rows_in)
        one_hot(settings, incidence)
        capacity, pull = capacities(
            rows(came, at_capacity, rows_in), settings, total_in[...]
        )
        notes[pl.ds(0, ut), :] = capacity
        to_units(to_buses(flow, factors), incidence, grid)
        total = [jnp.zeros((ut, LANES), f32)]

        def put(hour, lifted, low):
            new = jnp.maximum(lifted - pull, 0.0)
            upper[pl.ds(hour * ut, ut), :] = new
            lower[pl.ds(hour * ut, ut), :] = low
            total[0] = total[0] + new

        def received(first_row, count=ut):
            return lambda hour: came[pl.ds(hour * rows_in + first_row, count), :]

        local(
            received(at_upper), received(at_lower), received(at_power), grid,
            received(at_price, 1), settings, writer(power), bar, put,
        )
        for peer in range(ndev):
            out[pl.ds(peer * ut, ut), :] = total[0]
        copies.send(out, total_o)
        copies.close()

    def second(
        shift, bar, load, flow, line, upper, lower, power, notes, settings, shift_far,
        new_flow, new_power, lifted, low, sent, shift_v, incidence, grid, new_bar, semaphores,
    ):
        factors = bring_lines(Copies(semaphores), shift, shift_far, shift_v)
        one_hot(settings, incidence)
        injection = inject(bar, load, incidence)
        sent[pl.ds(0, hours), :] = injection.astype(f32)
        network(injection, flow, factors, line, incidence, new_flow, grid)
        local(
            reader(upper), reader(lower), reader(power), grid,
            lambda hour: notes[pl.ds(ut + hour, 1), :], settings, writer(new_power), new_bar,
            lift(lifted, low),
        )
        sent[pl.ds(hours, hours), :] = inject(new_bar, load, incidence).astype(f32)

    def third(
        shift, sent, load, flow, line, upper, lower, power, notes, settings, shift_far,
        new_flow, new_power, lifted, low, grid, later,
        shift_v, incidence, new_bar, semaphores,
    ):
        factors = bring_lines(Copies(semaphores), shift, shift_far, shift_v)
        one_hot(settings, incidence)
        injection = sent[pl.ds(hours, hours), :].astype(bf16)
        network(injection, flow, factors, line, incidence, new_flow, grid)
        local(
            reader(upper), reader(lower), reader(power), grid,
            lambda hour: notes[pl.ds(ut + hour, 1), :], settings, writer(new_power), new_bar,
            lift(lifted, low),
        )
        injection = inject(new_bar, load, incidence)
        later[...] = injection.astype(f32)
        network(injection, new_flow, arrived(factors), line, incidence, new_flow, grid)

    def lift(lifted, low):
        def put(hour, new_lifted, new_low):
            lifted[pl.ds(hour * ut, ut), :] = new_lifted
            low[pl.ds(hour * ut, ut), :] = new_low

        return put

    def raise_upper(came, step, lifted, notes, settings, upper, new_notes):
        capacity, pull = capacities(part(notes, 0), settings, sum_blocks(came, 0, step))
        new_notes[pl.ds(0, ut), :] = capacity
        new_notes[pl.ds(ut, hours), :] = notes[pl.ds(ut, hours), :]
        total = jnp.zeros((ut, LANES), f32)
        for hour in range(hours):
            new = jnp.maximum(part(lifted, hour) - pull, 0.0)
            upper[pl.ds(hour * ut, ut), :] = new
            total = total + new
        return total

    def update(came, lifted, notes, settings, sent, upper, new_notes, out_o, out, semaphores):
        spread(out, ut, rows_update, sent[pl.ds(0, hours), :])
        spread(out, ut + bt, rows_update, sent[pl.ds(hours, hours), :])
        total = raise_upper(came, ut, lifted, notes, settings, upper, new_notes)
        for peer in range(ndev):
            out[pl.ds(peer * rows_update, ut), :] = total
        copies = Copies(semaphores)
        copies.send(out, out_o)
        copies.close()

    def last(
        came, lifted, lower, power, grid, notes, settings, load, later,
        new_notes, total_o, out_o, early_o, incidence, out, early, upper, bar, semaphores,
    ):
        copies = Copies(semaphores)
        for step in range(2):
            early[pl.ds(step * scen, scen), :] = wide(came, ut + step * bt, bt, rows_update)
        copies.send(early, early_o)
        total = raise_upper(came, rows_update, lifted, notes, settings, upper, new_notes)
        total_o[...] = total

        def put_power(hour, value):
            out[pl.ds(hour * rows_back, ut), :] = value

        def put(hour, new_lifted, low):
            out[pl.ds(hour * rows_back + ut, ut), :] = new_lifted
            out[pl.ds(hour * rows_back + 2 * ut, ut), :] = low

        local(
            reader(upper), reader(lower), reader(power), grid,
            lambda hour: notes[pl.ds(ut + hour, 1), :], settings, put_power, bar, put,
        )
        blocks = out.reshape(ndev, rows_back, LANES)
        at = pl.ds(0, back_bus)
        copies.send(blocks.at[:, at], out_o.at[:, at])
        one_hot(settings, incidence)
        spread(out, back_bus, rows_back, later[...])
        spread(out, back_bus + bt, rows_back, inject(bar, load, incidence).astype(f32))
        at = pl.ds(back_bus, rows_back - back_bus)
        copies.send(blocks.at[:, at], out_o.at[:, at])
        copies.close()

    def two_steps(value, injections, factors, line, at):
        flows = dual_step * across(injections, factors[...])
        for step in range(2):
            value = held_back(value + flows[step * scen : (step + 1) * scen], line, at)
        return value

    def hourly_flow(
        shift, line, early, flow, shift_far, new_o, early_v, flow_v, shift_v, new, semaphores
    ):
        copies = Copies(semaphores)
        come = [copies.bring(early, early_v), copies.bring(flow, flow_v)]
        factors = bring_lines(copies, shift, shift_far, shift_v)
        for copy in come:
            copy.wait()
        injections = early_v[...].astype(bf16)
        new[...] = wide(flow_v, 0, lt, lt)
        for at, part_v, wait in factors:
            wait()
            new[:, at] = two_steps(new[:, at], injections, part_v, line, at)
        copies.send(new, new_o)
        copies.close()

    def finish(
        came, total, notes, settings, line, shift, flow, shift_far,
        power_o, upper_o, lower_o, flow_o, capacity_o,
        shift_v, flow_v, notes_v, upper, own, out, semaphores,
    ):
        copies = Copies(semaphores)
        flow_came = copies.bring(flow, flow_v)
        factors = bring_lines(copies, shift, shift_far, shift_v)
        blocks = came.reshape(ndev, rows_back, LANES)
        copies.send(blocks.at[:, pl.ds(0, ut)], power_o)
        copies.send(blocks.at[:, pl.ds(2 * ut, ut)], lower_o)
        injections = jnp.concatenate(
            [wide(came, back_bus + step * bt, bt, rows_back) for step in range(2)], axis=0
        ).astype(bf16)
        flow_came.wait()
        row = 0
        for at, part_v, wait in factors:
            wait()
            value = two_steps(flow_v[:, at], injections, part_v, line, at)
            spread(out, row, lt, value)
            row += value.shape[1] // LANES
        copies.send(out.reshape(scen, lt, LANES), flow_o)
        capacity, pull = capacities(part(notes, 0), settings, total[...])
        for peer in range(ndev):
            upper[peer] = jnp.maximum(came[pl.ds(peer * rows_back + ut, ut), :] - pull, 0.0)
        copies.send(upper, upper_o)
        notes_v[...] = capacity
        own[...] = notes_v[pl.ds(lax.axis_index("hour"), 1), :]
        copies.send(own, capacity_o)
        copies.close()


    def tiles(vector):
        return vector.reshape(-1, LANES)

    line = line_limit.reshape(1, lines)
    shift_far = shift_factors

    state_v, incidence_v = (state, f32), ((buses, units), bf16)
    shift_v = ((lines - near_lines, buses), bf16)
    notes = (ut + hours, LANES)
    flops = 4 * hours * buses * (lines + units)

    total, settings, shift, sent = call(
        pack,
        [],
        [
            power.reshape(scen, ut, LANES),
            upper_dual.reshape(scen, ut, LANES),
            lower_dual.reshape(scen, ut, LANES),
            flow_dual.reshape(scen, lt, LANES),
            load.reshape(scen, buses),
            price.reshape(1, scen),
            capacity.reshape(1, LANES),
            tiles(leakage),
            tiles(initial_state),
            tiles(power_limit),
            tiles(capacity_cost),
            shift_far,
            tiles(unit_bus),
        ],
        [(ut, LANES), (5 * ut, LANES), ((near_lines, buses), bf16)],
        [(ndev, rows_in, LANES)],
        [
            ((scen, buses), bf16), ((1, scen), f32), ((1, LANES), f32), ((ut, LANES), jnp.int32),
            ((ndev * rows_in, LANES), f32),
        ],
        14,
    )
    came = exchange(sent).reshape(-1, LANES)
    total = add_up(total, two_stages)
    power, upper, lower, bar, flow, load, note, total = call(
        first,
        [came, total, shift, settings],
        [shift_far],
        [state] * 4 + [(hours, lines), (hours, buses), notes],
        [state],
        [shift_v, incidence_v, state_v, state_v],
        1 + FAR_PARTS,
        flops=flops,
    )
    came = exchange(total.reshape(ndev, ut, LANES)).reshape(-1, LANES)
    flow, power, lifted, lower, injections = call(
        second,
        [shift, bar, load, flow, line, upper, lower, power, note, settings],
        [shift_far],
        [(hours, lines)] + [state] * 3 + [(2 * hours, buses)],
        [],
        [shift_v, incidence_v, state_v, state_v],
        FAR_PARTS,
        flops=flops,
    )
    upper, note, sent = call(
        update,
        [came, lifted, note, settings, injections],
        [],
        [state, notes],
        [(ndev * rows_update, LANES)],
        [((ndev * rows_update, LANES), f32)],
        1,
    )
    came = exchange(sent.reshape(ndev, rows_update, LANES)).reshape(-1, LANES)
    flow, power, lifted, lower, grid, injection = call(
        third,
        [shift, injections, load, flow, line, upper, lower, power, note, settings],
        [shift_far],
        [(hours, lines)] + [state] * 4 + [(hours, buses)],
        [],
        [shift_v, incidence_v, state_v],
        FAR_PARTS,
        flops=2 * flops,
    )
    note, total, sent, early = call(
        last,
        [came, lifted, lower, power, grid, note, settings, load, injection],
        [],
        [notes, (ut, LANES)],
        [(ndev, rows_back, LANES), (2 * scen, buses)],
        [
            incidence_v, ((ndev * rows_back, LANES), f32), ((2 * scen, buses), f32), state_v,
            state_v,
        ],
        3,
        flops=flops,
    )
    came = exchange(sent).reshape(-1, LANES)
    total = add_up(total, two_stages)
    own_flow = ((scen * lt, LANES), f32)
    (flow,) = call(
        hourly_flow,
        [shift, line],
        [early, flow_dual.reshape(scen * lt, LANES), shift_far],
        [],
        [(scen, lines)],
        [((2 * scen, buses), f32), own_flow, shift_v, ((scen, lines), f32)],
        FAR_PARTS + 3,
        flops=flops,
    )
    hourly = (scen, ut, LANES)
    power, upper, lower, flow, capacity = call(
        finish,
        [came, total, note, settings, line, shift],
        [flow, shift_far],
        [],
        [hourly, hourly, hourly, (scen, lt, LANES), (1, LANES)],
        [
            shift_v, ((scen, lines), f32), ((ut, LANES), f32),
            (hourly, f32), ((1, LANES), f32), own_flow,
        ],
        6 + FAR_PARTS,
    )
    return (
        power.reshape(scen, 1, units),
        capacity.reshape(LANES),
        flow.reshape(scen, 1, lines),
        upper.reshape(scen, 1, units),
        lower.reshape(scen, 1, units),
    )


def on_device(power, capacity, flow_dual, *rest):
    ndev = lax.axis_size("hour")
    buses = rest[4].shape[1]
    fits = (
        ITERS == 4
        and power.shape[0] == ndev
        and power.shape[1] == 1
        and capacity.shape[0] == LANES
        and flow_dual.shape[2] % (16 * FAR_PARTS * LANES) == 0
        and ndev % (2 * SUBLANES) == 0
        and ndev & (ndev - 1) == 0
        and all(size % (SUBLANES * LANES) == 0 for size in (power.shape[2], flow_dual.shape[2]))
        and buses % LANES == 0
    )
    plan = by_scenarios if fits else by_units
    return plan(power, capacity, flow_dual, *rest)


def solution(mesh):
    return jax.shard_map(
        on_device,
        mesh=mesh,
        in_specs=(
            P("groups", "hour", None),
            P(("groups", "hour")),
            P("groups", "hour", None),
            P("groups", "hour", None),
            P("groups", "hour", None),
            P("groups", "hour"),
            P("groups", "hour", None),
            P(),
            P(),
            P(),
            P(),
            P("groups"),
            P(),
            P(),
        ),
        out_specs=(
            P("groups", "hour", None),
            P(("groups", "hour")),
            P("groups", "hour", None),
            P("groups", "hour", None),
            P("groups", "hour", None),
        ),
        check_vma=False,
    )
```

```python
import jax
import jax.numpy as jnp
from jax import lax
from jax.experimental import pallas as pl
from jax.experimental.pallas import tpu as pltpu
from jax.sharding import PartitionSpec as P

ITERS = 4


primal_step = 0.05
dual_step = 0.01
LANES = 128
SUBLANES = 8
NEAR = 5
FAR_PARTS = 2


def compose(earlier, later):
    return (earlier[0] * later[0], later[0] * earlier[1] + later[1])


def chain_scan(factor, values, reverse):
    factors = jnp.broadcast_to(factor, values.shape)
    return lax.associative_scan(compose, (factors, values), reverse=reverse, axis=1)[1]


def grid_gradient(flow_dual, shift_factors, incidence):
    scen, hours, lines = flow_dual.shape
    bus_dual = jnp.dot(
        flow_dual.astype(jnp.bfloat16).reshape(-1, lines),
        shift_factors,
        preferred_element_type=jnp.float32,
    ).astype(jnp.bfloat16)
    grid_grad = jnp.dot(bus_dual, incidence.T, preferred_element_type=jnp.float32)
    return grid_grad.reshape(scen, hours, incidence.shape[0])


def flow_update(flow_dual, power_bar, load, shift_factors, incidence, line_limit):
    scen, hours, lines = flow_dual.shape
    injection = jnp.dot(
        power_bar.astype(jnp.bfloat16).reshape(-1, incidence.shape[0]),
        incidence,
        preferred_element_type=jnp.float32,
    )
    injection = (injection - load.astype(jnp.float32).reshape(-1, incidence.shape[1])).astype(
        jnp.bfloat16
    )
    flows = jnp.dot(injection, shift_factors.T, preferred_element_type=jnp.float32).reshape(
        scen, hours, lines
    )
    probe = flow_dual + dual_step * flows
    return probe - dual_step * jnp.clip(probe / dual_step, -line_limit, line_limit)


def by_units(
    power,
    capacity,
    flow_dual,
    upper_dual,
    lower_dual,
    price,
    load,
    shift_factors,
    line_limit,
    unit_bus,
    leakage,
    initial_state,
    power_limit,
    capacity_cost,
):
    retain = 1.0 - leakage
    buses = shift_factors.shape[1]
    incidence = (unit_bus[:, None] == jnp.arange(buses, dtype=jnp.int32)[None, :]).astype(
        jnp.bfloat16
    )
    scen, hdev, units = power.shape
    unit_dev = capacity.shape[0]
    ndev = lax.axis_size("hour")
    position = lax.axis_index("hour")
    hours_total = hdev * ndev

    def own(vector):
        return lax.dynamic_slice_in_dim(vector, position * unit_dev, unit_dev)

    upper_units, lower_units = (
        lax.all_to_all(upper_dual, "hour", split_axis=2, concat_axis=1, tiled=True),
        lax.all_to_all(lower_dual, "hour", split_axis=2, concat_axis=1, tiled=True),
    )
    retain_own = own(retain)
    start_own = own(initial_state)
    cost_own = own(capacity_cost)
    for step in range(ITERS):
        grid_grad = grid_gradient(flow_dual, shift_factors, incidence)
        adjoint_units = -chain_scan(retain_own, upper_units - lower_units, True)
        state_grad = lax.all_to_all(adjoint_units, "hour", split_axis=1, concat_axis=2, tiled=True)
        trial_power = jnp.clip(
            power - primal_step * (grid_grad + state_grad - price[:, :, None]),
            -power_limit,
            power_limit,
        )
        dual_total = jnp.sum(upper_units, axis=(0, 1))
        trial_capacity = jnp.maximum(
            capacity - primal_step * (hours_total * cost_own - dual_total / scen), 0.0
        )
        power_bar = 2.0 * trial_power - power
        capacity_bar = 2.0 * trial_capacity - capacity
        flow_dual = flow_update(flow_dual, power_bar, load, shift_factors, incidence, line_limit)
        bar_units = lax.all_to_all(power_bar, "hour", split_axis=2, concat_axis=1, tiled=True)
        driven = -bar_units
        driven = driven.at[:, 0, :].add(retain_own * start_own)
        state_bar = chain_scan(retain_own, driven, False)
        upper_units = jnp.maximum(upper_units + dual_step * (state_bar - capacity_bar), 0.0)
        lower_units = jnp.maximum(lower_units - dual_step * state_bar, 0.0)
        power = trial_power
        capacity = trial_capacity
    upper_dual, lower_dual = (
        lax.all_to_all(upper_units, "hour", split_axis=1, concat_axis=2, tiled=True),
        lax.all_to_all(lower_units, "hour", split_axis=1, concat_axis=2, tiled=True),
    )
    return (power, capacity, flow_dual, upper_dual, lower_dual)


def by_scenarios(
    power,
    capacity,
    flow_dual,
    upper_dual,
    lower_dual,
    price,
    load,
    shift_factors,
    line_limit,
    unit_bus,
    leakage,
    initial_state,
    power_limit,
    capacity_cost,
):
    ndev = lax.axis_size("hour")
    position = lax.axis_index("hour")
    scen = hours = ndev
    units = power.shape[2]
    lines, buses = shift_factors.shape
    ut, lt, bt = units // LANES, lines // LANES, buses // LANES
    near_lines = lines * NEAR // 16
    small = -(-(bt + 2) // SUBLANES) * SUBLANES
    at_power, at_upper, at_lower, at_flow = 0, ut, 2 * ut, 3 * ut
    at_total = at_flow + lt
    at_load = at_total
    at_price, at_capacity = at_load + bt, at_load + bt + 1
    rows_in = at_load + small
    back_bus = 3 * ut
    rows_back = back_bus + 2 * bt
    rows_update = ut + 2 * bt
    f32, bf16 = jnp.float32, jnp.bfloat16
    state = (hours * ut, LANES)

    def call(body, near, far, outs, outs_far, scratch, copies, flops=0):
        moved = sum(a.size * a.dtype.itemsize for a in near + far)
        inner, outer = (pl.BlockSpec(memory_space=m) for m in (pltpu.VMEM, pltpu.HBM))
        return pl.pallas_call(
            body,
            out_shape=[pltpu.VMEM(*s) if isinstance(s[0], tuple) else pltpu.VMEM(s, f32) for s in outs]
            + [pltpu.HBM(s, f32) for s in outs_far],
            in_specs=[inner] * len(near) + [outer] * len(far),
            out_specs=[inner] * len(outs) + [outer] * len(outs_far),
            scratch_shapes=[pltpu.VMEM(*s) for s in scratch] + [pltpu.SemaphoreType.DMA((copies,))],
            compiler_params=pltpu.CompilerParams(vmem_limit_bytes=24 * 1024 * 1024),
            cost_estimate=pl.CostEstimate(flops=flops, bytes_accessed=moved, transcendentals=0),
        )(*near, *(pltpu.with_memory_space_constraint(a, pltpu.HBM) for a in far))

    class Copies:
        def __init__(self, semaphores):
            self.semaphores, self.count, self.sent = semaphores, 0, []

        def bring(self, source, target):
            copy = pltpu.make_async_copy(source, target, self.semaphores.at[self.count])
            self.count += 1
            copy.start()
            return copy

        def send(self, source, target):
            self.sent.append(self.bring(source, target))

        def close(self):
            for copy in self.sent:
                copy.wait()

    def gather_up(value, stages):
        terms = [value]
        for stage in stages:
            value = sum(terms)
            terms = [value] + [
                lax.ppermute(value, "hour", [(j, j ^ other) for j in range(ndev)])
                for other in stage
            ]
        return terms

    bits = [1 << b for b in range(ndev.bit_length() - 1)]
    half = 1 << (len(bits) // 2)
    two_stages = [range(1, half), range(half, ndev, half)]

    def exchange(blocks):
        return lax.all_to_all(blocks, "hour", split_axis=0, concat_axis=0, tiled=True)

    def rows(ref, first, step):
        return ref[pl.ds(first, ref.shape[0] // step, stride=step), :]

    def wide(ref, first, count, step):
        return jnp.concatenate([rows(ref, first + j, step) for j in range(count)], axis=1)

    def spread(ref, first, step, value):
        for j in range(value.shape[1] // LANES):
            ref[pl.ds(first + j, value.shape[0], stride=step), :] = value[
                :, j * LANES : (j + 1) * LANES
            ]

    def part(ref, index):
        return ref[pl.ds(index * ut, ut), :]

    def bring_lines(copies, near, far, far_v, axis=0):
        size = (lines - near_lines) // FAR_PARTS
        result = [(pl.ds(0, near_lines), near, lambda: None)]
        for c in range(FAR_PARTS):
            source, target = pl.ds(near_lines + c * size, size), pl.ds(c * size, size)
            if axis == 0:
                part_v = far_v.at[target]
                copy = copies.bring(far.at[source], part_v)
            else:
                part_v = far_v.at[:, target]
                copy = copies.bring(far.at[:, source], part_v)
            result.append((source, part_v, copy.wait))
        return result

    def arrived(factors):
        return [(at, part_v, lambda: None) for at, part_v, _ in factors]

    def one_hot(settings, incidence):
        buses_of = lax.broadcasted_iota(jnp.int32, (buses, LANES), 0).astype(f32)
        for j in range(ut):
            same = buses_of == settings[pl.ds(4 * ut + j, 1), :]
            incidence[:, pl.ds(j * LANES, LANES)] = jnp.where(same, 1.0, 0.0).astype(bf16)

    def to_units(bus_dual, incidence, grid):
        spread(
            grid, 0, ut,
            jnp.dot(bus_dual.astype(bf16), incidence[...], preferred_element_type=f32),
        )

    def across(left, right):
        return lax.dot_general(left, right, (((1,), (1,)), ((), ())), preferred_element_type=f32)

    def inject(bar, load, incidence):
        wide_bar = wide(bar, 0, ut, ut).astype(bf16)
        return (across(wide_bar, incidence[...]) - load[...]).astype(bf16)

    def to_buses(flow, shift):
        total = jnp.zeros((hours, buses), f32)
        for at, factors, wait in shift:
            wait()
            total = total + jnp.dot(
                flow[:, at].astype(bf16), factors[...], preferred_element_type=f32
            )
        return total

    def held_back(probe, limit, at):
        bound = dual_step * limit[:, at]
        return probe - jnp.clip(probe, -bound, bound)

    def network(injection, flow, shift, limit, incidence, new_flow, grid):
        for at, factors, wait in shift:
            wait()
            probe = flow[:, at] + dual_step * across(injection, factors[...])
            new_flow[:, at] = held_back(probe, limit, at)
        to_units(to_buses(new_flow, arrived(shift)), incidence, grid)

    def local(upper, lower, before, grid, price, settings, put_power, bar, put):
        keep, bound = part(settings, 0), part(settings, 2)
        carry = jnp.zeros((ut, LANES), f32)
        for hour in reversed(range(hours)):
            carry = keep * carry + (upper(hour) - lower(hour))
            old = before(hour)
            gradient = part(grid, hour) - carry - price(hour)
            trial = jnp.clip(old - primal_step * gradient, -bound, bound)
            put_power(hour, trial)
            bar[pl.ds(hour * ut, ut), :] = 2.0 * trial - old
        level = part(settings, 1)
        for hour in range(hours):
            level = keep * level - part(bar, hour)
            put(
                hour,
                upper(hour) + dual_step * level,
                jnp.maximum(lower(hour) - dual_step * level, 0.0),
            )

    def capacities(capacity, settings, total):
        cost = part(settings, 3)
        trial = jnp.maximum(capacity - primal_step * (hours * cost - total / scen), 0.0)
        return trial, dual_step * (2.0 * trial - capacity)

    def sum_blocks(ref, first, step):
        return sum(ref[pl.ds(hour * step + first, ut), :] for hour in range(hours))

    def reader(ref):
        return lambda hour: part(ref, hour)

    def writer(ref):
        def put(hour, value):
            ref[pl.ds(hour * ut, ut), :] = value

        return put


    def pack(power, upper, lower, flow, load, price, capacity, *rest):
        vectors, shift_far, unit_bus, total_o, settings, shift, out = rest[:4], *rest[4:10]
        load_v, price_v, capacity_v, units_v, blocks_v, semaphores = rest[10:]
        copies = Copies(semaphores)
        blocks = blocks_v.reshape(ndev, rows_in, LANES)
        places = [
            blocks.at[:, pl.ds(at, source.shape[1])]
            for source, at in (
                (upper, at_upper), (flow, at_flow), (power, at_power), (lower, at_lower),
            )
        ]
        big = [copies.bring(*pair) for pair in zip((upper, flow, power, lower), places)]
        come = [
            copies.bring(load, load_v),
            copies.bring(price, price_v),
            copies.bring(capacity, capacity_v),
            copies.bring(unit_bus, units_v),
        ] + [
            copies.bring(vector, settings.at[pl.ds(place * ut, ut)])
            for place, vector in enumerate(vectors)
        ]
        copies.send(shift_far.at[pl.ds(0, near_lines)], shift)
        for peer in range(ndev):
            blocks_v[pl.ds(peer * rows_in + at_load, small), :] = jnp.zeros((small, LANES), f32)
        for copy in come:
            copy.wait()
        spread(blocks_v, at_load, rows_in, load_v[...].astype(f32))
        across = lax.broadcasted_iota(jnp.int32, (ndev, ndev), 0)
        along = lax.broadcasted_iota(jnp.int32, (ndev, ndev), 1)
        own_price = jnp.sum(
            jnp.where(across == along, jnp.broadcast_to(price_v[...], (ndev, ndev)), 0.0),
            axis=1, keepdims=True,
        )
        spread(blocks_v, at_price, rows_in, jnp.broadcast_to(own_price, (ndev, LANES)))
        spread(blocks_v, at_capacity, rows_in, jnp.broadcast_to(capacity_v[...], (ndev, LANES)))
        for copy in big:
            copy.wait()
        copies.send(blocks, out)
        total_o[...] = sum_blocks(blocks_v, at_upper, rows_in)
        settings[pl.ds(0, ut), :] = 1.0 - settings[pl.ds(0, ut), :]
        settings[pl.ds(4 * ut, ut), :] = units_v[...].astype(f32)
        copies.close()

    def first(came, shift, settings, shift_far, turned, *rest):
        del turned
        power, lifted, lower, bar, flow, load, notes, shift_v, incidence, grid, semaphores = rest
        copies = Copies(semaphores)
        factors = bring_lines(copies, shift, shift_far, shift_v)
        flow[...] = wide(came, at_flow, lt, rows_in)
        load[...] = wide(came, at_load, bt, rows_in)
        notes[pl.ds(ut, hours), :] = rows(came, at_price, rows_in)
        one_hot(settings, incidence)
        notes[pl.ds(0, ut), :] = rows(came, at_capacity, rows_in)
        to_units(to_buses(flow, factors), incidence, grid)
        def received(first_row, count=ut):
            return lambda hour: came[pl.ds(hour * rows_in + first_row, count), :]

        local(
            received(at_upper), received(at_lower), received(at_power), grid,
            received(at_price, 1), settings, writer(power), bar, lift(lifted, lower),
        )

    def begin(lifted, notes, settings, *rest):
        *terms, upper, new_notes, total_o, out, semaphores = rest
        total = raise_upper(sum(term[...] for term in terms), lifted, notes, settings, upper, new_notes)
        for peer in range(ndev):
            out[pl.ds(peer * ut, ut), :] = total
        copies = Copies(semaphores)
        copies.send(out, total_o)
        copies.close()

    def second(
        shift, bar, load, flow, line, upper, lower, power, notes, settings, shift_far,
        new_flow, new_power, lifted, low, sent, shift_v, incidence, grid, new_bar, semaphores,
    ):
        factors = bring_lines(Copies(semaphores), shift, shift_far, shift_v)
        one_hot(settings, incidence)
        injection = inject(bar, load, incidence)
        sent[pl.ds(0, hours), :] = injection.astype(f32)
        network(injection, flow, factors, line, incidence, new_flow, grid)
        local(
            reader(upper), reader(lower), reader(power), grid,
            lambda hour: notes[pl.ds(ut + hour, 1), :], settings, writer(new_power), new_bar,
            lift(lifted, low),
        )
        sent[pl.ds(hours, hours), :] = inject(new_bar, load, incidence).astype(f32)

    def third(
        shift, sent, load, flow, line, upper, lower, power, notes, settings, shift_far,
        new_flow, new_power, lifted, low, grid, later,
        shift_v, incidence, new_bar, semaphores,
    ):
        factors = bring_lines(Copies(semaphores), shift, shift_far, shift_v)
        one_hot(settings, incidence)
        injection = sent[pl.ds(hours, hours), :].astype(bf16)
        network(injection, flow, factors, line, incidence, new_flow, grid)
        local(
            reader(upper), reader(lower), reader(power), grid,
            lambda hour: notes[pl.ds(ut + hour, 1), :], settings, writer(new_power), new_bar,
            lift(lifted, low),
        )
        injection = inject(new_bar, load, incidence)
        later[...] = injection.astype(f32)
        network(injection, new_flow, arrived(factors), line, incidence, new_flow, grid)

    def lift(lifted, low):
        def put(hour, new_lifted, new_low):
            lifted[pl.ds(hour * ut, ut), :] = new_lifted
            low[pl.ds(hour * ut, ut), :] = new_low

        return put

    def raise_upper(total, lifted, notes, settings, upper, new_notes):
        capacity, pull = capacities(part(notes, 0), settings, total)
        new_notes[pl.ds(0, ut), :] = capacity
        new_notes[pl.ds(ut, hours), :] = notes[pl.ds(ut, hours), :]
        total = jnp.zeros((ut, LANES), f32)
        for hour in range(hours):
            new = jnp.maximum(part(lifted, hour) - pull, 0.0)
            upper[pl.ds(hour * ut, ut), :] = new
            total = total + new
        return total

    def update(came, lifted, notes, settings, sent, upper, new_notes, out_o, out, semaphores):
        spread(out, ut, rows_update, sent[pl.ds(0, hours), :])
        spread(out, ut + bt, rows_update, sent[pl.ds(hours, hours), :])
        total = raise_upper(sum_blocks(came, 0, ut), lifted, notes, settings, upper, new_notes)
        for peer in range(ndev):
            out[pl.ds(peer * rows_update, ut), :] = total
        copies = Copies(semaphores)
        copies.send(out, out_o)
        copies.close()

    def last(
        came, lifted, lower, power, grid, notes, settings, load, later,
        new_notes, total_o, out_o, early_o, incidence, out, early, upper, bar, semaphores,
    ):
        copies = Copies(semaphores)
        for step in range(2):
            early[pl.ds(step * scen, scen), :] = wide(came, ut + step * bt, bt, rows_update)
        copies.send(early, early_o)
        total = raise_upper(
            sum_blocks(came, 0, rows_update), lifted, notes, settings, upper, new_notes
        )
        total_o[...] = total

        def put_power(hour, value):
            out[pl.ds(hour * rows_back, ut), :] = value

        def put(hour, new_lifted, low):
            out[pl.ds(hour * rows_back + ut, ut), :] = new_lifted
            out[pl.ds(hour * rows_back + 2 * ut, ut), :] = low

        local(
            reader(upper), reader(lower), reader(power), grid,
            lambda hour: notes[pl.ds(ut + hour, 1), :], settings, put_power, bar, put,
        )
        blocks = out.reshape(ndev, rows_back, LANES)
        at = pl.ds(0, back_bus)
        copies.send(blocks.at[:, at], out_o.at[:, at])
        one_hot(settings, incidence)
        spread(out, back_bus, rows_back, later[...])
        spread(out, back_bus + bt, rows_back, inject(bar, load, incidence).astype(f32))
        at = pl.ds(back_bus, rows_back - back_bus)
        copies.send(blocks.at[:, at], out_o.at[:, at])
        copies.close()

    def two_steps(value, injections, factors, line, at):
        flows = dual_step * jnp.dot(injections, factors[...], preferred_element_type=f32)
        for step in range(2):
            value = held_back(value + flows[step * scen : (step + 1) * scen], line, at)
        return value

    def hourly_flow(
        turned, line, early, flow, turned_far, new_o, early_v, flow_v, turned_v, new, semaphores
    ):
        copies = Copies(semaphores)
        come = [copies.bring(early, early_v), copies.bring(flow, flow_v)]
        factors = bring_lines(copies, turned, turned_far, turned_v, 1)
        for copy in come:
            copy.wait()
        injections = early_v[...].astype(bf16)
        new[...] = wide(flow_v, 0, lt, lt)
        for at, part_v, wait in factors:
            wait()
            new[:, at] = two_steps(new[:, at], injections, part_v, line, at)
        copies.send(new, new_o)
        copies.close()

    def finish(
        came, line, turned, flow, turned_far, power_o, lower_o, flow_o,
        turned_v, flow_v, out, semaphores,
    ):
        copies = Copies(semaphores)
        flow_came = copies.bring(flow, flow_v)
        factors = bring_lines(copies, turned, turned_far, turned_v, 1)
        blocks = came.reshape(ndev, rows_back, LANES)
        copies.send(blocks.at[:, pl.ds(0, ut)], power_o)
        copies.send(blocks.at[:, pl.ds(2 * ut, ut)], lower_o)
        injections = jnp.concatenate(
            [wide(came, back_bus + step * bt, bt, rows_back) for step in range(2)], axis=0
        ).astype(bf16)
        flow_came.wait()
        row = 0
        for at, part_v, wait in factors:
            wait()
            value = two_steps(flow_v[:, at], injections, part_v, line, at)
            spread(out, row, lt, value)
            row += value.shape[1] // LANES
        copies.send(out.reshape(scen, lt, LANES), flow_o)
        copies.close()

    def finish_upper(came, notes, settings, *rest):
        *terms, upper_o, capacity_o, notes_v, upper, own, semaphores = rest
        copies = Copies(semaphores)
        capacity, pull = capacities(
            part(notes, 0), settings, sum(term[...] for term in terms)
        )
        for peer in range(ndev):
            upper[peer] = jnp.maximum(came[pl.ds(peer * rows_back + ut, ut), :] - pull, 0.0)
        copies.send(upper, upper_o)
        notes_v[...] = capacity
        own[...] = notes_v[pl.ds(lax.axis_index("hour"), 1), :]
        copies.send(own, capacity_o)
        copies.close()


    def tiles(vector):
        return vector.reshape(-1, LANES)

    line = line_limit.reshape(1, lines)
    shift_far, turned = shift_factors, shift_factors.T
    turned_near = turned[:, :near_lines]

    state_v, incidence_v = (state, f32), ((buses, units), bf16)
    shift_v, turned_v = ((lines - near_lines, buses), bf16), ((buses, lines - near_lines), bf16)
    notes = (ut + hours, LANES)
    flops = 4 * hours * buses * (lines + units)

    total, settings, shift, sent = call(
        pack,
        [],
        [
            power.reshape(scen, ut, LANES),
            upper_dual.reshape(scen, ut, LANES),
            lower_dual.reshape(scen, ut, LANES),
            flow_dual.reshape(scen, lt, LANES),
            load.reshape(scen, buses),
            price.reshape(1, scen),
            capacity.reshape(1, LANES),
            tiles(leakage),
            tiles(initial_state),
            tiles(power_limit),
            tiles(capacity_cost),
            shift_far,
            tiles(unit_bus),
        ],
        [(ut, LANES), (5 * ut, LANES), ((near_lines, buses), bf16)],
        [(ndev, rows_in, LANES)],
        [
            ((scen, buses), bf16), ((1, scen), f32), ((1, LANES), f32), ((ut, LANES), jnp.int32),
            ((ndev * rows_in, LANES), f32),
        ],
        14,
    )
    came = exchange(sent).reshape(-1, LANES)
    totals = gather_up(total, two_stages)
    power, lifted, lower, bar, flow, load, note = call(
        first,
        [came, shift, settings],
        [shift_far, turned],
        [state] * 4 + [(hours, lines), (hours, buses), notes],
        [],
        [shift_v, incidence_v, state_v],
        FAR_PARTS,
        flops=flops,
    )
    upper, note, total = call(
        begin, [lifted, note, settings, *totals], [], [state, notes], [state], [state_v], 1
    )
    came = exchange(total.reshape(ndev, ut, LANES)).reshape(-1, LANES)
    flow, power, lifted, lower, injections = call(
        second,
        [shift, bar, load, flow, line, upper, lower, power, note, settings],
        [shift_far],
        [(hours, lines)] + [state] * 3 + [(2 * hours, buses)],
        [],
        [shift_v, incidence_v, state_v, state_v],
        FAR_PARTS,
        flops=flops,
    )
    upper, note, sent = call(
        update,
        [came, lifted, note, settings, injections],
        [],
        [state, notes],
        [(ndev * rows_update, LANES)],
        [((ndev * rows_update, LANES), f32)],
        1,
    )
    came = exchange(sent.reshape(ndev, rows_update, LANES)).reshape(-1, LANES)
    flow, power, lifted, lower, grid, injection = call(
        third,
        [shift, injections, load, flow, line, upper, lower, power, note, settings],
        [shift_far],
        [(hours, lines)] + [state] * 4 + [(hours, buses)],
        [],
        [shift_v, incidence_v, state_v],
        FAR_PARTS,
        flops=2 * flops,
    )
    note, total, sent, early = call(
        last,
        [came, lifted, lower, power, grid, note, settings, load, injection],
        [],
        [notes, (ut, LANES)],
        [(ndev, rows_back, LANES), (2 * scen, buses)],
        [
            incidence_v, ((ndev * rows_back, LANES), f32), ((2 * scen, buses), f32), state_v,
            state_v,
        ],
        3,
        flops=flops,
    )
    came = exchange(sent).reshape(-1, LANES)
    totals = gather_up(total, two_stages)
    own_flow = ((scen * lt, LANES), f32)
    (flow,) = call(
        hourly_flow,
        [turned_near, line],
        [early, flow_dual.reshape(scen * lt, LANES), turned],
        [],
        [(scen, lines)],
        [((2 * scen, buses), f32), own_flow, turned_v, ((scen, lines), f32)],
        FAR_PARTS + 3,
        flops=flops,
    )
    hourly = (scen, ut, LANES)
    power, lower, flow = call(
        finish,
        [came, line, turned_near],
        [flow, turned],
        [],
        [hourly, hourly, (scen, lt, LANES)],
        [turned_v, ((scen, lines), f32), own_flow],
        FAR_PARTS + 4,
        flops=flops,
    )
    upper, capacity = call(
        finish_upper,
        [came, note, settings, *totals],
        [],
        [],
        [hourly, (1, LANES)],
        [((ut, LANES), f32), (hourly, f32), ((1, LANES), f32)],
        2,
    )
    return (
        power.reshape(scen, 1, units),
        capacity.reshape(LANES),
        flow.reshape(scen, 1, lines),
        upper.reshape(scen, 1, units),
        lower.reshape(scen, 1, units),
    )


def on_device(power, capacity, flow_dual, *rest):
    ndev = lax.axis_size("hour")
    buses = rest[4].shape[1]
    fits = (
        ITERS == 4
        and power.shape[0] == ndev
        and power.shape[1] == 1
        and capacity.shape[0] == LANES
        and flow_dual.shape[2] % (16 * FAR_PARTS * LANES) == 0
        and ndev % (2 * SUBLANES) == 0
        and ndev & (ndev - 1) == 0
        and all(size % (SUBLANES * LANES) == 0 for size in (power.shape[2], flow_dual.shape[2]))
        and buses % LANES == 0
    )
    plan = by_scenarios if fits else by_units
    return plan(power, capacity, flow_dual, *rest)


def solution(mesh):
    return jax.shard_map(
        on_device,
        mesh=mesh,
        in_specs=(
            P("groups", "hour", None),
            P(("groups", "hour")),
            P("groups", "hour", None),
            P("groups", "hour", None),
            P("groups", "hour", None),
            P("groups", "hour"),
            P("groups", "hour", None),
            P(),
            P(),
            P(),
            P(),
            P("groups"),
            P(),
            P(),
        ),
        out_specs=(
            P("groups", "hour", None),
            P(("groups", "hour")),
            P("groups", "hour", None),
            P("groups", "hour", None),
            P("groups", "hour", None),
        ),
        check_vma=False,
    )
```

```python
import jax
import jax.numpy as jnp
from jax import lax
from jax.experimental import pallas as pl
from jax.experimental.pallas import tpu as pltpu
from jax.sharding import PartitionSpec as P

ITERS = 4


primal_step = 0.05
dual_step = 0.01
LANES = 128
SUBLANES = 8
NEAR = 4
FAR_PARTS = 3


def compose(earlier, later):
    return (earlier[0] * later[0], later[0] * earlier[1] + later[1])


def chain_scan(factor, values, reverse):
    factors = jnp.broadcast_to(factor, values.shape)
    return lax.associative_scan(compose, (factors, values), reverse=reverse, axis=1)[1]


def grid_gradient(flow_dual, shift_factors, incidence):
    scen, hours, lines = flow_dual.shape
    bus_dual = jnp.dot(
        flow_dual.astype(jnp.bfloat16).reshape(-1, lines),
        shift_factors,
        preferred_element_type=jnp.float32,
    ).astype(jnp.bfloat16)
    grid_grad = jnp.dot(bus_dual, incidence.T, preferred_element_type=jnp.float32)
    return grid_grad.reshape(scen, hours, incidence.shape[0])


def flow_update(flow_dual, power_bar, load, shift_factors, incidence, line_limit):
    scen, hours, lines = flow_dual.shape
    injection = jnp.dot(
        power_bar.astype(jnp.bfloat16).reshape(-1, incidence.shape[0]),
        incidence,
        preferred_element_type=jnp.float32,
    )
    injection = (injection - load.astype(jnp.float32).reshape(-1, incidence.shape[1])).astype(
        jnp.bfloat16
    )
    flows = jnp.dot(injection, shift_factors.T, preferred_element_type=jnp.float32).reshape(
        scen, hours, lines
    )
    probe = flow_dual + dual_step * flows
    return probe - dual_step * jnp.clip(probe / dual_step, -line_limit, line_limit)


def by_units(
    power,
    capacity,
    flow_dual,
    upper_dual,
    lower_dual,
    price,
    load,
    shift_factors,
    line_limit,
    unit_bus,
    leakage,
    initial_state,
    power_limit,
    capacity_cost,
):
    retain = 1.0 - leakage
    buses = shift_factors.shape[1]
    incidence = (unit_bus[:, None] == jnp.arange(buses, dtype=jnp.int32)[None, :]).astype(
        jnp.bfloat16
    )
    scen, hdev, units = power.shape
    unit_dev = capacity.shape[0]
    ndev = lax.axis_size("hour")
    position = lax.axis_index("hour")
    hours_total = hdev * ndev

    def own(vector):
        return lax.dynamic_slice_in_dim(vector, position * unit_dev, unit_dev)

    upper_units, lower_units = (
        lax.all_to_all(upper_dual, "hour", split_axis=2, concat_axis=1, tiled=True),
        lax.all_to_all(lower_dual, "hour", split_axis=2, concat_axis=1, tiled=True),
    )
    retain_own = own(retain)
    start_own = own(initial_state)
    cost_own = own(capacity_cost)
    for step in range(ITERS):
        grid_grad = grid_gradient(flow_dual, shift_factors, incidence)
        adjoint_units = -chain_scan(retain_own, upper_units - lower_units, True)
        state_grad = lax.all_to_all(adjoint_units, "hour", split_axis=1, concat_axis=2, tiled=True)
        trial_power = jnp.clip(
            power - primal_step * (grid_grad + state_grad - price[:, :, None]),
            -power_limit,
            power_limit,
        )
        dual_total = jnp.sum(upper_units, axis=(0, 1))
        trial_capacity = jnp.maximum(
            capacity - primal_step * (hours_total * cost_own - dual_total / scen), 0.0
        )
        power_bar = 2.0 * trial_power - power
        capacity_bar = 2.0 * trial_capacity - capacity
        flow_dual = flow_update(flow_dual, power_bar, load, shift_factors, incidence, line_limit)
        bar_units = lax.all_to_all(power_bar, "hour", split_axis=2, concat_axis=1, tiled=True)
        driven = -bar_units
        driven = driven.at[:, 0, :].add(retain_own * start_own)
        state_bar = chain_scan(retain_own, driven, False)
        upper_units = jnp.maximum(upper_units + dual_step * (state_bar - capacity_bar), 0.0)
        lower_units = jnp.maximum(lower_units - dual_step * state_bar, 0.0)
        power = trial_power
        capacity = trial_capacity
    upper_dual, lower_dual = (
        lax.all_to_all(upper_units, "hour", split_axis=1, concat_axis=2, tiled=True),
        lax.all_to_all(lower_units, "hour", split_axis=1, concat_axis=2, tiled=True),
    )
    return (power, capacity, flow_dual, upper_dual, lower_dual)


def by_scenarios(
    power,
    capacity,
    flow_dual,
    upper_dual,
    lower_dual,
    price,
    load,
    shift_factors,
    line_limit,
    unit_bus,
    leakage,
    initial_state,
    power_limit,
    capacity_cost,
):
    ndev = lax.axis_size("hour")
    position = lax.axis_index("hour")
    scen = hours = ndev
    units = power.shape[2]
    lines, buses = shift_factors.shape
    ut, lt, bt = units // LANES, lines // LANES, buses // LANES
    near_lines = lines * NEAR // 16
    small = -(-(bt + 2) // SUBLANES) * SUBLANES
    at_power, at_upper, at_lower, at_flow = 0, ut, 2 * ut, 3 * ut
    at_total = at_flow + lt
    at_load = at_total
    at_price, at_capacity = at_load + bt, at_load + bt + 1
    rows_in = at_load + small
    back_bus = 3 * ut
    rows_back = back_bus + 2 * bt
    rows_update = ut + 2 * bt
    f32, bf16 = jnp.float32, jnp.bfloat16
    state = (hours * ut, LANES)

    def call(body, near, far, outs, outs_far, scratch, copies, flops=0):
        moved = sum(a.size * a.dtype.itemsize for a in near + far)
        inner, outer = (pl.BlockSpec(memory_space=m) for m in (pltpu.VMEM, pltpu.HBM))
        return pl.pallas_call(
            body,
            out_shape=[pltpu.VMEM(*s) if isinstance(s[0], tuple) else pltpu.VMEM(s, f32) for s in outs]
            + [pltpu.HBM(s, f32) for s in outs_far],
            in_specs=[inner] * len(near) + [outer] * len(far),
            out_specs=[inner] * len(outs) + [outer] * len(outs_far),
            scratch_shapes=[pltpu.VMEM(*s) for s in scratch] + [pltpu.SemaphoreType.DMA((copies,))],
            compiler_params=pltpu.CompilerParams(vmem_limit_bytes=24 * 1024 * 1024),
            cost_estimate=pl.CostEstimate(flops=flops, bytes_accessed=moved, transcendentals=0),
        )(*near, *(pltpu.with_memory_space_constraint(a, pltpu.HBM) for a in far))

    class Copies:
        def __init__(self, semaphores):
            self.semaphores, self.count, self.sent = semaphores, 0, []

        def bring(self, source, target):
            copy = pltpu.make_async_copy(source, target, self.semaphores.at[self.count])
            self.count += 1
            copy.start()
            return copy

        def send(self, source, target):
            self.sent.append(self.bring(source, target))

        def close(self):
            for copy in self.sent:
                copy.wait()

    def gather_up(value, stages):
        terms = [value]
        for stage in stages:
            value = sum(terms)
            terms = [value] + [
                lax.ppermute(value, "hour", [(j, j ^ other) for j in range(ndev)])
                for other in stage
            ]
        return terms

    bits = [1 << b for b in range(ndev.bit_length() - 1)]
    half = 1 << (len(bits) // 2)
    two_stages = [range(1, half), range(half, ndev, half)]
    three_stages = [range(1, half)] + [[bit] for bit in bits if bit >= half]

    def exchange(blocks):
        return lax.all_to_all(blocks, "hour", split_axis=0, concat_axis=0, tiled=True)

    def rows(ref, first, step):
        return ref[pl.ds(first, ref.shape[0] // step, stride=step), :]

    def wide(ref, first, count, step):
        return jnp.concatenate([rows(ref, first + j, step) for j in range(count)], axis=1)

    def spread(ref, first, step, value):
        for j in range(value.shape[1] // LANES):
            ref[pl.ds(first + j, value.shape[0], stride=step), :] = value[
                :, j * LANES : (j + 1) * LANES
            ]

    def part(ref, index):
        return ref[pl.ds(index * ut, ut), :]

    def bring_lines(copies, near, far, far_v, axis=0):
        size = (lines - near_lines) // FAR_PARTS
        result = [(pl.ds(0, near_lines), near, lambda: None)]
        for c in range(FAR_PARTS):
            source, target = pl.ds(near_lines + c * size, size), pl.ds(c * size, size)
            if axis == 0:
                part_v = far_v.at[target]
                copy = copies.bring(far.at[source], part_v)
            else:
                part_v = far_v.at[:, target]
                copy = copies.bring(far.at[:, source], part_v)
            result.append((source, part_v, copy.wait))
        return result

    def arrived(factors):
        return [(at, part_v, lambda: None) for at, part_v, _ in factors]

    def one_hot(settings, incidence):
        buses_of = lax.broadcasted_iota(jnp.int32, (buses, LANES), 0).astype(f32)
        for j in range(ut):
            same = buses_of == settings[pl.ds(4 * ut + j, 1), :]
            incidence[:, pl.ds(j * LANES, LANES)] = jnp.where(same, 1.0, 0.0).astype(bf16)

    def to_units(bus_dual, incidence, grid):
        spread(
            grid, 0, ut,
            jnp.dot(bus_dual.astype(bf16), incidence[...], preferred_element_type=f32),
        )

    def across(left, right):
        return lax.dot_general(left, right, (((1,), (1,)), ((), ())), preferred_element_type=f32)

    def inject(bar, load, incidence):
        wide_bar = wide(bar, 0, ut, ut).astype(bf16)
        return (across(wide_bar, incidence[...]) - load[...]).astype(bf16)

    def to_buses(flow, shift):
        total = jnp.zeros((hours, buses), f32)
        for at, factors, wait in shift:
            wait()
            total = total + jnp.dot(
                flow[:, at].astype(bf16), factors[...], preferred_element_type=f32
            )
        return total

    def held_back(probe, limit, at):
        bound = dual_step * limit[:, at]
        return probe - jnp.clip(probe, -bound, bound)

    def network(injection, flow, shift, limit, incidence, new_flow, grid):
        for at, factors, wait in shift:
            wait()
            probe = flow[:, at] + dual_step * across(injection, factors[...])
            new_flow[:, at] = held_back(probe, limit, at)
        to_units(to_buses(new_flow, arrived(shift)), incidence, grid)

    def local(upper, lower, before, grid, price, settings, put_power, bar, put):
        keep, bound = part(settings, 0), part(settings, 2)
        carry = jnp.zeros((ut, LANES), f32)
        for hour in reversed(range(hours)):
            carry = keep * carry + (upper(hour) - lower(hour))
            old = before(hour)
            gradient = part(grid, hour) - carry - price(hour)
            trial = jnp.clip(old - primal_step * gradient, -bound, bound)
            put_power(hour, trial)
            bar[pl.ds(hour * ut, ut), :] = 2.0 * trial - old
        level = part(settings, 1)
        for hour in range(hours):
            level = keep * level - part(bar, hour)
            put(
                hour,
                upper(hour) + dual_step * level,
                jnp.maximum(lower(hour) - dual_step * level, 0.0),
            )

    def capacities(capacity, settings, total):
        cost = part(settings, 3)
        trial = jnp.maximum(capacity - primal_step * (hours * cost - total / scen), 0.0)
        return trial, dual_step * (2.0 * trial - capacity)

    def sum_blocks(ref, first, step):
        return sum(ref[pl.ds(hour * step + first, ut), :] for hour in range(hours))

    def reader(ref):
        return lambda hour: part(ref, hour)

    def writer(ref):
        def put(hour, value):
            ref[pl.ds(hour * ut, ut), :] = value

        return put


    def pack(power, upper, lower, flow, load, price, capacity, *rest):
        vectors, shift_far, unit_bus, total_o, settings, shift, out = rest[:4], *rest[4:10]
        load_v, price_v, capacity_v, units_v, blocks_v, semaphores = rest[10:]
        copies = Copies(semaphores)
        blocks = blocks_v.reshape(ndev, rows_in, LANES)
        places = [
            blocks.at[:, pl.ds(at, source.shape[1])]
            for source, at in (
                (upper, at_upper), (flow, at_flow), (power, at_power), (lower, at_lower),
            )
        ]
        big = [copies.bring(*pair) for pair in zip((upper, flow, power, lower), places)]
        come = [
            copies.bring(load, load_v),
            copies.bring(price, price_v),
            copies.bring(capacity, capacity_v),
            copies.bring(unit_bus, units_v),
        ] + [
            copies.bring(vector, settings.at[pl.ds(place * ut, ut)])
            for place, vector in enumerate(vectors)
        ]
        copies.send(shift_far.at[pl.ds(0, near_lines)], shift)
        for peer in range(ndev):
            blocks_v[pl.ds(peer * rows_in + at_load, small), :] = jnp.zeros((small, LANES), f32)
        for copy in come:
            copy.wait()
        spread(blocks_v, at_load, rows_in, load_v[...].astype(f32))
        across = lax.broadcasted_iota(jnp.int32, (ndev, ndev), 0)
        along = lax.broadcasted_iota(jnp.int32, (ndev, ndev), 1)
        own_price = jnp.sum(
            jnp.where(across == along, jnp.broadcast_to(price_v[...], (ndev, ndev)), 0.0),
            axis=1, keepdims=True,
        )
        spread(blocks_v, at_price, rows_in, jnp.broadcast_to(own_price, (ndev, LANES)))
        spread(blocks_v, at_capacity, rows_in, jnp.broadcast_to(capacity_v[...], (ndev, LANES)))
        for copy in big:
            copy.wait()
        copies.send(blocks, out)
        total_o[...] = sum_blocks(blocks_v, at_upper, rows_in)
        settings[pl.ds(0, ut), :] = 1.0 - settings[pl.ds(0, ut), :]
        settings[pl.ds(4 * ut, ut), :] = units_v[...].astype(f32)
        copies.close()

    def first(came, shift, settings, shift_far, turned, *rest):
        del turned
        power, lifted, lower, bar, flow, load, notes, shift_v, incidence, grid, semaphores = rest
        copies = Copies(semaphores)
        factors = bring_lines(copies, shift, shift_far, shift_v)
        flow[...] = wide(came, at_flow, lt, rows_in)
        load[...] = wide(came, at_load, bt, rows_in)
        notes[pl.ds(ut, hours), :] = rows(came, at_price, rows_in)
        one_hot(settings, incidence)
        notes[pl.ds(0, ut), :] = rows(came, at_capacity, rows_in)
        to_units(to_buses(flow, factors), incidence, grid)
        def received(first_row, count=ut):
            return lambda hour: came[pl.ds(hour * rows_in + first_row, count), :]

        local(
            received(at_upper), received(at_lower), received(at_power), grid,
            received(at_price, 1), settings, writer(power), bar, lift(lifted, lower),
        )

    def begin(lifted, notes, settings, *rest):
        *terms, upper, new_notes, total_o, out, semaphores = rest
        total = raise_upper(sum(term[...] for term in terms), lifted, notes, settings, upper, new_notes)
        for peer in range(ndev):
            out[pl.ds(peer * ut, ut), :] = total
        copies = Copies(semaphores)
        copies.send(out, total_o)
        copies.close()

    def second(
        shift, bar, load, flow, line, upper, lower, power, notes, settings, shift_far,
        new_flow, new_power, lifted, low, sent, shift_v, incidence, grid, new_bar, semaphores,
    ):
        factors = bring_lines(Copies(semaphores), shift, shift_far, shift_v)
        one_hot(settings, incidence)
        injection = inject(bar, load, incidence)
        sent[pl.ds(0, hours), :] = injection.astype(f32)
        network(injection, flow, factors, line, incidence, new_flow, grid)
        local(
            reader(upper), reader(lower), reader(power), grid,
            lambda hour: notes[pl.ds(ut + hour, 1), :], settings, writer(new_power), new_bar,
            lift(lifted, low),
        )
        sent[pl.ds(hours, hours), :] = inject(new_bar, load, incidence).astype(f32)

    def third(
        shift, sent, load, flow, line, upper, lower, power, notes, settings, shift_far,
        new_flow, new_power, lifted, low, grid, later,
        shift_v, incidence, new_bar, semaphores,
    ):
        factors = bring_lines(Copies(semaphores), shift, shift_far, shift_v)
        one_hot(settings, incidence)
        injection = sent[pl.ds(hours, hours), :].astype(bf16)
        network(injection, flow, factors, line, incidence, new_flow, grid)
        local(
            reader(upper), reader(lower), reader(power), grid,
            lambda hour: notes[pl.ds(ut + hour, 1), :], settings, writer(new_power), new_bar,
            lift(lifted, low),
        )
        injection = inject(new_bar, load, incidence)
        later[...] = injection.astype(f32)
        network(injection, new_flow, arrived(factors), line, incidence, new_flow, grid)

    def lift(lifted, low):
        def put(hour, new_lifted, new_low):
            lifted[pl.ds(hour * ut, ut), :] = new_lifted
            low[pl.ds(hour * ut, ut), :] = new_low

        return put

    def raise_upper(total, lifted, notes, settings, upper, new_notes):
        capacity, pull = capacities(part(notes, 0), settings, total)
        new_notes[pl.ds(0, ut), :] = capacity
        new_notes[pl.ds(ut, hours), :] = notes[pl.ds(ut, hours), :]
        total = jnp.zeros((ut, LANES), f32)
        for hour in range(hours):
            new = jnp.maximum(part(lifted, hour) - pull, 0.0)
            upper[pl.ds(hour * ut, ut), :] = new
            total = total + new
        return total

    def update(came, lifted, notes, settings, sent, upper, new_notes, out_o, out, semaphores):
        spread(out, ut, rows_update, sent[pl.ds(0, hours), :])
        spread(out, ut + bt, rows_update, sent[pl.ds(hours, hours), :])
        total = raise_upper(sum_blocks(came, 0, ut), lifted, notes, settings, upper, new_notes)
        for peer in range(ndev):
            out[pl.ds(peer * rows_update, ut), :] = total
        copies = Copies(semaphores)
        copies.send(out, out_o)
        copies.close()

    def last(
        came, lifted, lower, power, grid, notes, settings, load, later,
        new_notes, total_o, out_o, early_o, incidence, out, early, upper, bar, semaphores,
    ):
        copies = Copies(semaphores)
        for step in range(2):
            early[pl.ds(step * scen, scen), :] = wide(came, ut + step * bt, bt, rows_update)
        copies.send(early, early_o)
        total = raise_upper(
            sum_blocks(came, 0, rows_update), lifted, notes, settings, upper, new_notes
        )
        total_o[...] = total

        def put_power(hour, value):
            out[pl.ds(hour * rows_back, ut), :] = value

        def put(hour, new_lifted, low):
            out[pl.ds(hour * rows_back + ut, ut), :] = new_lifted
            out[pl.ds(hour * rows_back + 2 * ut, ut), :] = low

        local(
            reader(upper), reader(lower), reader(power), grid,
            lambda hour: notes[pl.ds(ut + hour, 1), :], settings, put_power, bar, put,
        )
        blocks = out.reshape(ndev, rows_back, LANES)
        at = pl.ds(0, back_bus)
        copies.send(blocks.at[:, at], out_o.at[:, at])
        one_hot(settings, incidence)
        spread(out, back_bus, rows_back, later[...])
        spread(out, back_bus + bt, rows_back, inject(bar, load, incidence).astype(f32))
        at = pl.ds(back_bus, rows_back - back_bus)
        copies.send(blocks.at[:, at], out_o.at[:, at])
        copies.close()

    def two_steps(value, injections, factors, line, at):
        flows = dual_step * jnp.dot(injections, factors[...], preferred_element_type=f32)
        for step in range(2):
            value = held_back(value + flows[step * scen : (step + 1) * scen], line, at)
        return value

    def hourly_flow(
        turned, line, early, flow, turned_far, new_o, early_v, flow_v, turned_v, new, semaphores
    ):
        copies = Copies(semaphores)
        come = [copies.bring(early, early_v), copies.bring(flow, flow_v)]
        factors = bring_lines(copies, turned, turned_far, turned_v, 1)
        for copy in come:
            copy.wait()
        injections = early_v[...].astype(bf16)
        new[...] = wide(flow_v, 0, lt, lt)
        for at, part_v, wait in factors:
            wait()
            new[:, at] = two_steps(new[:, at], injections, part_v, line, at)
        copies.send(new, new_o)
        copies.close()

    def finish(
        came, line, turned, flow, turned_far, power_o, lower_o, flow_o,
        turned_v, flow_v, out, semaphores,
    ):
        copies = Copies(semaphores)
        flow_came = copies.bring(flow, flow_v)
        factors = bring_lines(copies, turned, turned_far, turned_v, 1)
        blocks = came.reshape(ndev, rows_back, LANES)
        copies.send(blocks.at[:, pl.ds(0, ut)], power_o)
        copies.send(blocks.at[:, pl.ds(2 * ut, ut)], lower_o)
        injections = jnp.concatenate(
            [wide(came, back_bus + step * bt, bt, rows_back) for step in range(2)], axis=0
        ).astype(bf16)
        flow_came.wait()
        row = 0
        for at, part_v, wait in factors:
            wait()
            value = two_steps(flow_v[:, at], injections, part_v, line, at)
            spread(out, row, lt, value)
            some = pl.ds(row, value.shape[1] // LANES)
            copies.send(out.reshape(scen, lt, LANES).at[:, some], flow_o.at[:, some])
            row += value.shape[1] // LANES
        copies.close()

    def finish_upper(came, notes, settings, *rest):
        *terms, upper_o, capacity_o, notes_v, upper, own, semaphores = rest
        copies = Copies(semaphores)
        capacity, pull = capacities(
            part(notes, 0), settings, sum(term[...] for term in terms)
        )
        for peer in range(ndev):
            upper[peer] = jnp.maximum(came[pl.ds(peer * rows_back + ut, ut), :] - pull, 0.0)
        copies.send(upper, upper_o)
        notes_v[...] = capacity
        own[...] = notes_v[pl.ds(lax.axis_index("hour"), 1), :]
        copies.send(own, capacity_o)
        copies.close()


    def tiles(vector):
        return vector.reshape(-1, LANES)

    line = line_limit.reshape(1, lines)
    shift_far, turned = shift_factors, shift_factors.T
    turned_near = turned[:, :near_lines]

    state_v, incidence_v = (state, f32), ((buses, units), bf16)
    shift_v, turned_v = ((lines - near_lines, buses), bf16), ((buses, lines - near_lines), bf16)
    notes = (ut + hours, LANES)
    flops = 4 * hours * buses * (lines + units)

    total, settings, shift, sent = call(
        pack,
        [],
        [
            power.reshape(scen, ut, LANES),
            upper_dual.reshape(scen, ut, LANES),
            lower_dual.reshape(scen, ut, LANES),
            flow_dual.reshape(scen, lt, LANES),
            load.reshape(scen, buses),
            price.reshape(1, scen),
            capacity.reshape(1, LANES),
            tiles(leakage),
            tiles(initial_state),
            tiles(power_limit),
            tiles(capacity_cost),
            shift_far,
            tiles(unit_bus),
        ],
        [(ut, LANES), (5 * ut, LANES), ((near_lines, buses), bf16)],
        [(ndev, rows_in, LANES)],
        [
            ((scen, buses), bf16), ((1, scen), f32), ((1, LANES), f32), ((ut, LANES), jnp.int32),
            ((ndev * rows_in, LANES), f32),
        ],
        14,
    )
    came = exchange(sent).reshape(-1, LANES)
    totals = gather_up(total, three_stages)
    power, lifted, lower, bar, flow, load, note = call(
        first,
        [came, shift, settings],
        [shift_far, turned],
        [state] * 4 + [(hours, lines), (hours, buses), notes],
        [],
        [shift_v, incidence_v, state_v],
        FAR_PARTS,
        flops=flops,
    )
    upper, note, total = call(
        begin, [lifted, note, settings, *totals], [], [state, notes], [state], [state_v], 1
    )
    came = exchange(total.reshape(ndev, ut, LANES)).reshape(-1, LANES)
    flow, power, lifted, lower, injections = call(
        second,
        [shift, bar, load, flow, line, upper, lower, power, note, settings],
        [shift_far],
        [(hours, lines)] + [state] * 3 + [(2 * hours, buses)],
        [],
        [shift_v, incidence_v, state_v, state_v],
        FAR_PARTS,
        flops=flops,
    )
    upper, note, sent = call(
        update,
        [came, lifted, note, settings, injections],
        [],
        [state, notes],
        [(ndev * rows_update, LANES)],
        [((ndev * rows_update, LANES), f32)],
        1,
    )
    came = exchange(sent.reshape(ndev, rows_update, LANES)).reshape(-1, LANES)
    flow, power, lifted, lower, grid, injection = call(
        third,
        [shift, injections, load, flow, line, upper, lower, power, note, settings],
        [shift_far],
        [(hours, lines)] + [state] * 4 + [(hours, buses)],
        [],
        [shift_v, incidence_v, state_v],
        FAR_PARTS,
        flops=2 * flops,
    )
    note, total, sent, early = call(
        last,
        [came, lifted, lower, power, grid, note, settings, load, injection],
        [],
        [notes, (ut, LANES)],
        [(ndev, rows_back, LANES), (2 * scen, buses)],
        [
            incidence_v, ((ndev * rows_back, LANES), f32), ((2 * scen, buses), f32), state_v,
            state_v,
        ],
        3,
        flops=flops,
    )
    came = exchange(sent).reshape(-1, LANES)
    totals = gather_up(total, two_stages)
    own_flow = ((scen * lt, LANES), f32)
    (flow,) = call(
        hourly_flow,
        [turned_near, line],
        [early, flow_dual.reshape(scen * lt, LANES), turned],
        [],
        [(scen, lines)],
        [((2 * scen, buses), f32), own_flow, turned_v, ((scen, lines), f32)],
        FAR_PARTS + 3,
        flops=flops,
    )
    hourly = (scen, ut, LANES)
    power, lower, flow = call(
        finish,
        [came, line, turned_near],
        [flow, turned],
        [],
        [hourly, hourly, (scen, lt, LANES)],
        [turned_v, ((scen, lines), f32), own_flow],
        2 * FAR_PARTS + 4,
        flops=flops,
    )
    upper, capacity = call(
        finish_upper,
        [came, note, settings, *totals],
        [],
        [],
        [hourly, (1, LANES)],
        [((ut, LANES), f32), (hourly, f32), ((1, LANES), f32)],
        2,
    )
    return (
        power.reshape(scen, 1, units),
        capacity.reshape(LANES),
        flow.reshape(scen, 1, lines),
        upper.reshape(scen, 1, units),
        lower.reshape(scen, 1, units),
    )


def on_device(power, capacity, flow_dual, *rest):
    ndev = lax.axis_size("hour")
    buses = rest[4].shape[1]
    fits = (
        ITERS == 4
        and power.shape[0] == ndev
        and power.shape[1] == 1
        and capacity.shape[0] == LANES
        and flow_dual.shape[2] % (16 * SUBLANES * LANES // 4) == 0
        and ndev % (2 * SUBLANES) == 0
        and ndev & (ndev - 1) == 0
        and all(size % (SUBLANES * LANES) == 0 for size in (power.shape[2], flow_dual.shape[2]))
        and buses % LANES == 0
    )
    plan = by_scenarios if fits else by_units
    return plan(power, capacity, flow_dual, *rest)


def solution(mesh):
    return jax.shard_map(
        on_device,
        mesh=mesh,
        in_specs=(
            P("groups", "hour", None),
            P(("groups", "hour")),
            P("groups", "hour", None),
            P("groups", "hour", None),
            P("groups", "hour", None),
            P("groups", "hour"),
            P("groups", "hour", None),
            P(),
            P(),
            P(),
            P(),
            P("groups"),
            P(),
            P(),
        ),
        out_specs=(
            P("groups", "hour", None),
            P(("groups", "hour")),
            P("groups", "hour", None),
            P("groups", "hour", None),
            P("groups", "hour", None),
        ),
        check_vma=False,
    )
```
